768 devices in a mesh: dp: 48 (over z, y_lo), mp: 16 (over y_hi, x, core).
Axes of the slice: x: 4, y: 8 (y_hi: 2, y_lo: 4; y = y_hi * 4 + y_lo), z: 12, core: 2. Of those that a mesh axis runs over, the one named last changes fastest.
Arguments:
- patches: bfloat16 [1152, 36864], P('mp', 'dp'), may hold values from -40 to 40
- counts: int32 [2304], replicated, may hold values from 4 to 16, as said below
- dest: int32 [2304], replicated, may hold values from 0 to 47, as said below
- w_qkv: bfloat16 [3, 1152, 1152], P(None, 'mp'), may hold values from -4 to 4
- w_out: bfloat16 [1152, 1152], P('mp'), may hold values from -0.1875 to 0.1875
- text: bfloat16 [2304, 1152], P(('dp', 'mp')), may hold values from -6 to 6
Outputs:
- grad_image: float32 [2304, 1152], P('dp', 'mp')
- grad_text: float32 [2304, 1152], P(('dp', 'mp'))
The draws below stay inside these ranges and needn't reach their ends.
Inputs may be any that keep to these rules, and one draw needn't show every extreme that they name: `counts`: every dp index holds 48 images; on some dp index every image that is sent to it has 16 patches. `dest`: entries s * 48 to s * 48 + 47 are a permutation of 0 to 47: every dp index sends exactly one image to every dp index.
All inputs are finite; a program needn't handle non-finite values.
Results may differ from the reference program's by a relative error of at most 0.0046.
Values may be sent and summed in bfloat16 or wider, within the bound.
A program may use at most 64 MiB of HBM per device.

```python
import math
import jax
import jax.numpy as jnp
from jax import lax

D = 1152
HEADS = 16
HD = 72
MAXP = 16
MINP = 4
IMG_DEV = 48
ROWS_DEV = 768
TOTAL = 2304


def routing_plan(key):
    key_perm, key_count, key_full = jax.random.split(key, 3)
    perm_keys = jax.random.split(key_perm, IMG_DEV)
    dest_table = jax.vmap(lambda one_key: jax.random.permutation(one_key, IMG_DEV))(perm_keys).astype(jnp.int32)
    count_table = jax.random.randint(key_count, (IMG_DEV, IMG_DEV), MINP, MAXP + 1).astype(jnp.int32)
    full_target = jax.random.randint(key_full, (), 0, IMG_DEV).astype(jnp.int32)
    count_table = jnp.where(dest_table == full_target, MAXP, count_table).astype(jnp.int32)
    return (count_table.reshape(TOTAL), dest_table.reshape(TOTAL))


def draw_counts(key, part):
    return routing_plan(key)[0]


def draw_dest(key, part):
    return routing_plan(key)[1]


def draw_patches(key, part):
    key = jax.random.fold_in(key, 7)
    key_base, key_rows, key_cols = jax.random.split(key, 3)
    shape_all = (D, IMG_DEV * ROWS_DEV)
    column_scale = jnp.exp(jax.random.uniform(key_cols, (D, 1), jnp.float32, jnp.log(0.5), jnp.log(3.0)))
    row_scale = jnp.exp(jax.random.uniform(key_rows, (1, IMG_DEV * ROWS_DEV), jnp.float32, jnp.log(0.5), jnp.log(3.0)))
    values = jnp.clip(jax.random.normal(key_base, shape_all, jnp.float32), -4.0, 4.0) * row_scale * column_scale
    return values.astype(jnp.bfloat16)


def draw_w_qkv(key, part):
    key = jax.random.fold_in(key, 5)
    key_query, key_second, key_value = jax.random.split(key, 3)
    spread = D ** (-0.5)
    query_w = jnp.clip(jax.random.normal(key_query, (D, D), jnp.float32), -4.0, 4.0) * spread
    second = jnp.clip(jax.random.normal(key_second, (D, D), jnp.float32), -4.0, 4.0) * spread
    value_w = jnp.clip(jax.random.normal(key_value, (D, D), jnp.float32), -4.0, 4.0) * spread
    key_w = second
    stacked = jnp.clip(jnp.stack([query_w, key_w, value_w]), -4.0, 4.0)
    return jnp.transpose(stacked, (0, 2, 1)).astype(jnp.bfloat16)


def levels(rng, extent, cuts, least, high):
    def one(dim, shards_of):
        heights = jax.random.uniform(jax.random.fold_in(jax.random.fold_in(rng, 6), dim), (shards_of,), jnp.float32, least / len(cuts), high / len(cuts))
        return jnp.repeat(jnp.exp(heights), extent[dim] // shards_of).reshape((-1,) + (1,) * (len(extent) - dim - 1))

    loudness = one(*cuts[0])
    for cut in cuts[1:]:
        loudness = loudness * one(*cut)
    return loudness


def gaussian(stream_key, shape, scale, bound, pieces=(), kind=jnp.bfloat16):
    gain = levels(stream_key, shape, pieces, -0.22, 0.18) if pieces else 1.0
    entries = jax.random.normal(stream_key, shape, jnp.float32) * scale * gain
    return jnp.minimum(jnp.maximum(entries, -bound), bound).astype(kind)


def setup_inputs(seed: int = 0) -> dict:
    streams_of = jax.random.split(jax.random.key(seed), 7)
    return {
        "patches": draw_patches(jax.random.fold_in(streams_of[6], 71), 0),
        "counts": draw_counts(jax.random.fold_in(streams_of[6], 71), 0),
        "dest": draw_dest(jax.random.fold_in(streams_of[6], 71), 0),
        "w_qkv": draw_w_qkv(jax.random.fold_in(streams_of[6], 71), 0),
        "w_out": gaussian(streams_of[4], (D, D), D ** -0.5, 0.1875, ((0, 16),)),
        "text": gaussian(streams_of[5], (TOTAL, D), 1.0, 6.0, ((0, 768),)),
    }


def routing(counts, dest):
    count_table = counts.reshape(IMG_DEV, IMG_DEV)
    dest_table = dest.reshape(IMG_DEV, IMG_DEV)
    start_table = (jnp.cumsum(count_table, axis=1) - count_table).astype(jnp.int32)
    targets = jnp.arange(IMG_DEV, dtype=jnp.int32)
    chosen = dest_table[None, :, :] == targets[:, None, None]
    got_count = lax.optimization_barrier(jnp.sum(jnp.where(chosen, count_table[None], 0), axis=2)).astype(jnp.int32)
    got_start = lax.optimization_barrier(jnp.sum(jnp.where(chosen, start_table[None], 0), axis=2)).astype(jnp.int32)
    got_index = lax.optimization_barrier(jnp.sum(jnp.where(chosen, targets[None, None, :], 0), axis=2)).astype(jnp.int32)
    image_ids = (targets[None, :] * IMG_DEV + got_index).astype(jnp.int32)
    return (got_count, got_start, image_ids)

def reference(patches, counts, dest, w_qkv, w_out, text):
    got_count, got_start, image_ids = routing(counts, dest)
    source_rows = patches.T.reshape(IMG_DEV, ROWS_DEV, D)
    position = jnp.arange(MAXP, dtype=jnp.int32)
    sources = jnp.arange(IMG_DEV, dtype=jnp.int32)

    def one_device(item):
        count_row, start_row = item
        valid_slot = position[None, :] < count_row[:, None]
        row_index = jnp.where(valid_slot, start_row[:, None] + position[None, :], 0).astype(jnp.int32)
        rows = source_rows[sources[:, None], row_index]
        rows = jnp.where(valid_slot[:, :, None], rows.astype(jnp.float32), 0.0)
        row_mean = lax.optimization_barrier(jnp.mean(rows, axis=-1, keepdims=True))
        centred = rows - row_mean
        row_var = lax.optimization_barrier(jnp.mean(centred * centred, axis=-1, keepdims=True))
        normed = (centred * lax.rsqrt(row_var + 1e-06)).astype(jnp.bfloat16).reshape(IMG_DEV * MAXP, D)
        projected = [jnp.dot(normed, w_qkv[which].T, preferred_element_type=jnp.float32).astype(jnp.bfloat16).reshape(IMG_DEV, MAXP, HEADS, HD) for which in range(3)]
        query, key_rows, value = projected
        scores = jnp.einsum('sphd,sqhd->shpq', query.astype(jnp.float32), key_rows.astype(jnp.float32)) / math.sqrt(HD)
        scores = jnp.where(valid_slot[:, None, None, :], scores, -1e+30)
        row_max = lax.optimization_barrier(jnp.max(scores, axis=-1, keepdims=True))
        raised = jnp.exp(scores - row_max)
        weights = (raised / lax.optimization_barrier(jnp.sum(raised, axis=-1, keepdims=True))).astype(jnp.bfloat16)
        mixed = jnp.einsum('shpq,sqhd->sphd', weights.astype(jnp.float32), value.astype(jnp.float32)).astype(jnp.bfloat16).reshape(IMG_DEV, MAXP, D)
        counts_float = count_row.astype(jnp.float32)[:, None]
        pooled_heads = (lax.optimization_barrier(jnp.sum(jnp.where(valid_slot[:, :, None], mixed.astype(jnp.float32), 0.0), axis=1)) / counts_float).astype(jnp.bfloat16)
        pooled = lax.optimization_barrier(jnp.sum(rows, axis=1)) / counts_float + jnp.dot(pooled_heads, w_out, preferred_element_type=jnp.float32)
        scale_rows = lax.rsqrt(lax.optimization_barrier(jnp.sum(pooled * pooled, axis=-1, keepdims=True)) + 1e-06)
        return (pooled * scale_rows).astype(jnp.bfloat16)
    image_unit = lax.map(one_device, (got_count, got_start)).reshape(TOTAL, D)
    flat_ids = image_ids.reshape(TOTAL)
    text_float = text.astype(jnp.float32)
    text_unit = (text_float * lax.rsqrt(lax.optimization_barrier(jnp.sum(text_float * text_float, axis=-1, keepdims=True)) + 1e-06)).astype(jnp.bfloat16)
    logits = 4.0 * jnp.dot(image_unit, text_unit.T, preferred_element_type=jnp.float32) - 2.0
    labels = jnp.where(flat_ids[:, None] == jnp.arange(TOTAL, dtype=jnp.int32)[None, :], 1.0, -1.0)
    dscaled = (-4.0 * labels * jax.nn.sigmoid(-labels * logits)).astype(jnp.bfloat16)
    grad_image = jnp.dot(dscaled, text_unit, preferred_element_type=jnp.float32)
    grad_text = jnp.dot(dscaled.T, image_unit, preferred_element_type=jnp.float32)
    return (grad_image, grad_text)
```

```python
import math

import jax
import jax.numpy as jnp
from jax import lax
from jax.experimental import pallas as pl
from jax.experimental.pallas import tpu as pltpu
from jax.sharding import PartitionSpec as P

HD = 72
MAXP = 16
NYL = 4
NYH = 2
NX = 4
NG = NYH * NX
LANES = 128
F32 = jnp.float32
BF16 = jnp.bfloat16
MESH = pl.DeviceIdType.MESH


def iota(shape, dim):
    return lax.broadcasted_iota(jnp.int32, shape, dim)


def dot_nn(a, b):
    return lax.dot_general(a, b, (((1,), (0,)), ((), ())), preferred_element_type=F32)


def dot_nt(a, b):
    return lax.dot_general(a, b, (((1,), (1,)), ((), ())), preferred_element_type=F32)


def make_kernel(dp_size, width, texts_here):
    nz = dp_size // NYL
    half = dp_size // 2
    images_here = half // NG
    pieces = width // LANES
    used = images_here * pieces
    packed = -(-used // 16) * 16
    slots = dp_size * MAXP
    half_slots = half * MAXP
    plane = NYL * NG
    rows = NYL * half
    text_rows = texts_here * 2 * nz
    wide = -(-(4 * HD) // LANES) * LANES

    def kernel(
        counts,
        dest,
        patches,
        w_qkv,
        w_out,
        text,
        grad_image,
        grad_text,
        outbox,
        inbox,
        w_qkv_peer,
        w_out_peer,
        feats,
        text_f,
        text_box,
        text_in,
        text_wide,
        text_full,
        text_pad,
        part_f,
        part_b,
        part_in,
        mean_f,
        unit_box,
        unit_in,
        unit_wide,
        unit_full,
        gi_box,
        gi_in,
        gi_sum,
        gy_box,
        gy_in,
        gt_f,
        gt_in,
        gt_box,
        gtz_in,
        local_sem,
        a2a_send,
        a2a_recv,
        w_send,
        w_recv,
        g_send,
        g_recv,
        text_send,
        text_recv,
        part_send,
        part_recv,
        unit_send,
        unit_recv,
        gi_send,
        gi_recv,
        gy_send,
        gy_recv,
        gt_send,
        gt_recv,
        gtz_send,
        gtz_recv,
    ):
        me = lax.axis_index("dp")
        mp = lax.axis_index("mp")
        g, c = mp // 2, mp % 2
        z, ylo = me // NYL, me % NYL
        yhi, x = g // NX, g % NX
        y = yhi * NYL + ylo
        other = 1 - c
        partner = (me, g * 2 + other)
        my_half = me // half
        my_slot = me % half
        extra = jnp.where(my_half == c, 0, 1)

        barrier = pltpu.get_barrier_semaphore()

        def greet(device):
            pl.semaphore_signal(barrier, inc=1, device_id=device, device_id_type=MESH)

        @pl.loop(0, half)
        def _(i):
            src = half * c + i
            greet((src, g * 2 + other))

            @pl.when(src != me)
            def _():
                greet((src, mp))

        greet(partner)

        @pl.loop(1, nz)
        def _(i):
            zz = lax.rem(z + i, nz)
            greet((zz * NYL + ylo, g * 2))
            greet((zz * NYL + ylo, g * 2 + 1))

        place = ylo * NG + g

        @pl.loop(1, plane)
        def _(i):
            q = lax.rem(place + i, plane)
            greet((z * NYL + q // NG, (q % NG) * 2 + c))

        @pl.loop(1, 2 * NYL)
        def _(i):
            q = lax.rem(y + i, 2 * NYL)
            greet((z * NYL + q % NYL, ((q // NYL) * NX + x) * 2 + other))

        own_counts = counts[pl.ds(me, 1), :]
        own_dest = dest[pl.ds(me, 1), :]
        lane = iota((slots, dp_size), 1)
        target = iota((slots, dp_size), 0) // MAXP
        index = jnp.sum(jnp.where(own_dest == target, lane, 0), axis=1, keepdims=True)
        start = jnp.sum(jnp.where(lane < index, own_counts, 0), axis=1, keepdims=True)
        count = jnp.sum(jnp.where(lane == index, own_counts, 0), axis=1, keepdims=True)
        position = iota((slots, 1), 0) % MAXP
        column = jnp.where(position < count, start + position, -1)
        chosen = (iota((slots, patches.shape[1]), 1) == column).astype(F32).astype(BF16)
        picked = dot_nt(chosen, patches[...]).astype(BF16)
        outbox[...] = picked.reshape(dp_size, MAXP, HD)

        total = (2 * half - 1 + extra) + 1 + 2 * (nz - 1) + (plane - 1) + (2 * NYL - 1)
        pl.semaphore_wait(barrier, total)

        def image_copy(d):
            return pltpu.make_async_remote_copy(
                src_ref=outbox.at[d],
                dst_ref=inbox.at[c * half + my_slot],
                send_sem=a2a_send,
                recv_sem=a2a_recv,
                device_id=(d, g * 2 + my_half),
                device_id_type=MESH,
            )

        @pl.loop(1, dp_size)
        def _(i):
            image_copy(lax.rem(me + i, dp_size)).start()

        own_copy = pltpu.make_async_copy(
            outbox.at[me], inbox.at[c * half + my_slot], local_sem
        )

        @pl.when(my_half == c)
        def _():
            own_copy.start()

        @pl.when(my_half != c)
        def _():
            image_copy(me).start()

        def swap(src, dst, i):
            return pltpu.make_async_remote_copy(
                src_ref=src,
                dst_ref=dst,
                send_sem=w_send.at[i],
                recv_sem=w_recv.at[i],
                device_id=partner,
                device_id_type=MESH,
            )

        swap_qkv = swap(w_qkv, w_qkv_peer, 0)
        swap_out = swap(w_out, w_out_peer, 1)
        swap_qkv.start()
        swap_out.start()

        text_float = text[...].astype(F32)
        text_unit = text_float * lax.rsqrt(
            jnp.sum(text_float * text_float, axis=1, keepdims=True) + 1e-6
        )
        text_f[...] = jnp.zeros_like(text_f)
        for t in range(texts_here):
            for k in range(pieces):
                text_f[t * pieces + k : t * pieces + k + 1, :] = text_unit[
                    t : t + 1, k * LANES : (k + 1) * LANES
                ]
        own_text = text_f[...].astype(BF16)
        text_box[...] = own_text
        text_in[c * nz + z] = own_text

        def text_copy(zz, core):
            return pltpu.make_async_remote_copy(
                src_ref=text_box,
                dst_ref=text_in.at[c * nz + z],
                send_sem=text_send,
                recv_sem=text_recv,
                device_id=(zz * NYL + ylo, g * 2 + core),
                device_id_type=MESH,
            )

        text_copy(z, other).start()

        @pl.loop(1, nz)
        def _(i):
            zz = lax.rem(z + i, nz)
            text_copy(zz, 0).start()
            text_copy(zz, 1).start()

        mine = pl.ds(pl.multiple_of(half * c, 8), half)
        got = jnp.sum(
            jnp.where(dest[mine, :] == me, counts[mine, :], 0), axis=1, keepdims=True
        )

        @pl.when(my_half == c)
        def _():
            own_copy.wait()
            pltpu.make_async_remote_copy(
                src_ref=inbox.at[pl.ds(0, 2 * half - 1)],
                dst_ref=inbox.at[pl.ds(0, 2 * half - 1)],
                send_sem=a2a_send,
                recv_sem=a2a_recv,
                device_id=partner,
                device_id_type=MESH,
            ).wait_recv()

        @pl.when(my_half != c)
        def _():
            pltpu.make_async_remote_copy(
                src_ref=inbox,
                dst_ref=inbox,
                send_sem=a2a_send,
                recv_sem=a2a_recv,
                device_id=partner,
                device_id_type=MESH,
            ).wait_recv()

        eye = (iota((HD, HD), 0) == iota((HD, HD), 1)).astype(F32).astype(BF16)
        low = dot_nt(eye, inbox[0:half].reshape(half_slots, HD))
        high = dot_nt(eye, inbox[half : 2 * half].reshape(half_slots, HD))
        block = jnp.concatenate([low, high], axis=0).astype(BF16)
        for k in range(images_here):
            feats[k, g] = block[:, k * LANES : (k + 1) * LANES]

        across = (1 - yhi) * NX + x
        left_x, right_x = lax.rem(x + NX - 1, NX), lax.rem(x + 1, NX)
        far_x = lax.rem(x + 2, NX)

        def feat_copy(k, owner, to):
            return pltpu.make_async_remote_copy(
                src_ref=feats.at[k, owner],
                dst_ref=feats.at[k, owner],
                send_sem=g_send.at[k],
                recv_sem=g_recv.at[k, owner],
                device_id=(me, to * 2 + c),
                device_id_type=MESH,
            )

        own_row, far_row = yhi * NX, (1 - yhi) * NX
        left, right = own_row + left_x, own_row + right_x
        for k in range(images_here):
            feat_copy(k, g, across).start()
            feat_copy(k, g, left).start()
            feat_copy(k, g, right).start()

        def relay(k, row, flip):
            feat_copy(k, row + left_x, left).wait_recv()
            if not flip:
                feat_copy(k, row + left_x, right).start()
            feat_copy(k, row + right_x, left).wait_recv()
            if flip:
                feat_copy(k, row + right_x, left).start()

        for k in range(images_here):
            relay(k, own_row, k % 2 == 1)
            feat_copy(k, across, across).wait_recv()
            feat_copy(k, across, left).start()
            feat_copy(k, across, right).start()

        swap_qkv.wait()
        swap_out.wait()

        part_f[...] = jnp.zeros_like(part_f)
        mean_f[...] = jnp.zeros_like(mean_f)
        row8, lane8 = iota((NG, LANES), 0), iota((NG, LANES), 1)
        same = iota((LANES, LANES), 0) // MAXP == iota((LANES, LANES), 1) // MAXP
        for k in range(images_here):
            relay(k, far_row, k % 2 == 0)
            feat_copy(k, own_row + far_x, left).wait_recv()
            feat_copy(k, far_row + far_x, left).wait_recv()
            raw = feats[k].reshape(width, LANES)
            full = raw.astype(F32)
            centred = full - jnp.sum(full, axis=0, keepdims=True) / width
            variance = jnp.sum(centred * centred, axis=0, keepdims=True) / width
            normed = (centred * lax.rsqrt(variance + 1e-6)).astype(BF16)
            got_k = got[k * NG : (k + 1) * NG]
            got_float = got_k.astype(F32)
            real = (lane8 // MAXP == row8) & (lane8 % MAXP < got_k)
            real_float = real.astype(F32)
            key_real = jnp.max(real_float, axis=0, keepdims=True) > 0.5
            member = real_float.astype(BF16)
            keep = same & key_real
            term = jnp.zeros((NG, width), F32)
            for wq, wo in ((w_qkv, w_out), (w_qkv_peer, w_out_peer)):
                projected = dot_nn(wq[...], normed)
                query = jnp.transpose(projected[0:HD]).astype(BF16)
                key = projected[HD : 2 * HD].astype(BF16)
                value = projected[2 * HD : 3 * HD].astype(BF16)
                scores = dot_nn(query, key) / math.sqrt(HD)
                scores = jnp.where(keep, scores, -1e30)
                raised = jnp.exp(scores - jnp.max(scores, axis=1, keepdims=True))
                weights = (raised / jnp.sum(raised, axis=1, keepdims=True)).astype(BF16)
                mixed = dot_nt(value, weights).astype(BF16)
                pooled = (dot_nt(member, mixed) / got_float).astype(BF16)
                term = term + dot_nn(pooled, wo[...])
            for p in range(pieces):
                part_f[pl.ds(k * pieces + p, NG, stride=packed), :] = term[
                    :, p * LANES : (p + 1) * LANES
                ]
            here = (lane8 // MAXP == g).astype(F32).astype(BF16)
            own_got = jnp.sum(
                jnp.where(iota((NG, 1), 0) == g, got_float, 0.0), axis=0, keepdims=True
            )
            mean = dot_nt(here, raw) / own_got
            for p in range(pieces):
                r = k * pieces + p
                mean_f[r : r + 1, :] = mean[0:1, p * LANES : (p + 1) * LANES]

        part_b[...] = part_f[...].astype(BF16).reshape(NG, packed, LANES)

        def part_copy(gg):
            return pltpu.make_async_remote_copy(
                src_ref=part_b.at[gg],
                dst_ref=part_in.at[g],
                send_sem=part_send,
                recv_sem=part_recv,
                device_id=(me, gg * 2 + c),
                device_id_type=MESH,
            )

        @pl.loop(1, NG)
        def _(i):
            part_copy(lax.rem(g + i, NG)).start()

        part_in[g] = part_b[g]

        pltpu.make_async_remote_copy(
            src_ref=text_in.at[pl.ds(0, 2 * nz - 1)],
            dst_ref=text_in.at[pl.ds(0, 2 * nz - 1)],
            send_sem=text_send,
            recv_sem=text_recv,
            device_id=partner,
            device_id_type=MESH,
        ).wait()
        text_wide[...] = text_in[...].astype(F32).reshape(2 * nz * packed, LANES)
        for t in range(texts_here):
            for p in range(pieces):
                text_full[t * 2 * nz : (t + 1) * 2 * nz, p * LANES : (p + 1) * LANES] = (
                    text_wide[pl.ds(t * pieces + p, 2 * nz, stride=packed), :]
                )
        text_pad[...] = jnp.zeros_like(text_pad)
        for xx in range(NX):
            for q in range(4):
                m = ((q // 2) * NX + xx) * 2 + q % 2
                text_pad[:, xx * wide + q * HD : xx * wide + (q + 1) * HD] = text_full[
                    :, m * HD : (m + 1) * HD
                ]
        text_rows_b = text_full[...].astype(BF16)
        text_cols_b = text_pad[...].astype(BF16)

        part_seven = pltpu.make_async_remote_copy(
            src_ref=part_in.at[pl.ds(0, NG - 1)],
            dst_ref=part_in.at[pl.ds(0, NG - 1)],
            send_sem=part_send,
            recv_sem=part_recv,
            device_id=partner,
            device_id_type=MESH,
        )
        part_seven.wait()
        pooled = jnp.sum(part_in[...].astype(F32), axis=0) + mean_f[...]
        squares = jnp.sum(pooled * pooled, axis=1, keepdims=True)
        row_id = iota((packed, 1), 0)
        scale = jnp.zeros((packed, 1), F32)
        for k in range(images_here):
            inside = (row_id >= k * pieces) & (row_id < (k + 1) * pieces)
            norm = jnp.sum(jnp.where(inside, squares, 0.0), axis=0, keepdims=True)
            scale = jnp.where(inside, lax.rsqrt(norm + 1e-6), scale)
        own_unit = (pooled * scale).astype(BF16)
        unit_box[...] = own_unit
        unit_in[place] = own_unit

        def unit_copy(q):
            return pltpu.make_async_remote_copy(
                src_ref=unit_box,
                dst_ref=unit_in.at[place],
                send_sem=unit_send,
                recv_sem=unit_recv,
                device_id=(z * NYL + q // NG, (q % NG) * 2 + c),
                device_id_type=MESH,
            )

        @pl.loop(1, plane)
        def _(i):
            unit_copy(lax.rem(place + i, plane)).start()

        pltpu.make_async_remote_copy(
            src_ref=unit_in.at[pl.ds(0, plane - 1)],
            dst_ref=unit_in.at[pl.ds(0, plane - 1)],
            send_sem=unit_send,
            recv_sem=unit_recv,
            device_id=partner,
            device_id_type=MESH,
        ).wait()
        unit_wide[...] = unit_in[...].astype(F32).reshape(plane * packed, LANES)
        for yy in range(NYL):
            for k in range(images_here):
                for p in range(pieces):
                    unit_full[
                        yy * half + k * NG : yy * half + (k + 1) * NG,
                        p * LANES : (p + 1) * LANES,
                    ] = unit_wide[
                        pl.ds(yy * NG * packed + k * pieces + p, NG, stride=packed), :
                    ]
        units = unit_full[...].astype(BF16)

        text_id = iota((text_rows, dp_size), 0)
        text_z = text_id % nz
        text_core = (text_id % (2 * nz)) // nz
        text_t = text_id // (2 * nz)
        col = iota((text_rows, dp_size), 1)
        source = (col == text_z * NYL + ylo).astype(F32).astype(BF16)
        dest_rows = dot_nn(source, dest[...].astype(F32).astype(BF16))
        pair_col = (g * 2 + text_core) * texts_here + text_t
        pair_dest = jnp.sum(
            jnp.where(col == pair_col, dest_rows, 0.0), axis=1, keepdims=True
        ).astype(jnp.int32)
        image_lane = iota((text_rows, rows), 1)
        image_source = c * half + image_lane % half
        image_dest = z * NYL + image_lane // half
        text_source = (iota((text_rows, 1), 0) % nz) * NYL + ylo
        paired = (image_source == text_source) & (image_dest == pair_dest)
        labels = jnp.where(paired, 1.0, -1.0)
        logits = 4.0 * dot_nt(text_rows_b, units) - 2.0
        dscaled = -4.0 * labels / (1.0 + jnp.exp(labels * logits))
        turned = jnp.transpose(dscaled).astype(BF16)
        dscaled = dscaled.astype(BF16)

        text_grad = dot_nn(dscaled, units)
        gt_f[...] = jnp.zeros_like(gt_f)
        for t in range(texts_here):
            for p in range(pieces):
                gt_f[pl.ds(t * pieces + p, 2 * nz, stride=packed), :] = text_grad[
                    t * 2 * nz : (t + 1) * 2 * nz, p * LANES : (p + 1) * LANES
                ]
        core_rows = nz * packed
        gt_copy = pltpu.make_async_remote_copy(
            src_ref=gt_f.at[pl.ds(pl.multiple_of(other * core_rows, 8), core_rows)],
            dst_ref=gt_in,
            send_sem=gt_send,
            recv_sem=gt_recv,
            device_id=partner,
            device_id_type=MESH,
        )
        gt_copy.start()

        for xx in range(NX):
            gi_box[xx] = dot_nn(turned, text_cols_b[:, xx * wide : (xx + 1) * wide]).astype(BF16)

        def gi_copy(xx):
            return pltpu.make_async_remote_copy(
                src_ref=gi_box.at[xx],
                dst_ref=gi_in.at[x],
                send_sem=gi_send,
                recv_sem=gi_recv,
                device_id=(me, (yhi * NX + xx) * 2 + c),
                device_id_type=MESH,
            )

        for i in range(1, NX):
            gi_copy(lax.rem(x + i, NX)).start()
        gi_in[x] = gi_box[x]

        gt_copy.wait()
        own_rows = gt_f[pl.ds(pl.multiple_of(c * core_rows, 8), core_rows), :]
        gt_box[...] = (own_rows + gt_in[...]).astype(BF16).reshape(nz, packed, LANES)

        def gtz_copy(zz):
            return pltpu.make_async_remote_copy(
                src_ref=gt_box.at[zz],
                dst_ref=gtz_in.at[z],
                send_sem=gtz_send,
                recv_sem=gtz_recv,
                device_id=(zz * NYL + ylo, mp),
                device_id_type=MESH,
            )

        @pl.loop(1, nz)
        def _(i):
            gtz_copy(lax.rem(z + i, nz)).start()

        gtz_in[z] = gt_box[z]

        pltpu.make_async_remote_copy(
            src_ref=gi_in.at[pl.ds(0, NX - 1)],
            dst_ref=gi_in.at[pl.ds(0, NX - 1)],
            send_sem=gi_send,
            recv_sem=gi_recv,
            device_id=partner,
            device_id_type=MESH,
        ).wait()
        gi_sum[...] = jnp.sum(gi_in[...].astype(F32), axis=0)

        gy_box[...] = jnp.zeros_like(gy_box)
        for yy in range(2 * NYL):
            for core in range(2):
                q = (yy // NYL) * 2 + core
                r = (yy % NYL) * half
                gy_box[yy * 2 + core, 0:half, 0:HD] = gi_sum[
                    r : r + half, q * HD : (q + 1) * HD
                ].astype(BF16)

        def gy_copy(yy, core):
            return pltpu.make_async_remote_copy(
                src_ref=gy_box.at[yy * 2 + core],
                dst_ref=gy_in.at[c * 2 * NYL + y],
                send_sem=gy_send,
                recv_sem=gy_recv,
                device_id=(z * NYL + yy % NYL, ((yy // NYL) * NX + x) * 2 + core),
                device_id_type=MESH,
            )

        gy_copy(y, other).start()

        @pl.loop(1, 2 * NYL)
        def _(i):
            yy = lax.rem(y + i, 2 * NYL)
            gy_copy(yy, 0).start()
            gy_copy(yy, 1).start()

        gy_in[c * 2 * NYL + y] = gy_box[y * 2 + c]

        pltpu.make_async_remote_copy(
            src_ref=gtz_in.at[pl.ds(0, nz - 1)],
            dst_ref=gtz_in.at[pl.ds(0, nz - 1)],
            send_sem=gtz_send,
            recv_sem=gtz_recv,
            device_id=partner,
            device_id_type=MESH,
        ).wait()
        summed = jnp.sum(gtz_in[...].astype(F32), axis=0)
        for t in range(texts_here):
            for p in range(pieces):
                r = t * pieces + p
                grad_text[t : t + 1, p * LANES : (p + 1) * LANES] = summed[r : r + 1, :]

        pltpu.make_async_remote_copy(
            src_ref=gy_in.at[pl.ds(0, 4 * NYL - 1)],
            dst_ref=gy_in.at[pl.ds(0, 4 * NYL - 1)],
            send_sem=gy_send,
            recv_sem=gy_recv,
            device_id=partner,
            device_id_type=MESH,
        ).wait()
        for core in range(2):
            part = gy_in[core * 2 * NYL : (core + 1) * 2 * NYL].astype(F32)
            grad_image[core * half : (core + 1) * half, :] = jnp.sum(part, axis=0)[0:half, 0:HD]

        @pl.when(my_half == c)
        def _():
            pltpu.make_async_remote_copy(
                src_ref=outbox.at[pl.ds(0, dp_size - 1)],
                dst_ref=outbox.at[pl.ds(0, dp_size - 1)],
                send_sem=a2a_send,
                recv_sem=a2a_recv,
                device_id=partner,
                device_id_type=MESH,
            ).wait_send()

        @pl.when(my_half != c)
        def _():
            pltpu.make_async_remote_copy(
                src_ref=outbox,
                dst_ref=outbox,
                send_sem=a2a_send,
                recv_sem=a2a_recv,
                device_id=partner,
                device_id_type=MESH,
            ).wait_send()

        for k in range(images_here):
            pltpu.make_async_remote_copy(
                src_ref=feats.at[k, pl.ds(0, NG - 1)],
                dst_ref=feats.at[k, pl.ds(0, NG - 1)],
                send_sem=g_send.at[k],
                recv_sem=g_recv.at[k, 0],
                device_id=partner,
                device_id_type=MESH,
            ).wait_send()

    dma = pltpu.SemaphoreType.DMA
    scratch = [
        pltpu.VMEM((dp_size, MAXP, HD), BF16),
        pltpu.VMEM((2 * half, MAXP, HD), BF16),
        pltpu.VMEM((3 * HD, width), BF16),
        pltpu.VMEM((HD, width), BF16),
        pltpu.VMEM((images_here, NG, 2 * HD, LANES), BF16),
        pltpu.VMEM((packed, LANES), F32),
        pltpu.VMEM((packed, LANES), BF16),
        pltpu.VMEM((2 * nz, packed, LANES), BF16),
        pltpu.VMEM((2 * nz * packed, LANES), F32),
        pltpu.VMEM((text_rows, width), F32),
        pltpu.VMEM((text_rows, NX * wide), F32),
        pltpu.VMEM((NG * packed, LANES), F32),
        pltpu.VMEM((NG, packed, LANES), BF16),
        pltpu.VMEM((NG, packed, LANES), BF16),
        pltpu.VMEM((packed, LANES), F32),
        pltpu.VMEM((packed, LANES), BF16),
        pltpu.VMEM((plane, packed, LANES), BF16),
        pltpu.VMEM((plane * packed, LANES), F32),
        pltpu.VMEM((rows, width), F32),
        pltpu.VMEM((NX, rows, wide), BF16),
        pltpu.VMEM((NX, rows, wide), BF16),
        pltpu.VMEM((rows, wide), F32),
        pltpu.VMEM((4 * NYL, -(-half // 16) * 16, LANES), BF16),
        pltpu.VMEM((4 * NYL, -(-half // 16) * 16, LANES), BF16),
        pltpu.VMEM((2 * nz * packed, LANES), F32),
        pltpu.VMEM((nz * packed, LANES), F32),
        pltpu.VMEM((nz, packed, LANES), BF16),
        pltpu.VMEM((nz, packed, LANES), BF16),
        dma,
        dma,
        dma,
        dma((2,)),
        dma((2,)),
        dma((images_here,)),
        dma((images_here, NG)),
        dma,
        dma,
        dma,
        dma,
        dma,
        dma,
        dma,
        dma,
        dma,
        dma,
        dma,
        dma,
        dma,
        dma,
    ]
    return kernel, scratch


def on_device(patches, counts, dest, w_qkv, w_out, text):
    dp_size = lax.axis_size("dp")
    width = w_qkv.shape[2]
    texts_here = text.shape[0]
    kernel, scratch = make_kernel(dp_size, width, texts_here)
    vmem = pl.BlockSpec(memory_space=pltpu.VMEM)
    return pl.pallas_call(
        kernel,
        out_shape=(
            jax.ShapeDtypeStruct((dp_size, HD), F32),
            jax.ShapeDtypeStruct((texts_here, width), F32),
        ),
        in_specs=[vmem] * 6,
        out_specs=(vmem, vmem),
        scratch_shapes=scratch,
        compiler_params=pltpu.CompilerParams(
            collective_id=0, has_side_effects=True, vmem_limit_bytes=40 * 1024 * 1024
        ),
    )(
        counts.reshape(dp_size, dp_size),
        dest.reshape(dp_size, dp_size),
        patches,
        w_qkv.reshape(3 * HD, width),
        w_out,
        text,
    )


def solution(mesh):
    placed = (P("mp", "dp"), P(), P(), P(None, "mp", None), P("mp", None), P(("dp", "mp"), None))
    return jax.shard_map(
        on_device,
        mesh=mesh,
        in_specs=placed,
        out_specs=(P("dp", "mp"), P(("dp", "mp"), None)),
        check_vma=False,
    )
```

```python
import math

import jax
import jax.numpy as jnp
from jax import lax
from jax.experimental import pallas as pl
from jax.experimental.pallas import tpu as pltpu
from jax.sharding import PartitionSpec as P

HD = 72
MAXP = 16
NYL = 4
NYH = 2
NX = 4
NG = NYH * NX
LANES = 128
F32 = jnp.float32
BF16 = jnp.bfloat16
MESH = pl.DeviceIdType.MESH


def iota(shape, dim):
    return lax.broadcasted_iota(jnp.int32, shape, dim)


def dot_nn(a, b):
    return lax.dot_general(a, b, (((1,), (0,)), ((), ())), preferred_element_type=F32)


def dot_nt(a, b):
    return lax.dot_general(a, b, (((1,), (1,)), ((), ())), preferred_element_type=F32)


def make_kernel(dp_size, width, texts_here):
    nz = dp_size // NYL
    half = dp_size // 2
    images_here = half // NG
    pieces = width // LANES
    used = images_here * pieces
    packed = -(-used // 16) * 16
    slots = dp_size * MAXP
    half_slots = half * MAXP
    plane = NYL * NG
    rows = NYL * half
    text_rows = texts_here * 2 * nz
    wide = -(-(4 * HD) // LANES) * LANES

    def kernel(
        counts_in,
        dest_in,
        patches_in,
        w_qkv_in,
        w_out_in,
        text_arg,
        grad_image,
        grad_text,
        counts,
        dest,
        patches,
        w_qkv,
        w_out,
        text,
        in_sem,
        outbox,
        inbox,
        w_qkv_peer,
        w_out_peer,
        feats,
        qkv,
        text_f,
        text_box,
        text_in,
        text_wide,
        text_full,
        text_pad,
        part_f,
        part_b,
        part_in,
        mean_f,
        unit_box,
        unit_in,
        unit_wide,
        unit_full,
        gi_box,
        gi_in,
        gi_sum,
        gy_box,
        gy_in,
        gt_f,
        gt_in,
        gt_box,
        gtz_in,
        local_sem,
        a2a_send,
        a2a_recv,
        w_send,
        w_recv,
        g_send,
        g_recv,
        text_send,
        text_recv,
        part_send,
        part_recv,
        unit_send,
        unit_recv,
        gi_send,
        gi_recv,
        gy_send,
        gy_recv,
        gt_send,
        gt_recv,
        gtz_send,
        gtz_recv,
    ):
        me = lax.axis_index("dp")
        mp = lax.axis_index("mp")
        g, c = mp // 2, mp % 2
        z, ylo = me // NYL, me % NYL
        yhi, x = g // NX, g % NX
        y = yhi * NYL + ylo
        other = 1 - c
        partner = (me, g * 2 + other)
        my_half = me // half
        my_slot = me % half
        extra = jnp.where(my_half == c, 0, 1)

        loads = [
            pltpu.make_async_copy(src, dst, in_sem.at[i])
            for i, (src, dst) in enumerate(
                (
                    (dest_in, dest),
                    (counts_in, counts),
                    (patches_in, patches),
                    (w_qkv_in, w_qkv),
                    (w_out_in, w_out),
                    (text_arg, text),
                )
            )
        ]
        for load in loads:
            load.start()

        barrier = pltpu.get_barrier_semaphore()

        def greet(device):
            pl.semaphore_signal(barrier, inc=1, device_id=device, device_id_type=MESH)

        @pl.loop(0, half)
        def _(i):
            src = half * c + i
            greet((src, g * 2 + other))

            @pl.when(src != me)
            def _():
                greet((src, mp))

        greet(partner)

        @pl.loop(1, nz)
        def _(i):
            zz = lax.rem(z + i, nz)
            greet((zz * NYL + ylo, g * 2))
            greet((zz * NYL + ylo, g * 2 + 1))

        place = ylo * NG + g

        @pl.loop(1, plane)
        def _(i):
            q = lax.rem(place + i, plane)
            greet((z * NYL + q // NG, (q % NG) * 2 + c))

        @pl.loop(1, 2 * NYL)
        def _(i):
            q = lax.rem(y + i, 2 * NYL)
            greet((z * NYL + q % NYL, ((q // NYL) * NX + x) * 2 + other))

        loads[0].wait()
        loads[1].wait()
        first = me * dp_size
        table_rows = dp_size * dp_size // LANES
        span = iota((dp_size, LANES), 1)
        target = iota((dp_size, LANES), 0)
        index = jnp.zeros((dp_size, 1), jnp.int32)
        base = first // LANES
        own_rows = []
        for r in range(2):
            row = jnp.minimum(base + r, table_rows - 1)
            image = (base + r) * LANES + span - first
            inside = (image >= 0) & (image < dp_size) & (base + r < table_rows)
            image = jnp.where(inside, image, dp_size)
            own_rows.append((image, counts[pl.ds(row, 1), :]))
            hit = inside & (dest[pl.ds(row, 1), :] == target)
            index = index + jnp.sum(jnp.where(hit, image, 0), axis=1, keepdims=True)
        start = jnp.zeros((dp_size, 1), jnp.int32)
        count = jnp.zeros((dp_size, 1), jnp.int32)
        for image, own in own_rows:
            start = start + jnp.sum(jnp.where(image < index, own, 0), axis=1, keepdims=True)
            count = count + jnp.sum(jnp.where(image == index, own, 0), axis=1, keepdims=True)
        position = iota((dp_size, MAXP, 1), 1)
        column = jnp.where(
            position < count.reshape(dp_size, 1, 1), start.reshape(dp_size, 1, 1) + position, -1
        ).reshape(slots, 1)
        chosen = (iota((slots, patches.shape[1]), 1) == column).astype(F32).astype(BF16)
        loads[2].wait()
        picked = dot_nt(chosen, patches[...]).astype(BF16)
        outbox[...] = picked.reshape(dp_size, MAXP, HD)

        total = (2 * half - 1 + extra) + 1 + 2 * (nz - 1) + (plane - 1) + (2 * NYL - 1)
        pl.semaphore_wait(barrier, total)

        def image_copy(d):
            return pltpu.make_async_remote_copy(
                src_ref=outbox.at[d],
                dst_ref=inbox.at[c * half + my_slot],
                send_sem=a2a_send,
                recv_sem=a2a_recv,
                device_id=(d, g * 2 + my_half),
                device_id_type=MESH,
            )

        @pl.loop(0, nz)
        def _(j):
            zz = lax.rem(z + nz // 2 + ((j + 1) // 2) * (1 - 2 * (j % 2)) + nz, nz)
            for i in range(NYL):
                d = zz * NYL + lax.rem(ylo + NYL - 1 - i, NYL)

                @pl.when(d != me)
                def _():
                    image_copy(d).start()

        own_copy = pltpu.make_async_copy(
            outbox.at[me], inbox.at[c * half + my_slot], local_sem
        )

        @pl.when(my_half == c)
        def _():
            own_copy.start()

        @pl.when(my_half != c)
        def _():
            image_copy(me).start()

        def swap(src, dst, i):
            return pltpu.make_async_remote_copy(
                src_ref=src,
                dst_ref=dst,
                send_sem=w_send.at[i],
                recv_sem=w_recv.at[i],
                device_id=partner,
                device_id_type=MESH,
            )

        swap_qkv = swap(w_qkv, w_qkv_peer, 0)
        swap_out = swap(w_out, w_out_peer, 1)
        loads[3].wait()
        swap_qkv.start()
        loads[4].wait()
        swap_out.start()

        loads[5].wait()
        text_float = text[...].astype(F32)
        text_unit = text_float * lax.rsqrt(
            jnp.sum(text_float * text_float, axis=1, keepdims=True) + 1e-6
        )
        text_f[...] = jnp.zeros_like(text_f)
        for t in range(texts_here):
            for k in range(pieces):
                text_f[t * pieces + k : t * pieces + k + 1, :] = text_unit[
                    t : t + 1, k * LANES : (k + 1) * LANES
                ]
        own_text = text_f[...].astype(BF16)
        text_box[...] = own_text
        text_in[c * nz + z] = own_text

        def text_copy(zz, core):
            return pltpu.make_async_remote_copy(
                src_ref=text_box,
                dst_ref=text_in.at[c * nz + z],
                send_sem=text_send,
                recv_sem=text_recv,
                device_id=(zz * NYL + ylo, g * 2 + core),
                device_id_type=MESH,
            )

        got = jnp.zeros((half, LANES), jnp.int32)
        slot_row, slot_lane = iota((half, LANES), 0), iota((half, LANES), 1)
        half_rows = half * dp_size // LANES
        for r in range(half_rows):
            row = pl.ds(half_rows * c + r, 1)
            inside = (r * LANES + slot_lane) // dp_size == slot_row
            got = got + jnp.where(inside & (dest[row, :] == me), counts[row, :], 0)
        got = jnp.sum(got, axis=1, keepdims=True)

        @pl.when(my_half == c)
        def _():
            own_copy.wait()
            pltpu.make_async_remote_copy(
                src_ref=inbox.at[pl.ds(0, 2 * half - 1)],
                dst_ref=inbox.at[pl.ds(0, 2 * half - 1)],
                send_sem=a2a_send,
                recv_sem=a2a_recv,
                device_id=partner,
                device_id_type=MESH,
            ).wait_recv()

        @pl.when(my_half != c)
        def _():
            pltpu.make_async_remote_copy(
                src_ref=inbox,
                dst_ref=inbox,
                send_sem=a2a_send,
                recv_sem=a2a_recv,
                device_id=partner,
                device_id_type=MESH,
            ).wait_recv()

        eye = (iota((HD, HD), 0) == iota((HD, HD), 1)).astype(F32).astype(BF16)
        low = dot_nt(eye, inbox[0:half].reshape(half_slots, HD))
        high = dot_nt(eye, inbox[half : 2 * half].reshape(half_slots, HD))
        block = jnp.concatenate([low, high], axis=0).astype(BF16)
        for k in range(images_here):
            feats[k, g] = block[:, k * LANES : (k + 1) * LANES]

        across = (1 - yhi) * NX + x
        left_x, right_x = lax.rem(x + NX - 1, NX), lax.rem(x + 1, NX)
        far_x = lax.rem(x + 2, NX)

        def feat_copy(k, owner, to):
            return pltpu.make_async_remote_copy(
                src_ref=feats.at[k, owner],
                dst_ref=feats.at[k, owner],
                send_sem=g_send.at[k],
                recv_sem=g_recv.at[k, owner],
                device_id=(me, to * 2 + c),
                device_id_type=MESH,
            )

        own_row, far_row = yhi * NX, (1 - yhi) * NX
        left, right = own_row + left_x, own_row + right_x
        for k in range(images_here):
            feat_copy(k, g, across).start()
            feat_copy(k, g, left).start()
            feat_copy(k, g, right).start()

        text_copy(z, other).start()

        @pl.loop(1, nz)
        def _(i):
            zz = lax.rem(z + i, nz)
            text_copy(zz, 0).start()
            text_copy(zz, 1).start()

        def relay(k, row, flip):
            feat_copy(k, row + left_x, left).wait_recv()
            if not flip:
                feat_copy(k, row + left_x, right).start()
            feat_copy(k, row + right_x, left).wait_recv()
            if flip:
                feat_copy(k, row + right_x, left).start()

        for k in range(images_here):
            relay(k, own_row, k % 2 == 1)
            feat_copy(k, across, across).wait_recv()
            feat_copy(k, across, left).start()
            feat_copy(k, across, right).start()

        swap_qkv.wait()
        swap_out.wait()

        part_f[...] = jnp.zeros_like(part_f)
        mean_f[...] = jnp.zeros_like(mean_f)
        for k in range(images_here):
            relay(k, far_row, k % 2 == 0)
            feat_copy(k, own_row + far_x, left).wait_recv()
            feat_copy(k, far_row + far_x, left).wait_recv()
            full = feats[k].reshape(width, LANES).astype(F32)
            centred = full - jnp.sum(full, axis=0, keepdims=True) / width
            variance = jnp.sum(centred * centred, axis=0, keepdims=True) / width
            normed = (centred * lax.rsqrt(variance + 1e-6)).astype(BF16)
            qkv[k, 0] = dot_nn(w_qkv[...], normed)
            qkv[k, 1] = dot_nn(w_qkv_peer[...], normed)
        row8, lane8 = iota((NG, LANES), 0), iota((NG, LANES), 1)
        same = iota((LANES, LANES), 0) // MAXP == iota((LANES, LANES), 1) // MAXP
        terms = []
        for k in range(images_here):
            got_k = got[k * NG : (k + 1) * NG]
            got_float = got_k.astype(F32)
            real = (lane8 // MAXP == row8) & (lane8 % MAXP < got_k)
            real_float = real.astype(F32)
            key_real = jnp.max(real_float, axis=0, keepdims=True) > 0.5
            member = real_float.astype(BF16)
            keep = same & key_real
            term = jnp.zeros((NG, width), F32)
            for h, wo in enumerate((w_out, w_out_peer)):
                query = jnp.transpose(qkv[k, h, 0:HD]).astype(BF16)
                key = qkv[k, h, HD : 2 * HD].astype(BF16)
                value = qkv[k, h, 2 * HD : 3 * HD].astype(BF16)
                scores = dot_nn(query, key) / math.sqrt(HD)
                scores = jnp.where(keep, scores, -1e30)
                raised = jnp.exp(scores - jnp.max(scores, axis=1, keepdims=True))
                weights = (raised / jnp.sum(raised, axis=1, keepdims=True)).astype(BF16)
                mixed = dot_nt(value, weights).astype(BF16)
                pooled = (dot_nt(member, mixed) / got_float).astype(BF16)
                term = term + dot_nn(pooled, wo[...])
            terms.append(term)
        for k in range(images_here):
            for p in range(pieces):
                part_f[pl.ds(k * pieces + p, NG, stride=packed), :] = terms[k][
                    :, p * LANES : (p + 1) * LANES
                ]

        part_b[...] = part_f[...].astype(BF16).reshape(NG, packed, LANES)

        def part_copy(gg):
            return pltpu.make_async_remote_copy(
                src_ref=part_b.at[gg],
                dst_ref=part_in.at[g],
                send_sem=part_send,
                recv_sem=part_recv,
                device_id=(me, gg * 2 + c),
                device_id_type=MESH,
            )

        @pl.loop(1, NG)
        def _(i):
            part_copy(lax.rem(g + i, NG)).start()

        part_in[g] = part_b[g]

        here = (lane8 // MAXP == g).astype(F32).astype(BF16)
        for k in range(images_here):
            own_got = jnp.sum(
                jnp.where(iota((NG, 1), 0) == g, got[k * NG : (k + 1) * NG], 0),
                axis=0,
                keepdims=True,
            ).astype(F32)
            mean = dot_nt(here, feats[k].reshape(width, LANES)) / own_got
            for p in range(pieces):
                r = k * pieces + p
                mean_f[r : r + 1, :] = mean[0:1, p * LANES : (p + 1) * LANES]

        pltpu.make_async_remote_copy(
            src_ref=text_in.at[pl.ds(0, 2 * nz - 1)],
            dst_ref=text_in.at[pl.ds(0, 2 * nz - 1)],
            send_sem=text_send,
            recv_sem=text_recv,
            device_id=partner,
            device_id_type=MESH,
        ).wait()
        text_wide[...] = text_in[...].astype(F32).reshape(2 * nz * packed, LANES)
        for t in range(texts_here):
            for p in range(pieces):
                text_full[t * 2 * nz : (t + 1) * 2 * nz, p * LANES : (p + 1) * LANES] = (
                    text_wide[pl.ds(t * pieces + p, 2 * nz, stride=packed), :]
                )
        text_pad[...] = jnp.zeros_like(text_pad)
        for xx in range(NX):
            for q in range(4):
                m = ((q // 2) * NX + xx) * 2 + q % 2
                text_pad[:, xx * wide + q * HD : xx * wide + (q + 1) * HD] = text_full[
                    :, m * HD : (m + 1) * HD
                ]
        text_rows_b = text_full[...].astype(BF16)
        text_cols_b = text_pad[...].astype(BF16)

        part_seven = pltpu.make_async_remote_copy(
            src_ref=part_in.at[pl.ds(0, NG - 1)],
            dst_ref=part_in.at[pl.ds(0, NG - 1)],
            send_sem=part_send,
            recv_sem=part_recv,
            device_id=partner,
            device_id_type=MESH,
        )
        part_seven.wait()
        pooled = jnp.sum(part_in[...].astype(F32), axis=0) + mean_f[...]
        squares = jnp.sum(pooled * pooled, axis=1, keepdims=True)
        row_id = iota((packed, 1), 0)
        scale = jnp.zeros((packed, 1), F32)
        for k in range(images_here):
            inside = (row_id >= k * pieces) & (row_id < (k + 1) * pieces)
            norm = jnp.sum(jnp.where(inside, squares, 0.0), axis=0, keepdims=True)
            scale = jnp.where(inside, lax.rsqrt(norm + 1e-6), scale)
        own_unit = (pooled * scale).astype(BF16)
        unit_box[...] = own_unit
        unit_in[place] = own_unit

        def unit_copy(q):
            return pltpu.make_async_remote_copy(
                src_ref=unit_box,
                dst_ref=unit_in.at[place],
                send_sem=unit_send,
                recv_sem=unit_recv,
                device_id=(z * NYL + q // NG, (q % NG) * 2 + c),
                device_id_type=MESH,
            )

        @pl.loop(0, 2 * NYL)
        def _(j):
            yy = lax.rem(y + NYL + ((j + 1) // 2) * (1 - 2 * (j % 2)) + 2 * NYL, 2 * NYL)
            for i in (2, 1, 3, 0):
                q = (yy % NYL) * NG + (yy // NYL) * NX + lax.rem(x + i, NX)

                @pl.when(q != place)
                def _():
                    unit_copy(q).start()

        text_row = iota((text_rows, 1), 0)
        text_source = (text_row % nz) * NYL + ylo
        text_core = (text_row % (2 * nz)) // nz
        pair_at = text_source * dp_size + (g * 2 + text_core) * texts_here + text_row // (2 * nz)
        pair_lane = iota((text_rows, LANES), 1)
        pair_dest = jnp.zeros((text_rows, LANES), jnp.int32)
        for r in range(table_rows):
            pair_dest = pair_dest + jnp.where(
                pair_at == r * LANES + pair_lane, dest[r : r + 1, :], 0
            )
        pair_dest = jnp.sum(pair_dest, axis=1, keepdims=True)
        image_lane = iota((text_rows, rows), 1)
        image_source = c * half + image_lane % half
        image_dest = z * NYL + image_lane // half
        paired = (image_source == text_source) & (image_dest == pair_dest)
        labels = jnp.where(paired, 1.0, -1.0)

        pltpu.make_async_remote_copy(
            src_ref=unit_in.at[pl.ds(0, plane - 1)],
            dst_ref=unit_in.at[pl.ds(0, plane - 1)],
            send_sem=unit_send,
            recv_sem=unit_recv,
            device_id=partner,
            device_id_type=MESH,
        ).wait()
        unit_wide[...] = unit_in[...].astype(F32).reshape(plane * packed, LANES)
        for yy in range(NYL):
            for k in range(images_here):
                for p in range(pieces):
                    unit_full[
                        yy * half + k * NG : yy * half + (k + 1) * NG,
                        p * LANES : (p + 1) * LANES,
                    ] = unit_wide[
                        pl.ds(yy * NG * packed + k * pieces + p, NG, stride=packed), :
                    ]
        units = unit_full[...].astype(BF16)

        logits = 4.0 * dot_nt(text_rows_b, units) - 2.0
        dscaled = -4.0 * labels / (1.0 + jnp.exp(labels * logits))
        turned = jnp.transpose(dscaled).astype(BF16)
        dscaled = dscaled.astype(BF16)

        for xx in range(NX):
            gi_box[xx] = dot_nn(turned, text_cols_b[:, xx * wide : (xx + 1) * wide]).astype(BF16)

        def gi_copy(xx):
            return pltpu.make_async_remote_copy(
                src_ref=gi_box.at[xx],
                dst_ref=gi_in.at[x],
                send_sem=gi_send,
                recv_sem=gi_recv,
                device_id=(me, (yhi * NX + xx) * 2 + c),
                device_id_type=MESH,
            )

        for i in range(1, NX):
            gi_copy(lax.rem(x + i, NX)).start()
        gi_in[x] = gi_box[x]

        text_grad = dot_nn(dscaled, units)
        gt_f[...] = jnp.zeros_like(gt_f)
        for t in range(texts_here):
            for p in range(pieces):
                gt_f[pl.ds(t * pieces + p, 2 * nz, stride=packed), :] = text_grad[
                    t * 2 * nz : (t + 1) * 2 * nz, p * LANES : (p + 1) * LANES
                ]
        core_rows = nz * packed
        gt_copy = pltpu.make_async_remote_copy(
            src_ref=gt_f.at[pl.ds(pl.multiple_of(other * core_rows, 8), core_rows)],
            dst_ref=gt_in,
            send_sem=gt_send,
            recv_sem=gt_recv,
            device_id=partner,
            device_id_type=MESH,
        )
        gt_copy.start()

        gt_copy.wait()
        own_sums = gt_f[pl.ds(pl.multiple_of(c * core_rows, 8), core_rows), :]
        gt_box[...] = (own_sums + gt_in[...]).astype(BF16).reshape(nz, packed, LANES)

        def gtz_copy(zz):
            return pltpu.make_async_remote_copy(
                src_ref=gt_box.at[zz],
                dst_ref=gtz_in.at[z],
                send_sem=gtz_send,
                recv_sem=gtz_recv,
                device_id=(zz * NYL + ylo, mp),
                device_id_type=MESH,
            )

        @pl.loop(1, nz)
        def _(i):
            gtz_copy(lax.rem(z + i, nz)).start()

        gtz_in[z] = gt_box[z]

        pltpu.make_async_remote_copy(
            src_ref=gi_in.at[pl.ds(0, NX - 1)],
            dst_ref=gi_in.at[pl.ds(0, NX - 1)],
            send_sem=gi_send,
            recv_sem=gi_recv,
            device_id=partner,
            device_id_type=MESH,
        ).wait()
        gi_sum[...] = jnp.sum(gi_in[...].astype(F32), axis=0)

        gy_box[...] = jnp.zeros_like(gy_box)
        for yy in range(2 * NYL):
            for core in range(2):
                q = (yy // NYL) * 2 + core
                r = (yy % NYL) * half
                gy_box[yy * 2 + core, 0:half, 0:HD] = gi_sum[
                    r : r + half, q * HD : (q + 1) * HD
                ].astype(BF16)

        def gy_copy(yy, core):
            return pltpu.make_async_remote_copy(
                src_ref=gy_box.at[yy * 2 + core],
                dst_ref=gy_in.at[c * 2 * NYL + y],
                send_sem=gy_send,
                recv_sem=gy_recv,
                device_id=(z * NYL + yy % NYL, ((yy // NYL) * NX + x) * 2 + core),
                device_id_type=MESH,
            )

        gy_copy(y, other).start()

        @pl.loop(1, 2 * NYL)
        def _(i):
            yy = lax.rem(y + i, 2 * NYL)
            gy_copy(yy, 0).start()
            gy_copy(yy, 1).start()

        gy_in[c * 2 * NYL + y] = gy_box[y * 2 + c]

        pltpu.make_async_remote_copy(
            src_ref=gtz_in.at[pl.ds(0, nz - 1)],
            dst_ref=gtz_in.at[pl.ds(0, nz - 1)],
            send_sem=gtz_send,
            recv_sem=gtz_recv,
            device_id=partner,
            device_id_type=MESH,
        ).wait()
        summed = jnp.sum(gtz_in[...].astype(F32), axis=0)
        for t in range(texts_here):
            for p in range(pieces):
                r = t * pieces + p
                grad_text[t : t + 1, p * LANES : (p + 1) * LANES] = summed[r : r + 1, :]

        pltpu.make_async_remote_copy(
            src_ref=gy_in.at[pl.ds(0, 4 * NYL - 1)],
            dst_ref=gy_in.at[pl.ds(0, 4 * NYL - 1)],
            send_sem=gy_send,
            recv_sem=gy_recv,
            device_id=partner,
            device_id_type=MESH,
        ).wait()
        for core in range(2):
            part = gy_in[core * 2 * NYL : (core + 1) * 2 * NYL].astype(F32)
            grad_image[core * half : (core + 1) * half, :] = jnp.sum(part, axis=0)[0:half, 0:HD]

        @pl.when(my_half == c)
        def _():
            pltpu.make_async_remote_copy(
                src_ref=outbox.at[pl.ds(0, dp_size - 1)],
                dst_ref=outbox.at[pl.ds(0, dp_size - 1)],
                send_sem=a2a_send,
                recv_sem=a2a_recv,
                device_id=partner,
                device_id_type=MESH,
            ).wait_send()

        @pl.when(my_half != c)
        def _():
            pltpu.make_async_remote_copy(
                src_ref=outbox,
                dst_ref=outbox,
                send_sem=a2a_send,
                recv_sem=a2a_recv,
                device_id=partner,
                device_id_type=MESH,
            ).wait_send()

        for k in range(images_here):
            pltpu.make_async_remote_copy(
                src_ref=feats.at[k, pl.ds(0, NG - 1)],
                dst_ref=feats.at[k, pl.ds(0, NG - 1)],
                send_sem=g_send.at[k],
                recv_sem=g_recv.at[k, 0],
                device_id=partner,
                device_id_type=MESH,
            ).wait_send()

    dma = pltpu.SemaphoreType.DMA
    scratch = [
        pltpu.VMEM((dp_size * dp_size // LANES, LANES), jnp.int32),
        pltpu.VMEM((dp_size * dp_size // LANES, LANES), jnp.int32),
        pltpu.VMEM((HD, dp_size * MAXP), BF16),
        pltpu.VMEM((3 * HD, width), BF16),
        pltpu.VMEM((HD, width), BF16),
        pltpu.VMEM((texts_here, width), BF16),
        dma((6,)),
        pltpu.VMEM((dp_size, MAXP, HD), BF16),
        pltpu.VMEM((2 * half, MAXP, HD), BF16),
        pltpu.VMEM((3 * HD, width), BF16),
        pltpu.VMEM((HD, width), BF16),
        pltpu.VMEM((images_here, NG, 2 * HD, LANES), BF16),
        pltpu.VMEM((images_here, 2, 3 * HD, LANES), F32),
        pltpu.VMEM((packed, LANES), F32),
        pltpu.VMEM((packed, LANES), BF16),
        pltpu.VMEM((2 * nz, packed, LANES), BF16),
        pltpu.VMEM((2 * nz * packed, LANES), F32),
        pltpu.VMEM((text_rows, width), F32),
        pltpu.VMEM((text_rows, NX * wide), F32),
        pltpu.VMEM((NG * packed, LANES), F32),
        pltpu.VMEM((NG, packed, LANES), BF16),
        pltpu.VMEM((NG, packed, LANES), BF16),
        pltpu.VMEM((packed, LANES), F32),
        pltpu.VMEM((packed, LANES), BF16),
        pltpu.VMEM((plane, packed, LANES), BF16),
        pltpu.VMEM((plane * packed, LANES), F32),
        pltpu.VMEM((rows, width), F32),
        pltpu.VMEM((NX, rows, wide), BF16),
        pltpu.VMEM((NX, rows, wide), BF16),
        pltpu.VMEM((rows, wide), F32),
        pltpu.VMEM((4 * NYL, -(-half // 16) * 16, LANES), BF16),
        pltpu.VMEM((4 * NYL, -(-half // 16) * 16, LANES), BF16),
        pltpu.VMEM((2 * nz * packed, LANES), F32),
        pltpu.VMEM((nz * packed, LANES), F32),
        pltpu.VMEM((nz, packed, LANES), BF16),
        pltpu.VMEM((nz, packed, LANES), BF16),
        dma,
        dma,
        dma,
        dma((2,)),
        dma((2,)),
        dma((images_here,)),
        dma((images_here, NG)),
        dma,
        dma,
        dma,
        dma,
        dma,
        dma,
        dma,
        dma,
        dma,
        dma,
        dma,
        dma,
        dma,
        dma,
    ]
    return kernel, scratch


def on_device(patches, counts, dest, w_qkv, w_out, text):
    dp_size = lax.axis_size("dp")
    width = w_qkv.shape[2]
    texts_here = text.shape[0]
    kernel, scratch = make_kernel(dp_size, width, texts_here)
    vmem = pl.BlockSpec(memory_space=pltpu.VMEM)
    return pl.pallas_call(
        kernel,
        out_shape=(
            jax.ShapeDtypeStruct((dp_size, HD), F32),
            jax.ShapeDtypeStruct((texts_here, width), F32),
        ),
        in_specs=[pl.BlockSpec(memory_space=pltpu.HBM)] * 6,
        out_specs=(vmem, vmem),
        scratch_shapes=scratch,
        compiler_params=pltpu.CompilerParams(
            collective_id=0, has_side_effects=True, vmem_limit_bytes=40 * 1024 * 1024
        ),
    )(
        counts.reshape(-1, LANES),
        dest.reshape(-1, LANES),
        patches,
        w_qkv.reshape(3 * HD, width),
        w_out,
        text,
    )


def solution(mesh):
    placed = (P("mp", "dp"), P(), P(), P(None, "mp", None), P("mp", None), P(("dp", "mp"), None))
    return jax.shard_map(
        on_device,
        mesh=mesh,
        in_specs=placed,
        out_specs=(P("dp", "mp"), P(("dp", "mp"), None)),
        check_vma=False,
    )
```

```python
import math

import jax
import jax.numpy as jnp
from jax import lax
from jax.experimental import pallas as pl
from jax.experimental.pallas import tpu as pltpu
from jax.sharding import PartitionSpec as P

HD = 72
MAXP = 16
NYL = 4
NYH = 2
NX = 4
NG = NYH * NX
LANES = 128
F32 = jnp.float32
BF16 = jnp.bfloat16
MESH = pl.DeviceIdType.MESH


def iota(shape, dim):
    return lax.broadcasted_iota(jnp.int32, shape, dim)


def dot_nn(a, b):
    return lax.dot_general(a, b, (((1,), (0,)), ((), ())), preferred_element_type=F32)


def dot_nt(a, b):
    return lax.dot_general(a, b, (((1,), (1,)), ((), ())), preferred_element_type=F32)


def wrap(value, size):
    return jnp.where(value >= size, value - size, value)


def make_kernel(dp_size, width, texts_here):
    nz = dp_size // NYL
    half = dp_size // 2
    images_here = half // NG
    pieces = width // LANES
    used = images_here * pieces
    packed = -(-used // 16) * 16
    slots = dp_size * MAXP
    half_slots = half * MAXP
    plane = NYL * NG
    rows = NYL * half
    text_rows = texts_here * 2 * nz
    wide = -(-(4 * HD) // LANES) * LANES

    def kernel(
        counts_in,
        dest_in,
        patches_in,
        w_qkv_in,
        w_out_in,
        text_arg,
        grad_image,
        grad_text,
        counts,
        dest,
        patches,
        w_qkv,
        w_out,
        text,
        in_sem,
        outbox,
        inbox,
        w_qkv_peer,
        w_out_peer,
        feats,
        qkv,
        text_f,
        text_box,
        text_in,
        text_wide,
        text_full,
        text_pad,
        part_f,
        part_b,
        part_in,
        mean_f,
        unit_box,
        unit_in,
        unit_wide,
        unit_full,
        gi_box,
        gi_in,
        gi_sum,
        gy_box,
        gy_in,
        gt_f,
        gt_in,
        gt_box,
        gtz_in,
        local_sem,
        a2a_send,
        a2a_recv,
        w_send,
        w_recv,
        g_send,
        g_recv,
        text_send,
        text_recv,
        swap_send,
        swap_recv,
        part_send,
        part_recv,
        unit_send,
        unit_recv,
        gi_send,
        gi_recv,
        gy_send,
        gy_recv,
        gt_send,
        gt_recv,
        gtz_send,
        gtz_recv,
    ):
        me = lax.axis_index("dp")
        mp = lax.axis_index("mp")
        g, c = mp // 2, mp % 2
        z, ylo = me // NYL, me % NYL
        yhi, x = g // NX, g % NX
        y = yhi * NYL + ylo
        other = 1 - c
        partner = (me, g * 2 + other)
        my_half = me // half
        my_slot = me % half
        extra = jnp.where(my_half == c, 0, 1)

        loads = [
            pltpu.make_async_copy(src, dst, in_sem.at[i])
            for i, (src, dst) in enumerate(
                (
                    (dest_in, dest),
                    (counts_in, counts),
                    (patches_in, patches),
                    (w_qkv_in, w_qkv),
                    (w_out_in, w_out),
                    (text_arg, text),
                )
            )
        ]
        for load in loads:
            load.start()

        barrier = pltpu.get_barrier_semaphore()

        def greet(device):
            pl.semaphore_signal(barrier, inc=1, device_id=device, device_id_type=MESH)

        @pl.loop(0, half)
        def _(i):
            src = half * c + i
            greet((src, g * 2 + other))

            @pl.when(src != me)
            def _():
                greet((src, mp))

        greet(partner)

        @pl.loop(1, nz)
        def _(i):
            greet((wrap(z + i, nz) * NYL + ylo, mp))

        place = ylo * NG + g

        @pl.loop(1, plane)
        def _(i):
            q = (place + i) % plane
            greet((z * NYL + q // NG, (q % NG) * 2 + c))

        @pl.loop(1, 2 * NYL)
        def _(i):
            q = (y + i) % (2 * NYL)
            greet((z * NYL + q % NYL, ((q // NYL) * NX + x) * 2 + other))

        for buffer in (text_f, text_pad, part_f, mean_f, gt_f, gy_box):
            buffer[...] = jnp.zeros_like(buffer)

        loads[0].wait()
        loads[1].wait()
        first = me * dp_size
        table_rows = dp_size * dp_size // LANES
        span = iota((dp_size, LANES), 1)
        target = iota((dp_size, LANES), 0)
        index = jnp.zeros((dp_size, 1), jnp.int32)
        base = first // LANES
        own_rows = []
        for r in range(2):
            row = jnp.minimum(base + r, table_rows - 1)
            image = (base + r) * LANES + span - first
            inside = (image >= 0) & (image < dp_size) & (base + r < table_rows)
            image = jnp.where(inside, image, dp_size)
            own_rows.append((image, counts[pl.ds(row, 1), :]))
            hit = inside & (dest[pl.ds(row, 1), :] == target)
            index = index + jnp.sum(jnp.where(hit, image, 0), axis=1, keepdims=True)
        start = jnp.zeros((dp_size, 1), jnp.int32)
        count = jnp.zeros((dp_size, 1), jnp.int32)
        for image, own in own_rows:
            start = start + jnp.sum(jnp.where(image < index, own, 0), axis=1, keepdims=True)
            count = count + jnp.sum(jnp.where(image == index, own, 0), axis=1, keepdims=True)
        position = iota((dp_size, MAXP, 1), 1)
        column = jnp.where(
            position < count.reshape(dp_size, 1, 1), start.reshape(dp_size, 1, 1) + position, -1
        ).reshape(slots, 1)
        chosen = (iota((slots, patches.shape[1]), 1) == column).astype(F32).astype(BF16)
        loads[2].wait()
        picked = dot_nt(chosen, patches[...]).astype(BF16)
        outbox[...] = picked.reshape(dp_size, MAXP, HD)

        total = (2 * half - 1 + extra) + 1 + (nz - 1) + (plane - 1) + (2 * NYL - 1)
        pl.semaphore_wait(barrier, total)

        def image_copy(d):
            return pltpu.make_async_remote_copy(
                src_ref=outbox.at[d],
                dst_ref=inbox.at[c * half + my_slot],
                send_sem=a2a_send,
                recv_sem=a2a_recv,
                device_id=(d, g * 2 + my_half),
                device_id_type=MESH,
            )

        @pl.loop(0, nz)
        def _(j):
            step = (j + 1) // 2
            zz = wrap(z + nz // 2 + jnp.where(j % 2 == 1, nz - step, step), nz)
            zz = wrap(zz, nz)
            for i in range(NYL):
                d = zz * NYL + (ylo + NYL - 1 - i) % NYL

                @pl.when(d != me)
                def _():
                    image_copy(d).start()

        own_copy = pltpu.make_async_copy(
            outbox.at[me], inbox.at[c * half + my_slot], local_sem
        )

        @pl.when(my_half == c)
        def _():
            own_copy.start()

        @pl.when(my_half != c)
        def _():
            image_copy(me).start()

        def swap(src, dst, i):
            return pltpu.make_async_remote_copy(
                src_ref=src,
                dst_ref=dst,
                send_sem=w_send.at[i],
                recv_sem=w_recv.at[i],
                device_id=partner,
                device_id_type=MESH,
            )

        swap_qkv = swap(w_qkv, w_qkv_peer, 0)
        swap_out = swap(w_out, w_out_peer, 1)
        loads[3].wait()
        swap_qkv.start()
        loads[4].wait()
        swap_out.start()

        loads[5].wait()
        text_float = text[...].astype(F32)
        text_unit = text_float * lax.rsqrt(
            jnp.sum(text_float * text_float, axis=1, keepdims=True) + 1e-6
        )
        for t in range(texts_here):
            for k in range(pieces):
                text_f[t * pieces + k : t * pieces + k + 1, :] = text_unit[
                    t : t + 1, k * LANES : (k + 1) * LANES
                ]
        own_text = text_f[...].astype(BF16)
        text_box[...] = own_text
        text_in[c * nz + z] = own_text

        def text_copy(zz):
            return pltpu.make_async_remote_copy(
                src_ref=text_box,
                dst_ref=text_in.at[c * nz + z],
                send_sem=text_send,
                recv_sem=text_recv,
                device_id=(zz * NYL + ylo, mp),
                device_id_type=MESH,
            )

        own_texts = text_in.at[pl.ds(c * nz, nz)]
        text_swap = pltpu.make_async_remote_copy(
            src_ref=own_texts,
            dst_ref=own_texts,
            send_sem=swap_send,
            recv_sem=swap_recv,
            device_id=partner,
            device_id_type=MESH,
        )

        got = jnp.zeros((half, LANES), jnp.int32)
        slot_row, slot_lane = iota((half, LANES), 0), iota((half, LANES), 1)
        half_rows = half * dp_size // LANES
        for r in range(half_rows):
            row = pl.ds(half_rows * c + r, 1)
            inside = (r * LANES + slot_lane) // dp_size == slot_row
            got = got + jnp.where(inside & (dest[row, :] == me), counts[row, :], 0)
        got = jnp.sum(got, axis=1, keepdims=True)

        @pl.when(my_half == c)
        def _():
            own_copy.wait()
            pltpu.make_async_remote_copy(
                src_ref=inbox.at[pl.ds(0, 2 * half - 1)],
                dst_ref=inbox.at[pl.ds(0, 2 * half - 1)],
                send_sem=a2a_send,
                recv_sem=a2a_recv,
                device_id=partner,
                device_id_type=MESH,
            ).wait_recv()

        @pl.when(my_half != c)
        def _():
            pltpu.make_async_remote_copy(
                src_ref=inbox,
                dst_ref=inbox,
                send_sem=a2a_send,
                recv_sem=a2a_recv,
                device_id=partner,
                device_id_type=MESH,
            ).wait_recv()

        eye = (iota((HD, HD), 0) == iota((HD, HD), 1)).astype(F32).astype(BF16)
        low = dot_nt(eye, inbox[0:half].reshape(half_slots, HD))
        high = dot_nt(eye, inbox[half : 2 * half].reshape(half_slots, HD))
        block = jnp.concatenate([low, high], axis=0).astype(BF16)
        for k in range(images_here):
            feats[k, g] = block[:, k * LANES : (k + 1) * LANES]

        across = (1 - yhi) * NX + x
        left_x, right_x = lax.rem(x + NX - 1, NX), lax.rem(x + 1, NX)
        far_x = lax.rem(x + 2, NX)

        def feat_copy(k, owner, to):
            return pltpu.make_async_remote_copy(
                src_ref=feats.at[k, owner],
                dst_ref=feats.at[k, owner],
                send_sem=g_send.at[k],
                recv_sem=g_recv.at[k, owner],
                device_id=(me, to * 2 + c),
                device_id_type=MESH,
            )

        own_row, far_row = yhi * NX, (1 - yhi) * NX
        left, right = own_row + left_x, own_row + right_x
        for k in range(images_here):
            feat_copy(k, g, across).start()
            feat_copy(k, g, left).start()
            feat_copy(k, g, right).start()

        @pl.loop(1, nz)
        def _(i):
            text_copy(wrap(z + i, nz)).start()

        for k in range(images_here):
            feat_copy(k, left, left).wait_recv()
            if k % 2 == 0:
                feat_copy(k, left, right).start()
            feat_copy(k, right, left).wait_recv()
            if k % 2 == 1:
                feat_copy(k, right, left).start()
            feat_copy(k, across, across).wait_recv()
            feat_copy(k, across, own_row + far_x).start()
            feat_copy(k, across, left).start()
            feat_copy(k, across, right).start()

        swap_qkv.wait()
        swap_out.wait()

        for k in range(images_here):
            feat_copy(k, own_row + far_x, left).wait_recv()
            for xx in (left_x, right_x, far_x):
                feat_copy(k, far_row + xx, left).wait_recv()
            full = feats[k].reshape(width, LANES).astype(F32)
            centred = full - jnp.sum(full, axis=0, keepdims=True) / width
            variance = jnp.sum(centred * centred, axis=0, keepdims=True) / width
            normed = (centred * lax.rsqrt(variance + 1e-6)).astype(BF16)
            qkv[k, 0] = dot_nn(w_qkv[...], normed)
            qkv[k, 1] = dot_nn(w_qkv_peer[...], normed)
        pltpu.make_async_remote_copy(
            src_ref=text_in.at[pl.ds(0, nz - 1)],
            dst_ref=text_in.at[pl.ds(0, nz - 1)],
            send_sem=text_send,
            recv_sem=text_recv,
            device_id=partner,
            device_id_type=MESH,
        ).wait()
        text_swap.start()
        row8, lane8 = iota((NG, LANES), 0), iota((NG, LANES), 1)
        same = iota((LANES, LANES), 0) // MAXP == iota((LANES, LANES), 1) // MAXP
        terms = []
        for k in range(images_here):
            got_k = got[k * NG : (k + 1) * NG]
            got_float = got_k.astype(F32)
            real = (lane8 // MAXP == row8) & (lane8 % MAXP < got_k)
            real_float = real.astype(F32)
            key_real = jnp.max(real_float, axis=0, keepdims=True) > 0.5
            member = real_float.astype(BF16)
            keep = same & key_real
            term = jnp.zeros((NG, width), F32)
            for h, wo in enumerate((w_out, w_out_peer)):
                query = jnp.transpose(qkv[k, h, 0:HD]).astype(BF16)
                key = qkv[k, h, HD : 2 * HD].astype(BF16)
                value = qkv[k, h, 2 * HD : 3 * HD].astype(BF16)
                scores = dot_nn(query, key) / math.sqrt(HD)
                scores = jnp.where(keep, scores, -1e30)
                raised = jnp.exp(scores - jnp.max(scores, axis=1, keepdims=True))
                weights = (raised / jnp.sum(raised, axis=1, keepdims=True)).astype(BF16)
                mixed = dot_nt(value, weights).astype(BF16)
                pooled = (dot_nt(member, mixed) / got_float).astype(BF16)
                term = term + dot_nn(pooled, wo[...])
            terms.append(term)
        for k in range(images_here):
            for p in range(pieces):
                part_f[pl.ds(k * pieces + p, NG, stride=packed), :] = terms[k][
                    :, p * LANES : (p + 1) * LANES
                ]

        part_b[...] = part_f[...].astype(BF16).reshape(NG, packed, LANES)

        def part_copy(gg):
            return pltpu.make_async_remote_copy(
                src_ref=part_b.at[gg],
                dst_ref=part_in.at[g],
                send_sem=part_send,
                recv_sem=part_recv,
                device_id=(me, gg * 2 + c),
                device_id_type=MESH,
            )

        @pl.loop(1, NG)
        def _(i):
            part_copy((g + i) % NG).start()

        part_in[g] = part_b[g]

        here = (lane8 // MAXP == g).astype(F32).astype(BF16)
        for k in range(images_here):
            own_got = jnp.sum(
                jnp.where(iota((NG, 1), 0) == g, got[k * NG : (k + 1) * NG], 0),
                axis=0,
                keepdims=True,
            ).astype(F32)
            mean = dot_nt(here, feats[k].reshape(width, LANES)) / own_got
            for p in range(pieces):
                r = k * pieces + p
                mean_f[r : r + 1, :] = mean[0:1, p * LANES : (p + 1) * LANES]

        text_swap.wait()
        text_wide[...] = text_in[...].astype(F32).reshape(2 * nz * packed, LANES)
        for t in range(texts_here):
            for p in range(pieces):
                text_full[t * 2 * nz : (t + 1) * 2 * nz, p * LANES : (p + 1) * LANES] = (
                    text_wide[pl.ds(t * pieces + p, 2 * nz, stride=packed), :]
                )
        for xx in range(NX):
            for q in range(4):
                m = ((q // 2) * NX + xx) * 2 + q % 2
                text_pad[:, xx * wide + q * HD : xx * wide + (q + 1) * HD] = text_full[
                    :, m * HD : (m + 1) * HD
                ]
        text_rows_b = text_full[...].astype(BF16)
        text_cols_b = text_pad[...].astype(BF16)

        part_seven = pltpu.make_async_remote_copy(
            src_ref=part_in.at[pl.ds(0, NG - 1)],
            dst_ref=part_in.at[pl.ds(0, NG - 1)],
            send_sem=part_send,
            recv_sem=part_recv,
            device_id=partner,
            device_id_type=MESH,
        )
        part_seven.wait()
        pooled = jnp.sum(part_in[...].astype(F32), axis=0) + mean_f[...]
        squares = jnp.sum(pooled * pooled, axis=1, keepdims=True)
        row_id = iota((packed, 1), 0)
        scale = jnp.zeros((packed, 1), F32)
        for k in range(images_here):
            inside = (row_id >= k * pieces) & (row_id < (k + 1) * pieces)
            norm = jnp.sum(jnp.where(inside, squares, 0.0), axis=0, keepdims=True)
            scale = jnp.where(inside, lax.rsqrt(norm + 1e-6), scale)
        own_unit = (pooled * scale).astype(BF16)
        unit_box[...] = own_unit
        unit_in[place] = own_unit

        def unit_copy(q):
            return pltpu.make_async_remote_copy(
                src_ref=unit_box,
                dst_ref=unit_in.at[place],
                send_sem=unit_send,
                recv_sem=unit_recv,
                device_id=(z * NYL + q // NG, (q % NG) * 2 + c),
                device_id_type=MESH,
            )

        @pl.loop(0, 2 * NYL)
        def _(j):
            step = (j + 1) // 2
            yy = (y + NYL + jnp.where(j % 2 == 1, 2 * NYL - step, step)) % (2 * NYL)
            for i in (2, 1, 3, 0):
                q = (yy % NYL) * NG + (yy // NYL) * NX + (x + i) % NX

                @pl.when(q != place)
                def _():
                    unit_copy(q).start()

        text_row = iota((text_rows, 1), 0)
        text_source = (text_row % nz) * NYL + ylo
        text_core = (text_row % (2 * nz)) // nz
        pair_at = text_source * dp_size + (g * 2 + text_core) * texts_here + text_row // (2 * nz)
        pair_lane = iota((text_rows, LANES), 1)
        pair_dest = jnp.zeros((text_rows, LANES), jnp.int32)
        for r in range(table_rows):
            pair_dest = pair_dest + jnp.where(
                pair_at == r * LANES + pair_lane, dest[r : r + 1, :], 0
            )
        pair_dest = jnp.sum(pair_dest, axis=1, keepdims=True)
        image_lane = iota((text_rows, rows), 1)
        image_source = c * half + image_lane % half
        image_dest = z * NYL + image_lane // half
        paired = (image_source == text_source) & (image_dest == pair_dest)
        labels = jnp.where(paired, 1.0, -1.0)

        pltpu.make_async_remote_copy(
            src_ref=unit_in.at[pl.ds(0, plane - 1)],
            dst_ref=unit_in.at[pl.ds(0, plane - 1)],
            send_sem=unit_send,
            recv_sem=unit_recv,
            device_id=partner,
            device_id_type=MESH,
        ).wait()
        unit_wide[...] = unit_in[...].astype(F32).reshape(plane * packed, LANES)
        for yy in range(NYL):
            for k in range(images_here):
                for p in range(pieces):
                    unit_full[
                        yy * half + k * NG : yy * half + (k + 1) * NG,
                        p * LANES : (p + 1) * LANES,
                    ] = unit_wide[
                        pl.ds(yy * NG * packed + k * pieces + p, NG, stride=packed), :
                    ]
        units = unit_full[...].astype(BF16)

        logits = 4.0 * dot_nt(text_rows_b, units) - 2.0
        dscaled = -4.0 * labels / (1.0 + jnp.exp(labels * logits))
        turned = jnp.transpose(dscaled).astype(BF16)
        dscaled = dscaled.astype(BF16)

        for xx in range(NX):
            gi_box[xx] = dot_nn(turned, text_cols_b[:, xx * wide : (xx + 1) * wide]).astype(BF16)

        def gi_copy(xx):
            return pltpu.make_async_remote_copy(
                src_ref=gi_box.at[xx],
                dst_ref=gi_in.at[x],
                send_sem=gi_send,
                recv_sem=gi_recv,
                device_id=(me, (yhi * NX + xx) * 2 + c),
                device_id_type=MESH,
            )

        for i in range(1, NX):
            gi_copy(lax.rem(x + i, NX)).start()
        gi_in[x] = gi_box[x]

        text_grad = dot_nn(dscaled, units)
        for t in range(texts_here):
            for p in range(pieces):
                gt_f[pl.ds(t * pieces + p, 2 * nz, stride=packed), :] = text_grad[
                    t * 2 * nz : (t + 1) * 2 * nz, p * LANES : (p + 1) * LANES
                ]
        core_rows = nz * packed
        gt_copy = pltpu.make_async_remote_copy(
            src_ref=gt_f.at[pl.ds(pl.multiple_of(other * core_rows, 8), core_rows)],
            dst_ref=gt_in,
            send_sem=gt_send,
            recv_sem=gt_recv,
            device_id=partner,
            device_id_type=MESH,
        )
        gt_copy.start()

        gt_copy.wait()
        own_sums = gt_f[pl.ds(pl.multiple_of(c * core_rows, 8), core_rows), :]
        gt_box[...] = (own_sums + gt_in[...]).astype(BF16).reshape(nz, packed, LANES)

        def gtz_copy(zz):
            return pltpu.make_async_remote_copy(
                src_ref=gt_box.at[zz],
                dst_ref=gtz_in.at[z],
                send_sem=gtz_send,
                recv_sem=gtz_recv,
                device_id=(zz * NYL + ylo, mp),
                device_id_type=MESH,
            )

        @pl.loop(1, nz)
        def _(i):
            gtz_copy(wrap(z + i, nz)).start()

        gtz_in[z] = gt_box[z]

        pltpu.make_async_remote_copy(
            src_ref=gi_in.at[pl.ds(0, NX - 1)],
            dst_ref=gi_in.at[pl.ds(0, NX - 1)],
            send_sem=gi_send,
            recv_sem=gi_recv,
            device_id=partner,
            device_id_type=MESH,
        ).wait()
        gi_sum[...] = jnp.sum(gi_in[...].astype(F32), axis=0)

        for yy in range(2 * NYL):
            for core in range(2):
                q = (yy // NYL) * 2 + core
                r = (yy % NYL) * half
                gy_box[yy * 2 + core, 0:half, 0:HD] = gi_sum[
                    r : r + half, q * HD : (q + 1) * HD
                ].astype(BF16)

        def gy_copy(yy, core):
            return pltpu.make_async_remote_copy(
                src_ref=gy_box.at[yy * 2 + core],
                dst_ref=gy_in.at[c * 2 * NYL + y],
                send_sem=gy_send,
                recv_sem=gy_recv,
                device_id=(z * NYL + yy % NYL, ((yy // NYL) * NX + x) * 2 + core),
                device_id_type=MESH,
            )

        gy_copy(y, other).start()

        @pl.loop(1, 2 * NYL)
        def _(i):
            yy = (y + i) % (2 * NYL)
            gy_copy(yy, 0).start()
            gy_copy(yy, 1).start()

        gy_in[c * 2 * NYL + y] = gy_box[y * 2 + c]

        pltpu.make_async_remote_copy(
            src_ref=gtz_in.at[pl.ds(0, nz - 1)],
            dst_ref=gtz_in.at[pl.ds(0, nz - 1)],
            send_sem=gtz_send,
            recv_sem=gtz_recv,
            device_id=partner,
            device_id_type=MESH,
        ).wait()
        summed = jnp.sum(gtz_in[...].astype(F32), axis=0)
        for t in range(texts_here):
            for p in range(pieces):
                r = t * pieces + p
                grad_text[t : t + 1, p * LANES : (p + 1) * LANES] = summed[r : r + 1, :]

        pltpu.make_async_remote_copy(
            src_ref=gy_in.at[pl.ds(0, 4 * NYL - 1)],
            dst_ref=gy_in.at[pl.ds(0, 4 * NYL - 1)],
            send_sem=gy_send,
            recv_sem=gy_recv,
            device_id=partner,
            device_id_type=MESH,
        ).wait()
        for core in range(2):
            part = gy_in[core * 2 * NYL : (core + 1) * 2 * NYL].astype(F32)
            grad_image[core * half : (core + 1) * half, :] = jnp.sum(part, axis=0)[0:half, 0:HD]

        @pl.when(my_half == c)
        def _():
            pltpu.make_async_remote_copy(
                src_ref=outbox.at[pl.ds(0, dp_size - 1)],
                dst_ref=outbox.at[pl.ds(0, dp_size - 1)],
                send_sem=a2a_send,
                recv_sem=a2a_recv,
                device_id=partner,
                device_id_type=MESH,
            ).wait_send()

        @pl.when(my_half != c)
        def _():
            pltpu.make_async_remote_copy(
                src_ref=outbox,
                dst_ref=outbox,
                send_sem=a2a_send,
                recv_sem=a2a_recv,
                device_id=partner,
                device_id_type=MESH,
            ).wait_send()

        for k in range(images_here):
            pltpu.make_async_remote_copy(
                src_ref=feats.at[k, pl.ds(0, NG - 1)],
                dst_ref=feats.at[k, pl.ds(0, NG - 1)],
                send_sem=g_send.at[k],
                recv_sem=g_recv.at[k, 0],
                device_id=partner,
                device_id_type=MESH,
            ).wait_send()

    dma = pltpu.SemaphoreType.DMA
    scratch = [
        pltpu.VMEM((dp_size * dp_size // LANES, LANES), jnp.int32),
        pltpu.VMEM((dp_size * dp_size // LANES, LANES), jnp.int32),
        pltpu.VMEM((HD, dp_size * MAXP), BF16),
        pltpu.VMEM((3 * HD, width), BF16),
        pltpu.VMEM((HD, width), BF16),
        pltpu.VMEM((texts_here, width), BF16),
        dma((6,)),
        pltpu.VMEM((dp_size, MAXP, HD), BF16),
        pltpu.VMEM((2 * half, MAXP, HD), BF16),
        pltpu.VMEM((3 * HD, width), BF16),
        pltpu.VMEM((HD, width), BF16),
        pltpu.VMEM((images_here, NG, 2 * HD, LANES), BF16),
        pltpu.VMEM((images_here, 2, 3 * HD, LANES), F32),
        pltpu.VMEM((packed, LANES), F32),
        pltpu.VMEM((packed, LANES), BF16),
        pltpu.VMEM((2 * nz, packed, LANES), BF16),
        pltpu.VMEM((2 * nz * packed, LANES), F32),
        pltpu.VMEM((text_rows, width), F32),
        pltpu.VMEM((text_rows, NX * wide), F32),
        pltpu.VMEM((NG * packed, LANES), F32),
        pltpu.VMEM((NG, packed, LANES), BF16),
        pltpu.VMEM((NG, packed, LANES), BF16),
        pltpu.VMEM((packed, LANES), F32),
        pltpu.VMEM((packed, LANES), BF16),
        pltpu.VMEM((plane, packed, LANES), BF16),
        pltpu.VMEM((plane * packed, LANES), F32),
        pltpu.VMEM((rows, width), F32),
        pltpu.VMEM((NX, rows, wide), BF16),
        pltpu.VMEM((NX, rows, wide), BF16),
        pltpu.VMEM((rows, wide), F32),
        pltpu.VMEM((4 * NYL, -(-half // 16) * 16, LANES), BF16),
        pltpu.VMEM((4 * NYL, -(-half // 16) * 16, LANES), BF16),
        pltpu.VMEM((2 * nz * packed, LANES), F32),
        pltpu.VMEM((nz * packed, LANES), F32),
        pltpu.VMEM((nz, packed, LANES), BF16),
        pltpu.VMEM((nz, packed, LANES), BF16),
        dma,
        dma,
        dma,
        dma((2,)),
        dma((2,)),
        dma((images_here,)),
        dma((images_here, NG)),
        dma,
        dma,
        dma,
        dma,
        dma,
        dma,
        dma,
        dma,
        dma,
        dma,
        dma,
        dma,
        dma,
        dma,
        dma,
        dma,
    ]
    return kernel, scratch


def on_device(patches, counts, dest, w_qkv, w_out, text):
    dp_size = lax.axis_size("dp")
    width = w_qkv.shape[2]
    texts_here = text.shape[0]
    kernel, scratch = make_kernel(dp_size, width, texts_here)
    vmem = pl.BlockSpec(memory_space=pltpu.VMEM)
    return pl.pallas_call(
        kernel,
        out_shape=(
            jax.ShapeDtypeStruct((dp_size, HD), F32),
            jax.ShapeDtypeStruct((texts_here, width), F32),
        ),
        in_specs=[pl.BlockSpec(memory_space=pltpu.HBM)] * 6,
        out_specs=(vmem, vmem),
        scratch_shapes=scratch,
        compiler_params=pltpu.CompilerParams(
            collective_id=0, has_side_effects=True, vmem_limit_bytes=58 * 1024 * 1024
        ),
    )(
        counts.reshape(-1, LANES),
        dest.reshape(-1, LANES),
        patches,
        w_qkv.reshape(3 * HD, width),
        w_out,
        text,
    )


def solution(mesh):
    placed = (P("mp", "dp"), P(), P(), P(None, "mp", None), P("mp", None), P(("dp", "mp"), None))
    return jax.shard_map(
        on_device,
        mesh=mesh,
        in_specs=placed,
        out_specs=(P("dp", "mp"), P(("dp", "mp"), None)),
        check_vma=False,
    )
```

```python
import math

import jax
import jax.numpy as jnp
from jax import lax
from jax.experimental import pallas as pl
from jax.experimental.pallas import tpu as pltpu
from jax.sharding import PartitionSpec as P

HD = 72
MAXP = 16
NYL = 4
NYH = 2
NX = 4
NG = NYH * NX
LANES = 128
F32 = jnp.float32
BF16 = jnp.bfloat16
MESH = pl.DeviceIdType.MESH


def iota(shape, dim):
    return lax.broadcasted_iota(jnp.int32, shape, dim)


def dot_nn(a, b):
    return lax.dot_general(a, b, (((1,), (0,)), ((), ())), preferred_element_type=F32)


def dot_nt(a, b):
    return lax.dot_general(a, b, (((1,), (1,)), ((), ())), preferred_element_type=F32)


def wrap(value, size):
    return jnp.where(value >= size, value - size, value)


def make_kernel(dp_size, width, texts_here):
    nz = dp_size // NYL
    half = dp_size // 2
    images_here = half // NG
    pieces = width // LANES
    used = images_here * pieces
    packed = -(-used // 16) * 16
    slots = dp_size * MAXP
    half_slots = half * MAXP
    plane = NYL * NG
    rows = NYL * half
    text_rows = texts_here * 2 * nz
    wide = -(-(4 * HD) // LANES) * LANES

    def kernel(
        counts_in,
        dest_in,
        patches_in,
        w_qkv_in,
        w_out_in,
        text_arg,
        grad_image,
        grad_text,
        counts,
        dest,
        patches,
        w_qkv,
        w_out,
        text,
        in_sem,
        outbox,
        inbox,
        w_qkv_peer,
        w_out_peer,
        feats,
        qkv,
        text_f,
        text_box,
        text_in,
        text_wide,
        text_full,
        text_pad,
        part_f,
        part_b,
        part_in,
        mean_f,
        unit_in,
        unit_wide,
        unit_full,
        gi_box,
        gi_in,
        gi_sum,
        gy_box,
        gy_in,
        gt_f,
        gt_in,
        gt_box,
        gtz_in,
        local_sem,
        a2a_send,
        a2a_recv,
        w_send,
        w_recv,
        g_send,
        g_recv,
        text_send,
        text_recv,
        swap_send,
        swap_recv,
        part_send,
        part_recv,
        unit_send,
        unit_recv,
        gi_send,
        gi_recv,
        gy_send,
        gy_recv,
        gt_send,
        gt_recv,
        gtz_send,
        gtz_recv,
    ):
        me = lax.axis_index("dp")
        mp = lax.axis_index("mp")
        g, c = mp // 2, mp % 2
        z, ylo = me // NYL, me % NYL
        yhi, x = g // NX, g % NX
        y = yhi * NYL + ylo
        other = 1 - c
        partner = (me, g * 2 + other)
        my_half = me // half
        my_slot = me % half
        extra = jnp.where(my_half == c, 0, 1)

        loads = [
            pltpu.make_async_copy(src, dst, in_sem.at[i])
            for i, (src, dst) in enumerate(
                (
                    (dest_in, dest),
                    (counts_in, counts),
                    (patches_in, patches),
                    (w_qkv_in, w_qkv),
                    (w_out_in, w_out),
                    (text_arg, text),
                )
            )
        ]
        for load in loads:
            load.start()

        barrier = pltpu.get_barrier_semaphore()

        def greet(device):
            pl.semaphore_signal(barrier, inc=1, device_id=device, device_id_type=MESH)

        @pl.loop(0, half)
        def _(i):
            src = half * c + i
            greet((src, g * 2 + other))

            @pl.when(src != me)
            def _():
                greet((src, mp))

        greet(partner)

        @pl.loop(1, nz)
        def _(i):
            greet((wrap(z + i, nz) * NYL + ylo, mp))

        place = ylo * NG + g

        @pl.loop(1, 2 * NYL)
        def _(i):
            q = (y + i) % (2 * NYL)
            greet((z * NYL + q % NYL, ((q // NYL) * NX + x) * 2))
            greet((z * NYL + q % NYL, ((q // NYL) * NX + x) * 2 + 1))

        for i in range(1, NX):
            greet((me, (yhi * NX + (x + i) % NX) * 2 + c))
            greet((me, ((1 - yhi) * NX + (x + i) % NX) * 2 + c))

        for buffer in (text_f, text_pad, part_f, mean_f, gt_f, gy_box):
            buffer[...] = jnp.zeros_like(buffer)

        loads[0].wait()
        loads[1].wait()
        first = me * dp_size
        table_rows = dp_size * dp_size // LANES
        span = iota((dp_size, LANES), 1)
        order = iota((dp_size, LANES), 0)
        step = (order // NYL + 1) // 2
        target = wrap(z + nz // 2 + jnp.where(order // NYL % 2 == 1, nz - step, step), nz)
        target = wrap(target, nz) * NYL + (ylo + NYL - 1 - order % NYL) % NYL
        index = jnp.zeros((dp_size, 1), jnp.int32)
        base = first // LANES
        own_rows = []
        for r in range(2):
            row = jnp.minimum(base + r, table_rows - 1)
            image = (base + r) * LANES + span - first
            inside = (image >= 0) & (image < dp_size) & (base + r < table_rows)
            image = jnp.where(inside, image, dp_size)
            own_rows.append((image, counts[pl.ds(row, 1), :]))
            hit = inside & (dest[pl.ds(row, 1), :] == target)
            index = index + jnp.sum(jnp.where(hit, image, 0), axis=1, keepdims=True)
        start = jnp.zeros((dp_size, 1), jnp.int32)
        count = jnp.zeros((dp_size, 1), jnp.int32)
        for image, own in own_rows:
            start = start + jnp.sum(jnp.where(image < index, own, 0), axis=1, keepdims=True)
            count = count + jnp.sum(jnp.where(image == index, own, 0), axis=1, keepdims=True)
        position = iota((dp_size, MAXP, 1), 1)
        column = jnp.where(
            position < count.reshape(dp_size, 1, 1), start.reshape(dp_size, 1, 1) + position, -1
        ).reshape(slots, 1)
        loads[2].wait()

        def image_copy(at, d):
            return pltpu.make_async_remote_copy(
                src_ref=outbox.at[at],
                dst_ref=inbox.at[c * half + my_slot],
                send_sem=a2a_send,
                recv_sem=a2a_recv,
                device_id=(d, g * 2 + my_half),
                device_id_type=MESH,
            )

        total = (2 * half - 1 + extra) + 1 + (nz - 1) + 2 * (2 * NYL - 1) + 2 * (NX - 1)
        blocks = 4
        block_rows = slots // blocks
        block_images = dp_size // blocks
        block_z = nz // blocks
        for n in range(blocks):
            chosen = iota((block_rows, patches.shape[1]), 1) == column[
                n * block_rows : (n + 1) * block_rows
            ]
            picked = dot_nt(chosen.astype(F32).astype(BF16), patches[...]).astype(BF16)
            outbox[n * block_images : (n + 1) * block_images] = picked.reshape(
                block_images, MAXP, HD
            )
            if n == 0:
                pl.semaphore_wait(barrier, total)
            last = n == blocks - 1

            @pl.loop(n * block_z, (n + 1) * block_z - (1 if last else 0))
            def _(j):
                step = (j + 1) // 2
                zz = wrap(z + nz // 2 + jnp.where(j % 2 == 1, nz - step, step), nz)
                zz = wrap(zz, nz)
                for i in range(NYL):
                    d = zz * NYL + (ylo + NYL - 1 - i) % NYL
                    image_copy(j * NYL + i, d).start()

            if last:
                for i in range(NYL - 1):
                    d = z * NYL + (ylo + NYL - 1 - i) % NYL
                    image_copy((nz - 1) * NYL + i, d).start()

        own_copy = pltpu.make_async_copy(
            outbox.at[dp_size - 1], inbox.at[c * half + my_slot], local_sem
        )

        @pl.when(my_half == c)
        def _():
            own_copy.start()

        @pl.when(my_half != c)
        def _():
            image_copy(dp_size - 1, me).start()

        def swap(src, dst, i):
            return pltpu.make_async_remote_copy(
                src_ref=src,
                dst_ref=dst,
                send_sem=w_send.at[i],
                recv_sem=w_recv.at[i],
                device_id=partner,
                device_id_type=MESH,
            )

        swap_qkv = swap(w_qkv, w_qkv_peer, 0)
        swap_out = swap(w_out, w_out_peer, 1)
        loads[3].wait()
        swap_qkv.start()
        loads[4].wait()
        swap_out.start()

        loads[5].wait()
        text_float = text[...].astype(F32)
        text_unit = text_float * lax.rsqrt(
            jnp.sum(text_float * text_float, axis=1, keepdims=True) + 1e-6
        )
        for t in range(texts_here):
            for k in range(pieces):
                text_f[t * pieces + k : t * pieces + k + 1, :] = text_unit[
                    t : t + 1, k * LANES : (k + 1) * LANES
                ]
        own_text = text_f[...].astype(BF16)
        text_box[...] = own_text
        text_in[c * nz + z] = own_text

        def text_copy(zz):
            return pltpu.make_async_remote_copy(
                src_ref=text_box,
                dst_ref=text_in.at[c * nz + z],
                send_sem=text_send,
                recv_sem=text_recv,
                device_id=(zz * NYL + ylo, mp),
                device_id_type=MESH,
            )

        own_texts = text_in.at[pl.ds(c * nz, nz)]
        text_swap = pltpu.make_async_remote_copy(
            src_ref=own_texts,
            dst_ref=own_texts,
            send_sem=swap_send,
            recv_sem=swap_recv,
            device_id=partner,
            device_id_type=MESH,
        )

        got = jnp.zeros((half, LANES), jnp.int32)
        slot_row, slot_lane = iota((half, LANES), 0), iota((half, LANES), 1)
        half_rows = half * dp_size // LANES
        for r in range(half_rows):
            row = pl.ds(half_rows * c + r, 1)
            inside = (r * LANES + slot_lane) // dp_size == slot_row
            got = got + jnp.where(inside & (dest[row, :] == me), counts[row, :], 0)
        got = jnp.sum(got, axis=1, keepdims=True)

        @pl.when(my_half == c)
        def _():
            own_copy.wait()
            pltpu.make_async_remote_copy(
                src_ref=inbox.at[pl.ds(0, 2 * half - 1)],
                dst_ref=inbox.at[pl.ds(0, 2 * half - 1)],
                send_sem=a2a_send,
                recv_sem=a2a_recv,
                device_id=partner,
                device_id_type=MESH,
            ).wait_recv()

        @pl.when(my_half != c)
        def _():
            pltpu.make_async_remote_copy(
                src_ref=inbox,
                dst_ref=inbox,
                send_sem=a2a_send,
                recv_sem=a2a_recv,
                device_id=partner,
                device_id_type=MESH,
            ).wait_recv()

        eye = (iota((HD, HD), 0) == iota((HD, HD), 1)).astype(F32).astype(BF16)

        across = (1 - yhi) * NX + x
        left_x, right_x = lax.rem(x + NX - 1, NX), lax.rem(x + 1, NX)
        far_x = lax.rem(x + 2, NX)

        def feat_copy(k, owner, to):
            return pltpu.make_async_remote_copy(
                src_ref=feats.at[k, owner],
                dst_ref=feats.at[k, owner],
                send_sem=g_send.at[k],
                recv_sem=g_recv.at[k, owner],
                device_id=(me, to * 2 + c),
                device_id_type=MESH,
            )

        own_row, far_row = yhi * NX, (1 - yhi) * NX
        left, right = own_row + left_x, own_row + right_x
        for k in range(images_here):
            low, high = (
                dot_nt(eye, inbox[r + k * NG : r + (k + 1) * NG].reshape(LANES, HD))
                for r in (0, half)
            )
            feats[k, g] = jnp.concatenate([low, high], axis=0).astype(BF16)
            feat_copy(k, g, across).start()
            feat_copy(k, g, left).start()
            feat_copy(k, g, right).start()

        @pl.loop(1, nz)
        def _(i):
            text_copy(wrap(z + i, nz)).start()

        for k in range(images_here):
            feat_copy(k, left, left).wait_recv()
            if k % 2 == 0:
                feat_copy(k, left, right).start()
            feat_copy(k, right, left).wait_recv()
            if k % 2 == 1:
                feat_copy(k, right, left).start()
            feat_copy(k, across, across).wait_recv()
            feat_copy(k, across, own_row + far_x).start()
            feat_copy(k, across, left).start()
            feat_copy(k, across, right).start()

        swap_qkv.wait()
        swap_out.wait()

        for k in range(images_here):
            feat_copy(k, own_row + far_x, left).wait_recv()
            for xx in (left_x, right_x, far_x):
                feat_copy(k, far_row + xx, left).wait_recv()
            full = feats[k].reshape(width, LANES).astype(F32)
            centred = full - jnp.sum(full, axis=0, keepdims=True) / width
            variance = jnp.sum(centred * centred, axis=0, keepdims=True) / width
            normed = (centred * lax.rsqrt(variance + 1e-6)).astype(BF16)
            qkv[k, 0] = dot_nn(w_qkv[...], normed)
            qkv[k, 1] = dot_nn(w_qkv_peer[...], normed)
        pltpu.make_async_remote_copy(
            src_ref=text_in.at[pl.ds(0, nz - 1)],
            dst_ref=text_in.at[pl.ds(0, nz - 1)],
            send_sem=text_send,
            recv_sem=text_recv,
            device_id=partner,
            device_id_type=MESH,
        ).wait()
        text_swap.start()
        row8, lane8 = iota((NG, LANES), 0), iota((NG, LANES), 1)
        same = iota((LANES, LANES), 0) // MAXP == iota((LANES, LANES), 1) // MAXP
        heads = ([], [])
        for k in range(images_here):
            got_k = got[k * NG : (k + 1) * NG]
            got_float = got_k.astype(F32)
            real = (lane8 // MAXP == row8) & (lane8 % MAXP < got_k)
            member = real.astype(F32).astype(BF16)
            key_count = jnp.broadcast_to(got_k.reshape(NG, 1, 1), (NG, MAXP, 1))
            key_count = key_count.reshape(LANES, 1)
            keep = same & (iota((LANES, 1), 0) % MAXP < key_count)
            for h in range(2):
                query = qkv[k, h, 0:HD].astype(BF16)
                key = jnp.transpose(qkv[k, h, HD : 2 * HD]).astype(BF16)
                value = qkv[k, h, 2 * HD : 3 * HD].astype(BF16)
                scores = dot_nn(key, query) / math.sqrt(HD)
                scores = jnp.where(keep, scores, -1e30)
                raised = jnp.exp(scores - jnp.max(scores, axis=0, keepdims=True))
                weights = (raised / jnp.sum(raised, axis=0, keepdims=True)).astype(BF16)
                mixed = dot_nn(value, weights).astype(BF16)
                heads[h].append(dot_nt(member, mixed) / got_float)
        term = jnp.zeros((half, width), F32)
        for pooled, wo in zip(heads, (w_out, w_out_peer)):
            term = term + dot_nn(jnp.concatenate(pooled, axis=0).astype(BF16), wo[...])
        for k in range(images_here):
            for p in range(pieces):
                part_f[pl.ds(k * pieces + p, NG, stride=packed), :] = term[
                    k * NG : (k + 1) * NG, p * LANES : (p + 1) * LANES
                ]

        part_b[...] = part_f[...].astype(BF16).reshape(NG, packed, LANES)

        def part_copy(gg):
            return pltpu.make_async_remote_copy(
                src_ref=part_b.at[gg],
                dst_ref=part_in.at[g],
                send_sem=part_send,
                recv_sem=part_recv,
                device_id=(me, gg * 2 + c),
                device_id_type=MESH,
            )

        @pl.loop(1, NG)
        def _(i):
            part_copy((g + i) % NG).start()

        part_in[g] = part_b[g]

        here = (lane8 // MAXP == g).astype(F32).astype(BF16)
        for k in range(images_here):
            own_got = jnp.sum(
                jnp.where(iota((NG, 1), 0) == g, got[k * NG : (k + 1) * NG], 0),
                axis=0,
                keepdims=True,
            ).astype(F32)
            mean = dot_nt(here, feats[k].reshape(width, LANES)) / own_got
            for p in range(pieces):
                r = k * pieces + p
                mean_f[r : r + 1, :] = mean[0:1, p * LANES : (p + 1) * LANES]

        text_swap.wait()
        text_wide[...] = text_in[...].astype(F32).reshape(2 * nz * packed, LANES)
        for t in range(texts_here):
            for p in range(pieces):
                text_full[t * 2 * nz : (t + 1) * 2 * nz, p * LANES : (p + 1) * LANES] = (
                    text_wide[pl.ds(t * pieces + p, 2 * nz, stride=packed), :]
                )
        for xx in range(NX):
            for q in range(4):
                m = ((q // 2) * NX + xx) * 2 + q % 2
                text_pad[:, xx * wide + q * HD : xx * wide + (q + 1) * HD] = text_full[
                    :, m * HD : (m + 1) * HD
                ]
        text_rows_b = text_full[...].astype(BF16)
        text_cols_b = text_pad[...].astype(BF16)

        part_seven = pltpu.make_async_remote_copy(
            src_ref=part_in.at[pl.ds(0, NG - 1)],
            dst_ref=part_in.at[pl.ds(0, NG - 1)],
            send_sem=part_send,
            recv_sem=part_recv,
            device_id=partner,
            device_id_type=MESH,
        )
        part_seven.wait()
        pooled = jnp.sum(part_in[...].astype(F32), axis=0) + mean_f[...]
        squares = jnp.sum(pooled * pooled, axis=1, keepdims=True)
        row_id = iota((packed, 1), 0)
        scale = jnp.zeros((packed, 1), F32)
        for k in range(images_here):
            inside = (row_id >= k * pieces) & (row_id < (k + 1) * pieces)
            norm = jnp.sum(jnp.where(inside, squares, 0.0), axis=0, keepdims=True)
            scale = jnp.where(inside, lax.rsqrt(norm + 1e-6), scale)
        own_unit = (pooled * scale).astype(BF16)
        unit_in[place] = own_unit

        def unit_y(step, at):
            q = (y + step) % (2 * NYL)
            return pltpu.make_async_remote_copy(
                src_ref=unit_in.at[at],
                dst_ref=unit_in.at[at],
                send_sem=unit_send,
                recv_sem=unit_recv.at[step],
                device_id=(z * NYL + q % NYL, ((q // NYL) * NX + x) * 2 + c),
                device_id_type=MESH,
            )

        def unit_x(at):
            for i in (2, 1, 3):
                pltpu.make_async_remote_copy(
                    src_ref=unit_in.at[at],
                    dst_ref=unit_in.at[at],
                    send_sem=unit_send,
                    recv_sem=unit_recv.at[0],
                    device_id=(me, (yhi * NX + (x + i) % NX) * 2 + c),
                    device_id_type=MESH,
                ).start()

        for step in (4, 3, 5, 2, 6, 1, 7):
            unit_y(step, place).start()
        unit_x(place)

        text_row = iota((text_rows, 1), 0)
        text_source = (text_row % nz) * NYL + ylo
        text_core = (text_row % (2 * nz)) // nz
        pair_at = text_source * dp_size + (g * 2 + text_core) * texts_here + text_row // (2 * nz)
        pair_lane = iota((text_rows, LANES), 1)
        pair_dest = jnp.zeros((text_rows, LANES), jnp.int32)
        for r in range(table_rows):
            pair_dest = pair_dest + jnp.where(
                pair_at == r * LANES + pair_lane, dest[r : r + 1, :], 0
            )
        pair_dest = jnp.sum(pair_dest, axis=1, keepdims=True)
        image_lane = iota((text_rows, rows), 1)
        image_source = c * half + image_lane % half
        image_dest = z * NYL + image_lane // half
        paired = (image_source == text_source) & (image_dest == pair_dest)
        labels = jnp.where(paired, 1.0, -1.0)

        for step in (1, 7, 2, 6, 3, 5, 4):
            q = (y + 2 * NYL - step) % (2 * NYL)
            at = (q % NYL) * NG + (q // NYL) * NX + x
            unit_y(step, at).wait_recv()
            unit_x(at)
        pltpu.make_async_remote_copy(
            src_ref=unit_in.at[pl.ds(0, plane - 2 * NYL)],
            dst_ref=unit_in.at[pl.ds(0, plane - 2 * NYL)],
            send_sem=unit_send,
            recv_sem=unit_recv.at[0],
            device_id=partner,
            device_id_type=MESH,
        ).wait_recv()
        unit_wide[...] = unit_in[...].astype(F32).reshape(plane * packed, LANES)
        for yy in range(NYL):
            for k in range(images_here):
                for p in range(pieces):
                    unit_full[
                        yy * half + k * NG : yy * half + (k + 1) * NG,
                        p * LANES : (p + 1) * LANES,
                    ] = unit_wide[
                        pl.ds(yy * NG * packed + k * pieces + p, NG, stride=packed), :
                    ]
        units = unit_full[...].astype(BF16)

        logits = 4.0 * dot_nt(text_rows_b, units) - 2.0
        dscaled = -4.0 * labels / (1.0 + jnp.exp(labels * logits))
        turned = jnp.transpose(dscaled).astype(BF16)
        dscaled = dscaled.astype(BF16)

        def gi_copy(n, xx):
            return pltpu.make_async_remote_copy(
                src_ref=gi_box.at[n, xx],
                dst_ref=gi_in.at[n, x],
                send_sem=gi_send.at[n],
                recv_sem=gi_recv.at[n],
                device_id=(me, (yhi * NX + xx) * 2 + c),
                device_id_type=MESH,
            )

        pair_rows = 2 * half
        for n in range(2):
            for xx in range(NX):
                gi_box[n, xx] = dot_nn(
                    turned[n * pair_rows : (n + 1) * pair_rows],
                    text_cols_b[:, xx * wide : (xx + 1) * wide],
                ).astype(BF16)
            for i in (2, 1, 3):
                gi_copy(n, (x + i) % NX).start()
            gi_in[n, x] = gi_box[n, x]

        text_grad = dot_nn(dscaled, units)
        for t in range(texts_here):
            for p in range(pieces):
                gt_f[pl.ds(t * pieces + p, 2 * nz, stride=packed), :] = text_grad[
                    t * 2 * nz : (t + 1) * 2 * nz, p * LANES : (p + 1) * LANES
                ]
        core_rows = nz * packed
        gt_copy = pltpu.make_async_remote_copy(
            src_ref=gt_f.at[pl.ds(pl.multiple_of(other * core_rows, 8), core_rows)],
            dst_ref=gt_in,
            send_sem=gt_send,
            recv_sem=gt_recv,
            device_id=partner,
            device_id_type=MESH,
        )
        gt_copy.start()

        gt_copy.wait()
        own_sums = gt_f[pl.ds(pl.multiple_of(c * core_rows, 8), core_rows), :]
        gt_box[...] = (own_sums + gt_in[...]).astype(BF16).reshape(nz, packed, LANES)

        def gtz_copy(zz):
            return pltpu.make_async_remote_copy(
                src_ref=gt_box.at[zz],
                dst_ref=gtz_in.at[z],
                send_sem=gtz_send,
                recv_sem=gtz_recv,
                device_id=(zz * NYL + ylo, mp),
                device_id_type=MESH,
            )

        @pl.loop(1, nz)
        def _(i):
            gtz_copy(wrap(z + i, nz)).start()

        gtz_in[z] = gt_box[z]

        def gy_copy(yy, core):
            return pltpu.make_async_remote_copy(
                src_ref=gy_box.at[yy * 2 + core],
                dst_ref=gy_in.at[c * 2 * NYL + y],
                send_sem=gy_send,
                recv_sem=gy_recv,
                device_id=(z * NYL + yy % NYL, ((yy // NYL) * NX + x) * 2 + core),
                device_id_type=MESH,
            )

        for n in range(2):
            pltpu.make_async_remote_copy(
                src_ref=gi_in.at[n, pl.ds(0, NX - 1)],
                dst_ref=gi_in.at[n, pl.ds(0, NX - 1)],
                send_sem=gi_send.at[n],
                recv_sem=gi_recv.at[n],
                device_id=partner,
                device_id_type=MESH,
            ).wait()
            gi_sum[...] = jnp.sum(gi_in[n].astype(F32), axis=0)
            turn = [(row * NYL + 2 * n + r, core) for row in (0, 1) for r in (0, 1) for core in (0, 1)]
            for yy, core in turn:
                q = (yy // NYL) * 2 + core
                r = (yy % 2) * half
                gy_box[yy * 2 + core, :, 0:HD] = gi_sum[
                    r : r + half, q * HD : (q + 1) * HD
                ].astype(BF16)
            for yy, core in turn:

                @pl.when((yy != y) | (core != c))
                def _():
                    gy_copy(yy, core).start()

        gy_in[c * 2 * NYL + y] = gy_box[y * 2 + c]

        pltpu.make_async_remote_copy(
            src_ref=gtz_in.at[pl.ds(0, nz - 1)],
            dst_ref=gtz_in.at[pl.ds(0, nz - 1)],
            send_sem=gtz_send,
            recv_sem=gtz_recv,
            device_id=partner,
            device_id_type=MESH,
        ).wait()
        summed = jnp.sum(gtz_in[...].astype(F32), axis=0)
        for t in range(texts_here):
            for p in range(pieces):
                r = t * pieces + p
                grad_text[t : t + 1, p * LANES : (p + 1) * LANES] = summed[r : r + 1, :]

        pltpu.make_async_remote_copy(
            src_ref=gy_in.at[pl.ds(0, 4 * NYL - 1)],
            dst_ref=gy_in.at[pl.ds(0, 4 * NYL - 1)],
            send_sem=gy_send,
            recv_sem=gy_recv,
            device_id=partner,
            device_id_type=MESH,
        ).wait()
        for core in range(2):
            part = gy_in[core * 2 * NYL : (core + 1) * 2 * NYL].astype(F32)
            grad_image[core * half : (core + 1) * half, :] = jnp.sum(part, axis=0)[:, 0:HD]

        pltpu.make_async_remote_copy(
            src_ref=unit_in.at[pl.ds(0, plane - 1)],
            dst_ref=unit_in.at[pl.ds(0, plane - 1)],
            send_sem=unit_send,
            recv_sem=unit_recv.at[0],
            device_id=partner,
            device_id_type=MESH,
        ).wait_send()

        @pl.when(my_half == c)
        def _():
            pltpu.make_async_remote_copy(
                src_ref=outbox.at[pl.ds(0, dp_size - 1)],
                dst_ref=outbox.at[pl.ds(0, dp_size - 1)],
                send_sem=a2a_send,
                recv_sem=a2a_recv,
                device_id=partner,
                device_id_type=MESH,
            ).wait_send()

        @pl.when(my_half != c)
        def _():
            pltpu.make_async_remote_copy(
                src_ref=outbox,
                dst_ref=outbox,
                send_sem=a2a_send,
                recv_sem=a2a_recv,
                device_id=partner,
                device_id_type=MESH,
            ).wait_send()

        for k in range(images_here):
            pltpu.make_async_remote_copy(
                src_ref=feats.at[k, pl.ds(0, NG - 1)],
                dst_ref=feats.at[k, pl.ds(0, NG - 1)],
                send_sem=g_send.at[k],
                recv_sem=g_recv.at[k, 0],
                device_id=partner,
                device_id_type=MESH,
            ).wait_send()

    dma = pltpu.SemaphoreType.DMA
    scratch = [
        pltpu.VMEM((dp_size * dp_size // LANES, LANES), jnp.int32),
        pltpu.VMEM((dp_size * dp_size // LANES, LANES), jnp.int32),
        pltpu.VMEM((HD, dp_size * MAXP), BF16),
        pltpu.VMEM((3 * HD, width), BF16),
        pltpu.VMEM((HD, width), BF16),
        pltpu.VMEM((texts_here, width), BF16),
        dma((6,)),
        pltpu.VMEM((dp_size, MAXP, HD), BF16),
        pltpu.VMEM((2 * half, MAXP, HD), BF16),
        pltpu.VMEM((3 * HD, width), BF16),
        pltpu.VMEM((HD, width), BF16),
        pltpu.VMEM((images_here, NG, 2 * HD, LANES), BF16),
        pltpu.VMEM((images_here, 2, 3 * HD, LANES), F32),
        pltpu.VMEM((packed, LANES), F32),
        pltpu.VMEM((packed, LANES), BF16),
        pltpu.VMEM((2 * nz, packed, LANES), BF16),
        pltpu.VMEM((2 * nz * packed, LANES), F32),
        pltpu.VMEM((text_rows, width), F32),
        pltpu.VMEM((text_rows, NX * wide), F32),
        pltpu.VMEM((NG * packed, LANES), F32),
        pltpu.VMEM((NG, packed, LANES), BF16),
        pltpu.VMEM((NG, packed, LANES), BF16),
        pltpu.VMEM((packed, LANES), F32),
        pltpu.VMEM((plane, packed, LANES), BF16),
        pltpu.VMEM((plane * packed, LANES), F32),
        pltpu.VMEM((rows, width), F32),
        pltpu.VMEM((2, NX, rows // 2, wide), BF16),
        pltpu.VMEM((2, NX, rows // 2, wide), BF16),
        pltpu.VMEM((rows // 2, wide), F32),
        pltpu.VMEM((4 * NYL, half, LANES), BF16),
        pltpu.VMEM((4 * NYL, half, LANES), BF16),
        pltpu.VMEM((2 * nz * packed, LANES), F32),
        pltpu.VMEM((nz * packed, LANES), F32),
        pltpu.VMEM((nz, packed, LANES), BF16),
        pltpu.VMEM((nz, packed, LANES), BF16),
        dma,
        dma,
        dma,
        dma((2,)),
        dma((2,)),
        dma((images_here,)),
        dma((images_here, NG)),
        dma,
        dma,
        dma,
        dma,
        dma,
        dma,
        dma,
        dma((2 * NYL,)),
        dma((2,)),
        dma((2,)),
        dma,
        dma,
        dma,
        dma,
        dma,
        dma,
    ]
    return kernel, scratch


def on_device(patches, counts, dest, w_qkv, w_out, text):
    dp_size = lax.axis_size("dp")
    width = w_qkv.shape[2]
    texts_here = text.shape[0]
    kernel, scratch = make_kernel(dp_size, width, texts_here)
    vmem = pl.BlockSpec(memory_space=pltpu.VMEM)
    return pl.pallas_call(
        kernel,
        out_shape=(
            jax.ShapeDtypeStruct((dp_size, HD), F32),
            jax.ShapeDtypeStruct((texts_here, width), F32),
        ),
        in_specs=[pl.BlockSpec(memory_space=pltpu.HBM)] * 6,
        out_specs=(vmem, vmem),
        scratch_shapes=scratch,
        compiler_params=pltpu.CompilerParams(
            collective_id=0, has_side_effects=True, vmem_limit_bytes=58 * 1024 * 1024
        ),
    )(
        counts.reshape(-1, LANES),
        dest.reshape(-1, LANES),
        patches,
        w_qkv.reshape(3 * HD, width),
        w_out,
        text,
    )


def solution(mesh):
    placed = (P("mp", "dp"), P(), P(), P(None, "mp", None), P("mp", None), P(("dp", "mp"), None))
    return jax.shard_map(
        on_device,
        mesh=mesh,
        in_specs=placed,
        out_specs=(P("dp", "mp"), P(("dp", "mp"), None)),
        check_vma=False,
    )
```

```python
import math

import jax
import jax.numpy as jnp
from jax import lax
from jax.experimental import pallas as pl
from jax.experimental.pallas import tpu as pltpu
from jax.sharding import PartitionSpec as P

HD = 72
MAXP = 16
NYL = 4
NYH = 2
NX = 4
NG = NYH * NX
LANES = 128
F32 = jnp.float32
BF16 = jnp.bfloat16
MESH = pl.DeviceIdType.MESH


def iota(shape, dim):
    return lax.broadcasted_iota(jnp.int32, shape, dim)


def dot_nn(a, b):
    return lax.dot_general(a, b, (((1,), (0,)), ((), ())), preferred_element_type=F32)


def dot_nt(a, b):
    return lax.dot_general(a, b, (((1,), (1,)), ((), ())), preferred_element_type=F32)


def wrap(value, size):
    return jnp.where(value >= size, value - size, value)


def make_kernel(dp_size, width, texts_here):
    nz = dp_size // NYL
    half = dp_size // 2
    images_here = half // NG
    pieces = width // LANES
    used = images_here * pieces
    packed = -(-used // 16) * 16
    slots = dp_size * MAXP
    half_slots = half * MAXP
    plane = NYL * NG
    rows = NYL * half
    text_rows = texts_here * 2 * nz
    wide = -(-(4 * HD) // LANES) * LANES

    def kernel(
        counts_in,
        dest_in,
        patches_in,
        w_qkv_in,
        w_out_in,
        text_arg,
        grad_image,
        grad_text,
        counts,
        dest,
        patches,
        w_qkv,
        w_out,
        text,
        in_sem,
        outbox,
        inbox,
        w_qkv_peer,
        w_out_peer,
        feats,
        text_f,
        text_box,
        text_in,
        text_wide,
        text_full,
        text_pad,
        part_f,
        part_b,
        part_in,
        mean_f,
        unit_in,
        unit_wide,
        unit_full,
        gi_box,
        gi_in,
        gi_sum,
        gy_box,
        gy_in,
        gt_f,
        gt_in,
        gt_box,
        gtz_in,
        local_sem,
        a2a_send,
        a2a_recv,
        w_send,
        w_recv,
        g_send,
        g_recv,
        text_send,
        text_recv,
        swap_send,
        swap_recv,
        part_send,
        part_recv,
        unit_send,
        unit_recv,
        gi_send,
        gi_recv,
        gy_send,
        gy_recv,
        gt_send,
        gt_recv,
        gtz_send,
        gtz_recv,
    ):
        me = lax.axis_index("dp")
        mp = lax.axis_index("mp")
        g, c = mp // 2, mp % 2
        z, ylo = me // NYL, me % NYL
        yhi, x = g // NX, g % NX
        y = yhi * NYL + ylo
        other = 1 - c
        partner = (me, g * 2 + other)
        my_half = me // half
        my_slot = me % half
        extra = jnp.where(my_half == c, 0, 1)

        loads = [
            pltpu.make_async_copy(src, dst, in_sem.at[i])
            for i, (src, dst) in enumerate(
                (
                    (dest_in, dest),
                    (counts_in, counts),
                    (patches_in, patches),
                    (w_qkv_in, w_qkv),
                    (w_out_in, w_out),
                    (text_arg, text),
                )
            )
        ]
        for load in loads:
            load.start()

        barrier = pltpu.get_barrier_semaphore()

        def greet(device):
            pl.semaphore_signal(barrier, inc=1, device_id=device, device_id_type=MESH)

        @pl.loop(0, half)
        def _(i):
            src = half * c + i
            greet((src, g * 2 + other))

            @pl.when(src != me)
            def _():
                greet((src, mp))

        greet(partner)

        @pl.loop(1, nz)
        def _(i):
            greet((wrap(z + i, nz) * NYL + ylo, mp))

        place = ylo * NG + g

        @pl.loop(1, 2 * NYL)
        def _(i):
            q = (y + i) % (2 * NYL)
            greet((z * NYL + q % NYL, ((q // NYL) * NX + x) * 2))
            greet((z * NYL + q % NYL, ((q // NYL) * NX + x) * 2 + 1))

        for i in range(1, NX):
            greet((me, (yhi * NX + (x + i) % NX) * 2 + c))
            greet((me, ((1 - yhi) * NX + (x + i) % NX) * 2 + c))

        for buffer in (text_f, text_pad, part_f, mean_f, gt_f, gy_box):
            buffer[...] = jnp.zeros_like(buffer)

        loads[0].wait()
        loads[1].wait()
        first = me * dp_size
        table_rows = dp_size * dp_size // LANES
        span = iota((dp_size, LANES), 1)
        order = iota((dp_size, LANES), 0)
        step = (order // NYL + 1) // 2
        target = wrap(z + nz // 2 + jnp.where(order // NYL % 2 == 1, nz - step, step), nz)
        target = wrap(target, nz) * NYL + (ylo + NYL - 1 - order % NYL) % NYL
        index = jnp.zeros((dp_size, 1), jnp.int32)
        base = first // LANES
        own_rows = []
        for r in range(2):
            row = jnp.minimum(base + r, table_rows - 1)
            image = (base + r) * LANES + span - first
            inside = (image >= 0) & (image < dp_size) & (base + r < table_rows)
            image = jnp.where(inside, image, dp_size)
            own_rows.append((image, counts[pl.ds(row, 1), :]))
            hit = inside & (dest[pl.ds(row, 1), :] == target)
            index = index + jnp.sum(jnp.where(hit, image, 0), axis=1, keepdims=True)
        start = jnp.zeros((dp_size, 1), jnp.int32)
        count = jnp.zeros((dp_size, 1), jnp.int32)
        for image, own in own_rows:
            start = start + jnp.sum(jnp.where(image < index, own, 0), axis=1, keepdims=True)
            count = count + jnp.sum(jnp.where(image == index, own, 0), axis=1, keepdims=True)
        position = iota((dp_size, MAXP, 1), 1)
        column = jnp.where(
            position < count.reshape(dp_size, 1, 1), start.reshape(dp_size, 1, 1) + position, -1
        ).reshape(slots, 1)
        loads[2].wait()

        def image_copy(at, d):
            return pltpu.make_async_remote_copy(
                src_ref=outbox.at[at],
                dst_ref=inbox.at[c * half + my_slot],
                send_sem=a2a_send,
                recv_sem=a2a_recv,
                device_id=(d, g * 2 + my_half),
                device_id_type=MESH,
            )

        total = (2 * half - 1 + extra) + 1 + (nz - 1) + 2 * (2 * NYL - 1) + 2 * (NX - 1)
        blocks = 4
        block_rows = slots // blocks
        block_images = dp_size // blocks
        block_z = nz // blocks
        for n in range(blocks):
            chosen = iota((block_rows, patches.shape[1]), 1) == column[
                n * block_rows : (n + 1) * block_rows
            ]
            picked = dot_nt(chosen.astype(F32).astype(BF16), patches[...]).astype(BF16)
            outbox[n * block_images : (n + 1) * block_images] = picked.reshape(
                block_images, MAXP, HD
            )
            if n == 0:
                pl.semaphore_wait(barrier, total)
            last = n == blocks - 1

            @pl.loop(n * block_z, (n + 1) * block_z - (1 if last else 0))
            def _(j):
                step = (j + 1) // 2
                zz = wrap(z + nz // 2 + jnp.where(j % 2 == 1, nz - step, step), nz)
                zz = wrap(zz, nz)
                for i in range(NYL):
                    d = zz * NYL + (ylo + NYL - 1 - i) % NYL
                    image_copy(j * NYL + i, d).start()

            if last:
                for i in range(NYL - 1):
                    d = z * NYL + (ylo + NYL - 1 - i) % NYL
                    image_copy((nz - 1) * NYL + i, d).start()

        own_copy = pltpu.make_async_copy(
            outbox.at[dp_size - 1], inbox.at[c * half + my_slot], local_sem
        )

        @pl.when(my_half == c)
        def _():
            own_copy.start()

        @pl.when(my_half != c)
        def _():
            image_copy(dp_size - 1, me).start()

        def swap(src, dst, i):
            return pltpu.make_async_remote_copy(
                src_ref=src,
                dst_ref=dst,
                send_sem=w_send.at[i],
                recv_sem=w_recv.at[i],
                device_id=partner,
                device_id_type=MESH,
            )

        swap_qkv = swap(w_qkv, w_qkv_peer, 0)
        swap_out = swap(w_out, w_out_peer, 1)
        loads[3].wait()
        swap_qkv.start()
        loads[4].wait()
        swap_out.start()

        loads[5].wait()
        text_float = text[...].astype(F32)
        text_unit = text_float * lax.rsqrt(
            jnp.sum(text_float * text_float, axis=1, keepdims=True) + 1e-6
        )
        for t in range(texts_here):
            for k in range(pieces):
                text_f[t * pieces + k : t * pieces + k + 1, :] = text_unit[
                    t : t + 1, k * LANES : (k + 1) * LANES
                ]
        own_text = text_f[...].astype(BF16)
        text_box[...] = own_text
        text_in[c * nz + z] = own_text

        def text_copy(zz):
            return pltpu.make_async_remote_copy(
                src_ref=text_box,
                dst_ref=text_in.at[c * nz + z],
                send_sem=text_send,
                recv_sem=text_recv,
                device_id=(zz * NYL + ylo, mp),
                device_id_type=MESH,
            )

        own_texts = text_in.at[pl.ds(c * nz, nz)]
        text_swap = pltpu.make_async_remote_copy(
            src_ref=own_texts,
            dst_ref=own_texts,
            send_sem=swap_send,
            recv_sem=swap_recv,
            device_id=partner,
            device_id_type=MESH,
        )

        got = jnp.zeros((half, LANES), jnp.int32)
        slot_row, slot_lane = iota((half, LANES), 0), iota((half, LANES), 1)
        half_rows = half * dp_size // LANES
        for r in range(half_rows):
            row = pl.ds(half_rows * c + r, 1)
            inside = (r * LANES + slot_lane) // dp_size == slot_row
            got = got + jnp.where(inside & (dest[row, :] == me), counts[row, :], 0)
        got = jnp.sum(got, axis=1, keepdims=True)

        @pl.when(my_half == c)
        def _():
            own_copy.wait()
            pltpu.make_async_remote_copy(
                src_ref=inbox.at[pl.ds(0, 2 * half - 1)],
                dst_ref=inbox.at[pl.ds(0, 2 * half - 1)],
                send_sem=a2a_send,
                recv_sem=a2a_recv,
                device_id=partner,
                device_id_type=MESH,
            ).wait_recv()

        @pl.when(my_half != c)
        def _():
            pltpu.make_async_remote_copy(
                src_ref=inbox,
                dst_ref=inbox,
                send_sem=a2a_send,
                recv_sem=a2a_recv,
                device_id=partner,
                device_id_type=MESH,
            ).wait_recv()

        eye = (iota((HD, HD), 0) == iota((HD, HD), 1)).astype(F32).astype(BF16)

        across = (1 - yhi) * NX + x
        left_x, right_x = lax.rem(x + NX - 1, NX), lax.rem(x + 1, NX)
        far_x = lax.rem(x + 2, NX)

        def feat_copy(k, owner, to):
            return pltpu.make_async_remote_copy(
                src_ref=feats.at[k, owner],
                dst_ref=feats.at[k, owner],
                send_sem=g_send.at[k],
                recv_sem=g_recv.at[k, owner],
                device_id=(me, to * 2 + c),
                device_id_type=MESH,
            )

        own_row, far_row = yhi * NX, (1 - yhi) * NX
        left, right = own_row + left_x, own_row + right_x
        for k in range(images_here):
            low, high = (
                dot_nt(eye, inbox[r + k * NG : r + (k + 1) * NG].reshape(LANES, HD))
                for r in (0, half)
            )
            feats[k, g] = jnp.concatenate([low, high], axis=0).astype(BF16)
            feat_copy(k, g, across).start()
            feat_copy(k, g, left).start()
            feat_copy(k, g, right).start()

        @pl.loop(1, nz)
        def _(i):
            text_copy(wrap(z + i, nz)).start()

        for k in range(images_here):
            feat_copy(k, left, left).wait_recv()
            if k % 2 == 0:
                feat_copy(k, left, right).start()
            feat_copy(k, right, left).wait_recv()
            if k % 2 == 1:
                feat_copy(k, right, left).start()
            feat_copy(k, across, across).wait_recv()
            feat_copy(k, across, own_row + far_x).start()
            feat_copy(k, across, left).start()
            feat_copy(k, across, right).start()

        swap_qkv.wait()
        swap_out.wait()

        row8, lane8 = iota((NG, LANES), 0), iota((NG, LANES), 1)
        same = iota((LANES, LANES), 0) // MAXP == iota((LANES, LANES), 1) // MAXP
        heads = ([], [])
        for k in range(images_here):
            feat_copy(k, own_row + far_x, left).wait_recv()
            for xx in (left_x, right_x, far_x):
                feat_copy(k, far_row + xx, left).wait_recv()
            full = feats[k].reshape(width, LANES).astype(F32)
            centred = full - jnp.sum(full, axis=0, keepdims=True) / width
            variance = jnp.sum(centred * centred, axis=0, keepdims=True) / width
            normed = (centred * lax.rsqrt(variance + 1e-6)).astype(BF16)
            got_k = got[k * NG : (k + 1) * NG]
            got_float = got_k.astype(F32)
            real = (lane8 // MAXP == row8) & (lane8 % MAXP < got_k)
            member = real.astype(F32).astype(BF16)
            key_count = jnp.broadcast_to(got_k.reshape(NG, 1, 1), (NG, MAXP, 1))
            key_count = key_count.reshape(LANES, 1)
            keep = same & (iota((LANES, 1), 0) % MAXP < key_count)
            for h, wq in enumerate((w_qkv, w_qkv_peer)):
                projected = dot_nn(wq[...], normed)
                query = projected[0:HD].astype(BF16)
                key = jnp.transpose(projected[HD : 2 * HD]).astype(BF16)
                value = projected[2 * HD : 3 * HD].astype(BF16)
                scores = dot_nn(key, query) / math.sqrt(HD)
                scores = jnp.where(keep, scores, -1e30)
                raised = jnp.exp(scores - jnp.max(scores, axis=0, keepdims=True))
                weights = (raised / jnp.sum(raised, axis=0, keepdims=True)).astype(BF16)
                mixed = dot_nn(value, weights).astype(BF16)
                heads[h].append(dot_nt(member, mixed) / got_float)
        pltpu.make_async_remote_copy(
            src_ref=text_in.at[pl.ds(0, nz - 1)],
            dst_ref=text_in.at[pl.ds(0, nz - 1)],
            send_sem=text_send,
            recv_sem=text_recv,
            device_id=partner,
            device_id_type=MESH,
        ).wait()
        text_swap.start()
        term = jnp.zeros((half, width), F32)
        for pooled, wo in zip(heads, (w_out, w_out_peer)):
            term = term + dot_nn(jnp.concatenate(pooled, axis=0).astype(BF16), wo[...])
        for k in range(images_here):
            for p in range(pieces):
                part_f[pl.ds(k * pieces + p, NG, stride=packed), :] = term[
                    k * NG : (k + 1) * NG, p * LANES : (p + 1) * LANES
                ]

        part_b[...] = part_f[...].astype(BF16).reshape(NG, packed, LANES)

        def part_copy(gg):
            return pltpu.make_async_remote_copy(
                src_ref=part_b.at[gg],
                dst_ref=part_in.at[g],
                send_sem=part_send,
                recv_sem=part_recv,
                device_id=(me, gg * 2 + c),
                device_id_type=MESH,
            )

        @pl.loop(1, NG)
        def _(i):
            part_copy((g + i) % NG).start()

        part_in[g] = part_b[g]

        here = (lane8 // MAXP == g).astype(F32).astype(BF16)
        for k in range(images_here):
            own_got = jnp.sum(
                jnp.where(iota((NG, 1), 0) == g, got[k * NG : (k + 1) * NG], 0),
                axis=0,
                keepdims=True,
            ).astype(F32)
            mean = dot_nt(here, feats[k].reshape(width, LANES)) / own_got
            for p in range(pieces):
                r = k * pieces + p
                mean_f[r : r + 1, :] = mean[0:1, p * LANES : (p + 1) * LANES]

        text_swap.wait()
        text_wide[...] = text_in[...].astype(F32).reshape(2 * nz * packed, LANES)
        for t in range(texts_here):
            for p in range(pieces):
                text_full[t * 2 * nz : (t + 1) * 2 * nz, p * LANES : (p + 1) * LANES] = (
                    text_wide[pl.ds(t * pieces + p, 2 * nz, stride=packed), :]
                )
        for xx in range(NX):
            for q in range(4):
                m = ((q // 2) * NX + xx) * 2 + q % 2
                text_pad[:, xx * wide + q * HD : xx * wide + (q + 1) * HD] = text_full[
                    :, m * HD : (m + 1) * HD
                ]
        text_rows_b = text_full[...].astype(BF16)
        text_cols_b = text_pad[...].astype(BF16)

        part_seven = pltpu.make_async_remote_copy(
            src_ref=part_in.at[pl.ds(0, NG - 1)],
            dst_ref=part_in.at[pl.ds(0, NG - 1)],
            send_sem=part_send,
            recv_sem=part_recv,
            device_id=partner,
            device_id_type=MESH,
        )
        part_seven.wait()
        pooled = jnp.sum(part_in[...].astype(F32), axis=0) + mean_f[...]
        squares = jnp.sum(pooled * pooled, axis=1, keepdims=True)
        row_id = iota((packed, 1), 0)
        scale = jnp.zeros((packed, 1), F32)
        for k in range(images_here):
            inside = (row_id >= k * pieces) & (row_id < (k + 1) * pieces)
            norm = jnp.sum(jnp.where(inside, squares, 0.0), axis=0, keepdims=True)
            scale = jnp.where(inside, lax.rsqrt(norm + 1e-6), scale)
        own_unit = (pooled * scale).astype(BF16)
        unit_in[place] = own_unit

        def unit_y(step, at):
            q = (y + step) % (2 * NYL)
            return pltpu.make_async_remote_copy(
                src_ref=unit_in.at[at],
                dst_ref=unit_in.at[at],
                send_sem=unit_send,
                recv_sem=unit_recv.at[step],
                device_id=(z * NYL + q % NYL, ((q // NYL) * NX + x) * 2 + c),
                device_id_type=MESH,
            )

        def unit_x(at):
            for i in (2, 1, 3):
                pltpu.make_async_remote_copy(
                    src_ref=unit_in.at[at],
                    dst_ref=unit_in.at[at],
                    send_sem=unit_send,
                    recv_sem=unit_recv.at[0],
                    device_id=(me, (yhi * NX + (x + i) % NX) * 2 + c),
                    device_id_type=MESH,
                ).start()

        for step in (4, 3, 5, 2, 6, 1, 7):
            unit_y(step, place).start()
        unit_x(place)

        text_row = iota((text_rows, 1), 0)
        text_source = (text_row % nz) * NYL + ylo
        text_core = (text_row % (2 * nz)) // nz
        pair_at = text_source * dp_size + (g * 2 + text_core) * texts_here + text_row // (2 * nz)
        pair_lane = iota((text_rows, LANES), 1)
        pair_dest = jnp.zeros((text_rows, LANES), jnp.int32)
        for r in range(table_rows):
            pair_dest = pair_dest + jnp.where(
                pair_at == r * LANES + pair_lane, dest[r : r + 1, :], 0
            )
        pair_dest = jnp.sum(pair_dest, axis=1, keepdims=True)
        image_lane = iota((text_rows, rows), 1)
        image_source = c * half + image_lane % half
        image_dest = z * NYL + image_lane // half
        paired = (image_source == text_source) & (image_dest == pair_dest)
        labels = jnp.where(paired, 1.0, -1.0)

        for step in (1, 7, 2, 6, 3, 5, 4):
            q = (y + 2 * NYL - step) % (2 * NYL)
            at = (q % NYL) * NG + (q // NYL) * NX + x
            unit_y(step, at).wait_recv()
            unit_x(at)
        pltpu.make_async_remote_copy(
            src_ref=unit_in.at[pl.ds(0, plane - 2 * NYL)],
            dst_ref=unit_in.at[pl.ds(0, plane - 2 * NYL)],
            send_sem=unit_send,
            recv_sem=unit_recv.at[0],
            device_id=partner,
            device_id_type=MESH,
        ).wait_recv()
        unit_wide[...] = unit_in[...].astype(F32).reshape(plane * packed, LANES)
        for yy in range(NYL):
            for k in range(images_here):
                for p in range(pieces):
                    unit_full[
                        yy * half + k * NG : yy * half + (k + 1) * NG,
                        p * LANES : (p + 1) * LANES,
                    ] = unit_wide[
                        pl.ds(yy * NG * packed + k * pieces + p, NG, stride=packed), :
                    ]
        units = unit_full[...].astype(BF16)

        logits = 4.0 * dot_nt(text_rows_b, units) - 2.0
        dscaled = -4.0 * labels / (1.0 + jnp.exp(labels * logits))
        turned = jnp.transpose(dscaled).astype(BF16)
        dscaled = dscaled.astype(BF16)

        def gi_copy(n, xx):
            return pltpu.make_async_remote_copy(
                src_ref=gi_box.at[n, xx],
                dst_ref=gi_in.at[n, x],
                send_sem=gi_send.at[n],
                recv_sem=gi_recv.at[n],
                device_id=(me, (yhi * NX + xx) * 2 + c),
                device_id_type=MESH,
            )

        pair_rows = 2 * half
        for n in range(2):
            for xx in range(NX):
                gi_box[n, xx] = dot_nn(
                    turned[n * pair_rows : (n + 1) * pair_rows],
                    text_cols_b[:, xx * wide : (xx + 1) * wide],
                ).astype(BF16)
            for i in (2, 1, 3):
                gi_copy(n, (x + i) % NX).start()
            gi_in[n, x] = gi_box[n, x]

        text_grad = dot_nn(dscaled, units)
        for t in range(texts_here):
            for p in range(pieces):
                gt_f[pl.ds(t * pieces + p, 2 * nz, stride=packed), :] = text_grad[
                    t * 2 * nz : (t + 1) * 2 * nz, p * LANES : (p + 1) * LANES
                ]
        core_rows = nz * packed
        gt_copy = pltpu.make_async_remote_copy(
            src_ref=gt_f.at[pl.ds(pl.multiple_of(other * core_rows, 8), core_rows)],
            dst_ref=gt_in,
            send_sem=gt_send,
            recv_sem=gt_recv,
            device_id=partner,
            device_id_type=MESH,
        )
        gt_copy.start()

        gt_copy.wait()
        own_sums = gt_f[pl.ds(pl.multiple_of(c * core_rows, 8), core_rows), :]
        gt_box[...] = (own_sums + gt_in[...]).astype(BF16).reshape(nz, packed, LANES)

        def gtz_copy(zz):
            return pltpu.make_async_remote_copy(
                src_ref=gt_box.at[zz],
                dst_ref=gtz_in.at[z],
                send_sem=gtz_send,
                recv_sem=gtz_recv,
                device_id=(zz * NYL + ylo, mp),
                device_id_type=MESH,
            )

        @pl.loop(1, nz)
        def _(i):
            gtz_copy(wrap(z + i, nz)).start()

        gtz_in[z] = gt_box[z]

        def gy_copy(yy, core):
            return pltpu.make_async_remote_copy(
                src_ref=gy_box.at[yy * 2 + core],
                dst_ref=gy_in.at[c * 2 * NYL + y],
                send_sem=gy_send,
                recv_sem=gy_recv,
                device_id=(z * NYL + yy % NYL, ((yy // NYL) * NX + x) * 2 + core),
                device_id_type=MESH,
            )

        for n in range(2):
            pltpu.make_async_remote_copy(
                src_ref=gi_in.at[n, pl.ds(0, NX - 1)],
                dst_ref=gi_in.at[n, pl.ds(0, NX - 1)],
                send_sem=gi_send.at[n],
                recv_sem=gi_recv.at[n],
                device_id=partner,
                device_id_type=MESH,
            ).wait()
            gi_sum[...] = jnp.sum(gi_in[n].astype(F32), axis=0)
            turn = [(row * NYL + 2 * n + r, core) for row in (0, 1) for r in (0, 1) for core in (0, 1)]
            for yy, core in turn:
                q = (yy // NYL) * 2 + core
                r = (yy % 2) * half
                gy_box[yy * 2 + core, :, 0:HD] = gi_sum[
                    r : r + half, q * HD : (q + 1) * HD
                ].astype(BF16)
            for yy, core in turn:

                @pl.when((yy != y) | (core != c))
                def _():
                    gy_copy(yy, core).start()

        gy_in[c * 2 * NYL + y] = gy_box[y * 2 + c]

        pltpu.make_async_remote_copy(
            src_ref=gtz_in.at[pl.ds(0, nz - 1)],
            dst_ref=gtz_in.at[pl.ds(0, nz - 1)],
            send_sem=gtz_send,
            recv_sem=gtz_recv,
            device_id=partner,
            device_id_type=MESH,
        ).wait()
        summed = jnp.sum(gtz_in[...].astype(F32), axis=0)
        for t in range(texts_here):
            for p in range(pieces):
                r = t * pieces + p
                grad_text[t : t + 1, p * LANES : (p + 1) * LANES] = summed[r : r + 1, :]

        pltpu.make_async_remote_copy(
            src_ref=gy_in.at[pl.ds(0, 4 * NYL - 1)],
            dst_ref=gy_in.at[pl.ds(0, 4 * NYL - 1)],
            send_sem=gy_send,
            recv_sem=gy_recv,
            device_id=partner,
            device_id_type=MESH,
        ).wait()
        for core in range(2):
            part = gy_in[core * 2 * NYL : (core + 1) * 2 * NYL].astype(F32)
            grad_image[core * half : (core + 1) * half, :] = jnp.sum(part, axis=0)[:, 0:HD]

        pltpu.make_async_remote_copy(
            src_ref=unit_in.at[pl.ds(0, plane - 1)],
            dst_ref=unit_in.at[pl.ds(0, plane - 1)],
            send_sem=unit_send,
            recv_sem=unit_recv.at[0],
            device_id=partner,
            device_id_type=MESH,
        ).wait_send()

        @pl.when(my_half == c)
        def _():
            pltpu.make_async_remote_copy(
                src_ref=outbox.at[pl.ds(0, dp_size - 1)],
                dst_ref=outbox.at[pl.ds(0, dp_size - 1)],
                send_sem=a2a_send,
                recv_sem=a2a_recv,
                device_id=partner,
                device_id_type=MESH,
            ).wait_send()

        @pl.when(my_half != c)
        def _():
            pltpu.make_async_remote_copy(
                src_ref=outbox,
                dst_ref=outbox,
                send_sem=a2a_send,
                recv_sem=a2a_recv,
                device_id=partner,
                device_id_type=MESH,
            ).wait_send()

        for k in range(images_here):
            pltpu.make_async_remote_copy(
                src_ref=feats.at[k, pl.ds(0, NG - 1)],
                dst_ref=feats.at[k, pl.ds(0, NG - 1)],
                send_sem=g_send.at[k],
                recv_sem=g_recv.at[k, 0],
                device_id=partner,
                device_id_type=MESH,
            ).wait_send()

    dma = pltpu.SemaphoreType.DMA
    scratch = [
        pltpu.VMEM((dp_size * dp_size // LANES, LANES), jnp.int32),
        pltpu.VMEM((dp_size * dp_size // LANES, LANES), jnp.int32),
        pltpu.VMEM((HD, dp_size * MAXP), BF16),
        pltpu.VMEM((3 * HD, width), BF16),
        pltpu.VMEM((HD, width), BF16),
        pltpu.VMEM((texts_here, width), BF16),
        dma((6,)),
        pltpu.VMEM((dp_size, MAXP, HD), BF16),
        pltpu.VMEM((2 * half, MAXP, HD), BF16),
        pltpu.VMEM((3 * HD, width), BF16),
        pltpu.VMEM((HD, width), BF16),
        pltpu.VMEM((images_here, NG, 2 * HD, LANES), BF16),
        pltpu.VMEM((packed, LANES), F32),
        pltpu.VMEM((packed, LANES), BF16),
        pltpu.VMEM((2 * nz, packed, LANES), BF16),
        pltpu.VMEM((2 * nz * packed, LANES), F32),
        pltpu.VMEM((text_rows, width), F32),
        pltpu.VMEM((text_rows, NX * wide), F32),
        pltpu.VMEM((NG * packed, LANES), F32),
        pltpu.VMEM((NG, packed, LANES), BF16),
        pltpu.VMEM((NG, packed, LANES), BF16),
        pltpu.VMEM((packed, LANES), F32),
        pltpu.VMEM((plane, packed, LANES), BF16),
        pltpu.VMEM((plane * packed, LANES), F32),
        pltpu.VMEM((rows, width), F32),
        pltpu.VMEM((2, NX, rows // 2, wide), BF16),
        pltpu.VMEM((2, NX, rows // 2, wide), BF16),
        pltpu.VMEM((rows // 2, wide), F32),
        pltpu.VMEM((4 * NYL, half, LANES), BF16),
        pltpu.VMEM((4 * NYL, half, LANES), BF16),
        pltpu.VMEM((2 * nz * packed, LANES), F32),
        pltpu.VMEM((nz * packed, LANES), F32),
        pltpu.VMEM((nz, packed, LANES), BF16),
        pltpu.VMEM((nz, packed, LANES), BF16),
        dma,
        dma,
        dma,
        dma((2,)),
        dma((2,)),
        dma((images_here,)),
        dma((images_here, NG)),
        dma,
        dma,
        dma,
        dma,
        dma,
        dma,
        dma,
        dma((2 * NYL,)),
        dma((2,)),
        dma((2,)),
        dma,
        dma,
        dma,
        dma,
        dma,
        dma,
    ]
    return kernel, scratch


def on_device(patches, counts, dest, w_qkv, w_out, text):
    dp_size = lax.axis_size("dp")
    width = w_qkv.shape[2]
    texts_here = text.shape[0]
    kernel, scratch = make_kernel(dp_size, width, texts_here)
    vmem = pl.BlockSpec(memory_space=pltpu.VMEM)
    return pl.pallas_call(
        kernel,
        out_shape=(
            jax.ShapeDtypeStruct((dp_size, HD), F32),
            jax.ShapeDtypeStruct((texts_here, width), F32),
        ),
        in_specs=[pl.BlockSpec(memory_space=pltpu.HBM)] * 6,
        out_specs=(vmem, vmem),
        scratch_shapes=scratch,
        compiler_params=pltpu.CompilerParams(
            collective_id=0, has_side_effects=True, vmem_limit_bytes=58 * 1024 * 1024
        ),
    )(
        counts.reshape(-1, LANES),
        dest.reshape(-1, LANES),
        patches,
        w_qkv.reshape(3 * HD, width),
        w_out,
        text,
    )


def solution(mesh):
    placed = (P("mp", "dp"), P(), P(), P(None, "mp", None), P("mp", None), P(("dp", "mp"), None))
    return jax.shard_map(
        on_device,
        mesh=mesh,
        in_specs=placed,
        out_specs=(P("dp", "mp"), P(("dp", "mp"), None)),
        check_vma=False,
    )
```

```python
import math

import jax
import jax.numpy as jnp
from jax import lax
from jax.experimental import pallas as pl
from jax.experimental.pallas import tpu as pltpu
from jax.sharding import PartitionSpec as P

HD = 72
MAXP = 16
NYL = 4
NYH = 2
NX = 4
NG = NYH * NX
LANES = 128
F32 = jnp.float32
BF16 = jnp.bfloat16
MESH = pl.DeviceIdType.MESH


def iota(shape, dim):
    return lax.broadcasted_iota(jnp.int32, shape, dim)


def dot_nn(a, b):
    return lax.dot_general(a, b, (((1,), (0,)), ((), ())), preferred_element_type=F32)


def dot_nt(a, b):
    return lax.dot_general(a, b, (((1,), (1,)), ((), ())), preferred_element_type=F32)


def wrap(value, size):
    return jnp.where(value >= size, value - size, value)


def make_kernel(dp_size, width, texts_here):
    nz = dp_size // NYL
    half = dp_size // 2
    images_here = half // NG
    pieces = width // LANES
    used = images_here * pieces
    packed = -(-used // 16) * 16
    slots = dp_size * MAXP
    half_slots = half * MAXP
    plane = NYL * NG
    rows = NYL * half
    text_rows = texts_here * 2 * nz
    wide = -(-(4 * HD) // LANES) * LANES

    def kernel(
        counts_in,
        dest_in,
        patches_in,
        w_qkv_in,
        w_out_in,
        text_arg,
        grad_image,
        grad_text,
        counts,
        dest,
        patches,
        w_qkv,
        w_out,
        text,
        in_sem,
        outbox,
        inbox,
        w_qkv_peer,
        w_out_peer,
        feats,
        qkv,
        text_f,
        text_box,
        text_in,
        text_wide,
        text_full,
        text_pad,
        part_f,
        part_b,
        part_in,
        mean_f,
        unit_in,
        unit_wide,
        unit_full,
        gi_box,
        gi_in,
        gi_sum,
        gy_box,
        gy_in,
        gt_f,
        gt_in,
        gt_box,
        gtz_in,
        local_sem,
        a2a_send,
        a2a_recv,
        w_send,
        w_recv,
        g_send,
        g_recv,
        text_send,
        text_recv,
        swap_send,
        swap_recv,
        part_send,
        part_recv,
        unit_send,
        unit_recv,
        gi_send,
        gi_recv,
        gy_send,
        gy_recv,
        gt_send,
        gt_recv,
        gtz_send,
        gtz_recv,
    ):
        me = lax.axis_index("dp")
        mp = lax.axis_index("mp")
        g, c = mp // 2, mp % 2
        z, ylo = me // NYL, me % NYL
        yhi, x = g // NX, g % NX
        y = yhi * NYL + ylo
        other = 1 - c
        partner = (me, g * 2 + other)
        my_half = me // half
        my_slot = me % half
        extra = jnp.where(my_half == c, 0, 1)

        loads = [
            pltpu.make_async_copy(src, dst, in_sem.at[i])
            for i, (src, dst) in enumerate(
                (
                    (dest_in, dest),
                    (counts_in, counts),
                    (patches_in, patches),
                    (w_qkv_in, w_qkv),
                    (w_out_in, w_out),
                    (text_arg, text),
                )
            )
        ]
        for load in loads:
            load.start()

        barrier = pltpu.get_barrier_semaphore()

        def greet(device):
            pl.semaphore_signal(barrier, inc=1, device_id=device, device_id_type=MESH)

        @pl.loop(0, half)
        def _(i):
            src = half * c + i
            greet((src, g * 2 + other))

            @pl.when(src != me)
            def _():
                greet((src, mp))

        greet(partner)

        @pl.loop(1, nz)
        def _(i):
            greet((wrap(z + i, nz) * NYL + ylo, mp))

        place = ylo * NG + g

        @pl.loop(1, 2 * NYL)
        def _(i):
            q = (y + i) % (2 * NYL)
            greet((z * NYL + q % NYL, ((q // NYL) * NX + x) * 2))
            greet((z * NYL + q % NYL, ((q // NYL) * NX + x) * 2 + 1))

        for i in range(1, NX):
            greet((me, (yhi * NX + (x + i) % NX) * 2 + c))
            greet((me, ((1 - yhi) * NX + (x + i) % NX) * 2 + c))

        for buffer in (text_f, text_pad, part_f, mean_f, gt_f, gy_box):
            buffer[...] = jnp.zeros_like(buffer)

        loads[0].wait()
        loads[1].wait()
        first = me * dp_size
        table_rows = dp_size * dp_size // LANES
        span = iota((dp_size, LANES), 1)
        order = iota((dp_size, LANES), 0)
        step = (order // NYL + 1) // 2
        target = wrap(z + nz // 2 + jnp.where(order // NYL % 2 == 1, nz - step, step), nz)
        target = wrap(target, nz) * NYL + (ylo + NYL - 1 - order % NYL) % NYL
        index = jnp.zeros((dp_size, 1), jnp.int32)
        base = first // LANES
        own_rows = []
        for r in range(2):
            row = jnp.minimum(base + r, table_rows - 1)
            image = (base + r) * LANES + span - first
            inside = (image >= 0) & (image < dp_size) & (base + r < table_rows)
            image = jnp.where(inside, image, dp_size)
            own_rows.append((image, counts[pl.ds(row, 1), :]))
            hit = inside & (dest[pl.ds(row, 1), :] == target)
            index = index + jnp.sum(jnp.where(hit, image, 0), axis=1, keepdims=True)
        start = jnp.zeros((dp_size, 1), jnp.int32)
        count = jnp.zeros((dp_size, 1), jnp.int32)
        for image, own in own_rows:
            start = start + jnp.sum(jnp.where(image < index, own, 0), axis=1, keepdims=True)
            count = count + jnp.sum(jnp.where(image == index, own, 0), axis=1, keepdims=True)
        position = iota((dp_size, MAXP, 1), 1)
        column = jnp.where(
            position < count.reshape(dp_size, 1, 1), start.reshape(dp_size, 1, 1) + position, -1
        ).reshape(slots, 1)
        loads[2].wait()

        def image_copy(at, d):
            return pltpu.make_async_remote_copy(
                src_ref=outbox.at[at],
                dst_ref=inbox.at[c * half + my_slot],
                send_sem=a2a_send,
                recv_sem=a2a_recv,
                device_id=(d, g * 2 + my_half),
                device_id_type=MESH,
            )

        total = (2 * half - 1 + extra) + 1 + (nz - 1) + 2 * (2 * NYL - 1) + 2 * (NX - 1)
        blocks = 4
        block_rows = slots // blocks
        block_images = dp_size // blocks
        block_z = nz // blocks
        for n in range(blocks):
            chosen = iota((block_rows, patches.shape[1]), 1) == column[
                n * block_rows : (n + 1) * block_rows
            ]
            picked = dot_nt(chosen.astype(F32).astype(BF16), patches[...]).astype(BF16)
            outbox[n * block_images : (n + 1) * block_images] = picked.reshape(
                block_images, MAXP, HD
            )
            if n == 0:
                pl.semaphore_wait(barrier, total)
            last = n == blocks - 1

            @pl.loop(n * block_z, (n + 1) * block_z - (1 if last else 0))
            def _(j):
                step = (j + 1) // 2
                zz = wrap(z + nz // 2 + jnp.where(j % 2 == 1, nz - step, step), nz)
                zz = wrap(zz, nz)
                for i in range(NYL):
                    d = zz * NYL + (ylo + NYL - 1 - i) % NYL
                    image_copy(j * NYL + i, d).start()

            if last:
                for i in range(NYL - 1):
                    d = z * NYL + (ylo + NYL - 1 - i) % NYL
                    image_copy((nz - 1) * NYL + i, d).start()

        own_copy = pltpu.make_async_copy(
            outbox.at[dp_size - 1], inbox.at[c * half + my_slot], local_sem
        )

        @pl.when(my_half == c)
        def _():
            own_copy.start()

        @pl.when(my_half != c)
        def _():
            image_copy(dp_size - 1, me).start()

        def swap(src, dst, i):
            return pltpu.make_async_remote_copy(
                src_ref=src,
                dst_ref=dst,
                send_sem=w_send.at[i],
                recv_sem=w_recv.at[i],
                device_id=partner,
                device_id_type=MESH,
            )

        swap_qkv = swap(w_qkv, w_qkv_peer, 0)
        swap_out = swap(w_out, w_out_peer, 1)
        loads[3].wait()
        swap_qkv.start()
        loads[4].wait()
        swap_out.start()

        loads[5].wait()
        text_float = text[...].astype(F32)
        text_unit = text_float * lax.rsqrt(
            jnp.sum(text_float * text_float, axis=1, keepdims=True) + 1e-6
        )
        for t in range(texts_here):
            for k in range(pieces):
                text_f[t * pieces + k : t * pieces + k + 1, :] = text_unit[
                    t : t + 1, k * LANES : (k + 1) * LANES
                ]
        own_text = text_f[...].astype(BF16)
        text_box[...] = own_text
        text_in[c * nz + z] = own_text

        def text_copy(zz):
            return pltpu.make_async_remote_copy(
                src_ref=text_box,
                dst_ref=text_in.at[c * nz + z],
                send_sem=text_send,
                recv_sem=text_recv,
                device_id=(zz * NYL + ylo, mp),
                device_id_type=MESH,
            )

        own_texts = text_in.at[pl.ds(c * nz, nz)]
        text_swap = pltpu.make_async_remote_copy(
            src_ref=own_texts,
            dst_ref=own_texts,
            send_sem=swap_send,
            recv_sem=swap_recv,
            device_id=partner,
            device_id_type=MESH,
        )

        got = jnp.zeros((half, LANES), jnp.int32)
        slot_row, slot_lane = iota((half, LANES), 0), iota((half, LANES), 1)
        half_rows = half * dp_size // LANES
        for r in range(half_rows):
            row = pl.ds(half_rows * c + r, 1)
            inside = (r * LANES + slot_lane) // dp_size == slot_row
            got = got + jnp.where(inside & (dest[row, :] == me), counts[row, :], 0)
        got = jnp.sum(got, axis=1, keepdims=True)

        @pl.when(my_half == c)
        def _():
            own_copy.wait()
            pltpu.make_async_remote_copy(
                src_ref=inbox.at[pl.ds(0, 2 * half - 1)],
                dst_ref=inbox.at[pl.ds(0, 2 * half - 1)],
                send_sem=a2a_send,
                recv_sem=a2a_recv,
                device_id=partner,
                device_id_type=MESH,
            ).wait_recv()

        @pl.when(my_half != c)
        def _():
            pltpu.make_async_remote_copy(
                src_ref=inbox,
                dst_ref=inbox,
                send_sem=a2a_send,
                recv_sem=a2a_recv,
                device_id=partner,
                device_id_type=MESH,
            ).wait_recv()

        eye = (iota((HD, HD), 0) == iota((HD, HD), 1)).astype(F32).astype(BF16)

        across = (1 - yhi) * NX + x
        left_x, right_x = lax.rem(x + NX - 1, NX), lax.rem(x + 1, NX)
        far_x = lax.rem(x + 2, NX)

        def feat_copy(k, owner, to):
            return pltpu.make_async_remote_copy(
                src_ref=feats.at[k, owner],
                dst_ref=feats.at[k, owner],
                send_sem=g_send.at[k],
                recv_sem=g_recv.at[k, owner],
                device_id=(me, to * 2 + c),
                device_id_type=MESH,
            )

        own_row, far_row = yhi * NX, (1 - yhi) * NX
        left, right = own_row + left_x, own_row + right_x
        for k in range(images_here):
            low, high = (
                dot_nt(eye, inbox[r + k * NG : r + (k + 1) * NG].reshape(LANES, HD))
                for r in (0, half)
            )
            feats[k, g] = jnp.concatenate([low, high], axis=0).astype(BF16)
            feat_copy(k, g, across).start()
            feat_copy(k, g, left).start()
            feat_copy(k, g, right).start()

        @pl.loop(1, nz)
        def _(i):
            text_copy(wrap(z + i, nz)).start()

        for k in range(images_here):
            feat_copy(k, left, left).wait_recv()
            if k % 2 == 0:
                feat_copy(k, left, right).start()
            feat_copy(k, right, left).wait_recv()
            if k % 2 == 1:
                feat_copy(k, right, left).start()
            feat_copy(k, across, across).wait_recv()
            feat_copy(k, across, own_row + far_x).start()
            feat_copy(k, across, left).start()
            feat_copy(k, across, right).start()

        swap_qkv.wait()
        swap_out.wait()

        for k in range(images_here):
            feat_copy(k, own_row + far_x, left).wait_recv()
            for xx in (left_x, right_x, far_x):
                feat_copy(k, far_row + xx, left).wait_recv()
            full = feats[k].reshape(width, LANES).astype(F32)
            centred = full - jnp.sum(full, axis=0, keepdims=True) / width
            variance = jnp.sum(centred * centred, axis=0, keepdims=True) / width
            normed = (centred * lax.rsqrt(variance + 1e-6)).astype(BF16)
            qkv[k, 0] = dot_nn(w_qkv[...], normed)
            qkv[k, 1] = dot_nn(w_qkv_peer[...], normed)
        pltpu.make_async_remote_copy(
            src_ref=text_in.at[pl.ds(0, nz - 1)],
            dst_ref=text_in.at[pl.ds(0, nz - 1)],
            send_sem=text_send,
            recv_sem=text_recv,
            device_id=partner,
            device_id_type=MESH,
        ).wait()
        text_swap.start()
        row8, lane8 = iota((NG, LANES), 0), iota((NG, LANES), 1)
        same = iota((LANES, LANES), 0) // MAXP == iota((LANES, LANES), 1) // MAXP
        heads = ([], [])
        for k in range(images_here):
            got_k = got[k * NG : (k + 1) * NG]
            got_float = got_k.astype(F32)
            real = (lane8 // MAXP == row8) & (lane8 % MAXP < got_k)
            member = real.astype(F32).astype(BF16)
            key_count = jnp.broadcast_to(got_k.reshape(NG, 1, 1), (NG, MAXP, 1))
            key_count = key_count.reshape(LANES, 1)
            keep = same & (iota((LANES, 1), 0) % MAXP < key_count)
            for h in range(2):
                query = qkv[k, h, 0:HD].astype(BF16)
                key = jnp.transpose(qkv[k, h, HD : 2 * HD]).astype(BF16)
                value = qkv[k, h, 2 * HD : 3 * HD].astype(BF16)
                scores = dot_nn(key, query) / math.sqrt(HD)
                scores = jnp.where(keep, scores, -1e30)
                raised = jnp.exp(scores - jnp.max(scores, axis=0, keepdims=True))
                weights = (raised / jnp.sum(raised, axis=0, keepdims=True)).astype(BF16)
                mixed = dot_nn(value, weights).astype(BF16)
                heads[h].append(dot_nt(member, mixed) / got_float)
        term = jnp.zeros((half, width), F32)
        for pooled, wo in zip(heads, (w_out, w_out_peer)):
            term = term + dot_nn(jnp.concatenate(pooled, axis=0).astype(BF16), wo[...])
        for k in range(images_here):
            for p in range(pieces):
                part_f[pl.ds(k * pieces + p, NG, stride=packed), :] = term[
                    k * NG : (k + 1) * NG, p * LANES : (p + 1) * LANES
                ]

        part_b[...] = part_f[...].astype(BF16).reshape(NG, packed, LANES)

        def part_copy(gg):
            return pltpu.make_async_remote_copy(
                src_ref=part_b.at[gg],
                dst_ref=part_in.at[g],
                send_sem=part_send,
                recv_sem=part_recv,
                device_id=(me, gg * 2 + c),
                device_id_type=MESH,
            )

        for row in (1 - yhi, yhi):
            for i in (2, 1, 3):
                part_copy(row * NX + (x + i) % NX).start()
        part_copy(across).start()

        part_in[g] = part_b[g]

        here = (lane8 // MAXP == g).astype(F32).astype(BF16)
        for k in range(images_here):
            own_got = jnp.sum(
                jnp.where(iota((NG, 1), 0) == g, got[k * NG : (k + 1) * NG], 0),
                axis=0,
                keepdims=True,
            ).astype(F32)
            mean = dot_nt(here, feats[k].reshape(width, LANES)) / own_got
            for p in range(pieces):
                r = k * pieces + p
                mean_f[r : r + 1, :] = mean[0:1, p * LANES : (p + 1) * LANES]

        text_swap.wait()
        text_wide[...] = text_in[...].astype(F32).reshape(2 * nz * packed, LANES)
        for t in range(texts_here):
            for p in range(pieces):
                text_full[t * 2 * nz : (t + 1) * 2 * nz, p * LANES : (p + 1) * LANES] = (
                    text_wide[pl.ds(t * pieces + p, 2 * nz, stride=packed), :]
                )
        for xx in range(NX):
            for q in range(4):
                m = ((q // 2) * NX + xx) * 2 + q % 2
                text_pad[:, xx * wide + q * HD : xx * wide + (q + 1) * HD] = text_full[
                    :, m * HD : (m + 1) * HD
                ]
        text_rows_b = text_full[...].astype(BF16)
        text_cols_b = text_pad[...].astype(BF16)

        part_seven = pltpu.make_async_remote_copy(
            src_ref=part_in.at[pl.ds(0, NG - 1)],
            dst_ref=part_in.at[pl.ds(0, NG - 1)],
            send_sem=part_send,
            recv_sem=part_recv,
            device_id=partner,
            device_id_type=MESH,
        )
        part_seven.wait()
        pooled = jnp.sum(part_in[...].astype(F32), axis=0) + mean_f[...]
        squares = jnp.sum(pooled * pooled, axis=1, keepdims=True)
        row_id = iota((packed, 1), 0)
        scale = jnp.zeros((packed, 1), F32)
        for k in range(images_here):
            inside = (row_id >= k * pieces) & (row_id < (k + 1) * pieces)
            norm = jnp.sum(jnp.where(inside, squares, 0.0), axis=0, keepdims=True)
            scale = jnp.where(inside, lax.rsqrt(norm + 1e-6), scale)
        own_unit = (pooled * scale).astype(BF16)
        unit_in[place] = own_unit

        def unit_y(step, at):
            q = (y + step) % (2 * NYL)
            return pltpu.make_async_remote_copy(
                src_ref=unit_in.at[at],
                dst_ref=unit_in.at[at],
                send_sem=unit_send,
                recv_sem=unit_recv.at[step],
                device_id=(z * NYL + q % NYL, ((q // NYL) * NX + x) * 2 + c),
                device_id_type=MESH,
            )

        def unit_x(at):
            for i in (2, 1, 3):
                pltpu.make_async_remote_copy(
                    src_ref=unit_in.at[at],
                    dst_ref=unit_in.at[at],
                    send_sem=unit_send,
                    recv_sem=unit_recv.at[0],
                    device_id=(me, (yhi * NX + (x + i) % NX) * 2 + c),
                    device_id_type=MESH,
                ).start()

        for step in (4, 3, 5, 2, 6, 1, 7):
            unit_y(step, place).start()
        unit_x(place)

        text_row = iota((text_rows, 1), 0)
        text_source = (text_row % nz) * NYL + ylo
        text_core = (text_row % (2 * nz)) // nz
        pair_at = text_source * dp_size + (g * 2 + text_core) * texts_here + text_row // (2 * nz)
        pair_lane = iota((text_rows, LANES), 1)
        pair_dest = jnp.zeros((text_rows, LANES), jnp.int32)
        for r in range(table_rows):
            pair_dest = pair_dest + jnp.where(
                pair_at == r * LANES + pair_lane, dest[r : r + 1, :], 0
            )
        pair_dest = jnp.sum(pair_dest, axis=1, keepdims=True)
        image_lane = iota((text_rows, rows), 1)
        image_source = c * half + image_lane % half
        image_dest = z * NYL + image_lane // half
        paired = (image_source == text_source) & (image_dest == pair_dest)
        labels = jnp.where(paired, 1.0, -1.0)

        for step in (1, 7, 2, 6, 3, 5, 4):
            q = (y + 2 * NYL - step) % (2 * NYL)
            at = (q % NYL) * NG + (q // NYL) * NX + x
            unit_y(step, at).wait_recv()
            unit_x(at)
        pltpu.make_async_remote_copy(
            src_ref=unit_in.at[pl.ds(0, plane - 2 * NYL)],
            dst_ref=unit_in.at[pl.ds(0, plane - 2 * NYL)],
            send_sem=unit_send,
            recv_sem=unit_recv.at[0],
            device_id=partner,
            device_id_type=MESH,
        ).wait_recv()
        unit_wide[...] = unit_in[...].astype(F32).reshape(plane * packed, LANES)
        for yy in range(NYL):
            for k in range(images_here):
                for p in range(pieces):
                    unit_full[
                        yy * half + k * NG : yy * half + (k + 1) * NG,
                        p * LANES : (p + 1) * LANES,
                    ] = unit_wide[
                        pl.ds(yy * NG * packed + k * pieces + p, NG, stride=packed), :
                    ]
        units = unit_full[...].astype(BF16)

        logits = 4.0 * dot_nt(text_rows_b, units) - 2.0
        dscaled = -4.0 * labels / (1.0 + jnp.exp(labels * logits))
        turned = jnp.transpose(dscaled).astype(BF16)
        dscaled = dscaled.astype(BF16)

        def gi_copy(n, xx):
            return pltpu.make_async_remote_copy(
                src_ref=gi_box.at[n, xx],
                dst_ref=gi_in.at[n, x],
                send_sem=gi_send.at[n],
                recv_sem=gi_recv.at[n],
                device_id=(me, (yhi * NX + xx) * 2 + c),
                device_id_type=MESH,
            )

        pair_rows = 2 * half
        for n in range(2):
            for xx in range(NX):
                gi_box[n, xx] = dot_nn(
                    turned[n * pair_rows : (n + 1) * pair_rows],
                    text_cols_b[:, xx * wide : (xx + 1) * wide],
                ).astype(BF16)
            for i in (2, 1, 3):
                gi_copy(n, (x + i) % NX).start()
            gi_in[n, x] = gi_box[n, x]

        text_grad = dot_nn(dscaled, units)
        for t in range(texts_here):
            for p in range(pieces):
                gt_f[pl.ds(t * pieces + p, 2 * nz, stride=packed), :] = text_grad[
                    t * 2 * nz : (t + 1) * 2 * nz, p * LANES : (p + 1) * LANES
                ]
        core_rows = nz * packed
        gt_copy = pltpu.make_async_remote_copy(
            src_ref=gt_f.at[pl.ds(pl.multiple_of(other * core_rows, 8), core_rows)],
            dst_ref=gt_in,
            send_sem=gt_send,
            recv_sem=gt_recv,
            device_id=partner,
            device_id_type=MESH,
        )
        gt_copy.start()

        gt_copy.wait()
        own_sums = gt_f[pl.ds(pl.multiple_of(c * core_rows, 8), core_rows), :]
        gt_box[...] = (own_sums + gt_in[...]).astype(BF16).reshape(nz, packed, LANES)

        def gtz_copy(zz):
            return pltpu.make_async_remote_copy(
                src_ref=gt_box.at[zz],
                dst_ref=gtz_in.at[z],
                send_sem=gtz_send,
                recv_sem=gtz_recv,
                device_id=(zz * NYL + ylo, mp),
                device_id_type=MESH,
            )

        for i in sorted(range(1, nz), key=lambda step: -min(step, nz - step)):
            gtz_copy(wrap(z + i, nz)).start()

        gtz_in[z] = gt_box[z]

        def gy_copy(yy, core):
            return pltpu.make_async_remote_copy(
                src_ref=gy_box.at[yy * 2 + core],
                dst_ref=gy_in.at[c * 2 * NYL + y],
                send_sem=gy_send,
                recv_sem=gy_recv,
                device_id=(z * NYL + yy % NYL, ((yy // NYL) * NX + x) * 2 + core),
                device_id_type=MESH,
            )

        for n in range(2):
            pltpu.make_async_remote_copy(
                src_ref=gi_in.at[n, pl.ds(0, NX - 1)],
                dst_ref=gi_in.at[n, pl.ds(0, NX - 1)],
                send_sem=gi_send.at[n],
                recv_sem=gi_recv.at[n],
                device_id=partner,
                device_id_type=MESH,
            ).wait()
            gi_sum[...] = jnp.sum(gi_in[n].astype(F32), axis=0)
            turn = [(row * NYL + 2 * n + r, core) for row in (0, 1) for r in (0, 1) for core in (0, 1)]
            for yy, core in turn:
                q = (yy // NYL) * 2 + core
                r = (yy % 2) * half
                gy_box[yy * 2 + core, :, 0:HD] = gi_sum[
                    r : r + half, q * HD : (q + 1) * HD
                ].astype(BF16)
            for yy, core in turn:

                @pl.when((yy != y) | (core != c))
                def _():
                    gy_copy(yy, core).start()

        gy_in[c * 2 * NYL + y] = gy_box[y * 2 + c]

        pltpu.make_async_remote_copy(
            src_ref=gtz_in.at[pl.ds(0, nz - 1)],
            dst_ref=gtz_in.at[pl.ds(0, nz - 1)],
            send_sem=gtz_send,
            recv_sem=gtz_recv,
            device_id=partner,
            device_id_type=MESH,
        ).wait()
        summed = jnp.sum(gtz_in[...].astype(F32), axis=0)
        for t in range(texts_here):
            for p in range(pieces):
                r = t * pieces + p
                grad_text[t : t + 1, p * LANES : (p + 1) * LANES] = summed[r : r + 1, :]

        pltpu.make_async_remote_copy(
            src_ref=gy_in.at[pl.ds(0, 4 * NYL - 1)],
            dst_ref=gy_in.at[pl.ds(0, 4 * NYL - 1)],
            send_sem=gy_send,
            recv_sem=gy_recv,
            device_id=partner,
            device_id_type=MESH,
        ).wait()
        for core in range(2):
            part = gy_in[core * 2 * NYL : (core + 1) * 2 * NYL].astype(F32)
            grad_image[core * half : (core + 1) * half, :] = jnp.sum(part, axis=0)[:, 0:HD]

        pltpu.make_async_remote_copy(
            src_ref=unit_in.at[pl.ds(0, plane - 1)],
            dst_ref=unit_in.at[pl.ds(0, plane - 1)],
            send_sem=unit_send,
            recv_sem=unit_recv.at[0],
            device_id=partner,
            device_id_type=MESH,
        ).wait_send()

        @pl.when(my_half == c)
        def _():
            pltpu.make_async_remote_copy(
                src_ref=outbox.at[pl.ds(0, dp_size - 1)],
                dst_ref=outbox.at[pl.ds(0, dp_size - 1)],
                send_sem=a2a_send,
                recv_sem=a2a_recv,
                device_id=partner,
                device_id_type=MESH,
            ).wait_send()

        @pl.when(my_half != c)
        def _():
            pltpu.make_async_remote_copy(
                src_ref=outbox,
                dst_ref=outbox,
                send_sem=a2a_send,
                recv_sem=a2a_recv,
                device_id=partner,
                device_id_type=MESH,
            ).wait_send()

        for k in range(images_here):
            pltpu.make_async_remote_copy(
                src_ref=feats.at[k, pl.ds(0, NG - 1)],
                dst_ref=feats.at[k, pl.ds(0, NG - 1)],
                send_sem=g_send.at[k],
                recv_sem=g_recv.at[k, 0],
                device_id=partner,
                device_id_type=MESH,
            ).wait_send()

    dma = pltpu.SemaphoreType.DMA
    scratch = [
        pltpu.VMEM((dp_size * dp_size // LANES, LANES), jnp.int32),
        pltpu.VMEM((dp_size * dp_size // LANES, LANES), jnp.int32),
        pltpu.VMEM((HD, dp_size * MAXP), BF16),
        pltpu.VMEM((3 * HD, width), BF16),
        pltpu.VMEM((HD, width), BF16),
        pltpu.VMEM((texts_here, width), BF16),
        dma((6,)),
        pltpu.VMEM((dp_size, MAXP, HD), BF16),
        pltpu.VMEM((2 * half, MAXP, HD), BF16),
        pltpu.VMEM((3 * HD, width), BF16),
        pltpu.VMEM((HD, width), BF16),
        pltpu.VMEM((images_here, NG, 2 * HD, LANES), BF16),
        pltpu.VMEM((images_here, 2, 3 * HD, LANES), F32),
        pltpu.VMEM((packed, LANES), F32),
        pltpu.VMEM((packed, LANES), BF16),
        pltpu.VMEM((2 * nz, packed, LANES), BF16),
        pltpu.VMEM((2 * nz * packed, LANES), F32),
        pltpu.VMEM((text_rows, width), F32),
        pltpu.VMEM((text_rows, NX * wide), F32),
        pltpu.VMEM((NG * packed, LANES), F32),
        pltpu.VMEM((NG, packed, LANES), BF16),
        pltpu.VMEM((NG, packed, LANES), BF16),
        pltpu.VMEM((packed, LANES), F32),
        pltpu.VMEM((plane, packed, LANES), BF16),
        pltpu.VMEM((plane * packed, LANES), F32),
        pltpu.VMEM((rows, width), F32),
        pltpu.VMEM((2, NX, rows // 2, wide), BF16),
        pltpu.VMEM((2, NX, rows // 2, wide), BF16),
        pltpu.VMEM((rows // 2, wide), F32),
        pltpu.VMEM((4 * NYL, half, LANES), BF16),
        pltpu.VMEM((4 * NYL, half, LANES), BF16),
        pltpu.VMEM((2 * nz * packed, LANES), F32),
        pltpu.VMEM((nz * packed, LANES), F32),
        pltpu.VMEM((nz, packed, LANES), BF16),
        pltpu.VMEM((nz, packed, LANES), BF16),
        dma,
        dma,
        dma,
        dma((2,)),
        dma((2,)),
        dma((images_here,)),
        dma((images_here, NG)),
        dma,
        dma,
        dma,
        dma,
        dma,
        dma,
        dma,
        dma((2 * NYL,)),
        dma((2,)),
        dma((2,)),
        dma,
        dma,
        dma,
        dma,
        dma,
        dma,
    ]
    return kernel, scratch


def on_device(patches, counts, dest, w_qkv, w_out, text):
    dp_size = lax.axis_size("dp")
    width = w_qkv.shape[2]
    texts_here = text.shape[0]
    kernel, scratch = make_kernel(dp_size, width, texts_here)
    vmem = pl.BlockSpec(memory_space=pltpu.VMEM)
    return pl.pallas_call(
        kernel,
        out_shape=(
            jax.ShapeDtypeStruct((dp_size, HD), F32),
            jax.ShapeDtypeStruct((texts_here, width), F32),
        ),
        in_specs=[pl.BlockSpec(memory_space=pltpu.HBM)] * 6,
        out_specs=(vmem, vmem),
        scratch_shapes=scratch,
        compiler_params=pltpu.CompilerParams(
            collective_id=0, has_side_effects=True, vmem_limit_bytes=40 * 1024 * 1024
        ),
    )(
        *(
            pltpu.with_memory_space_constraint(array, pltpu.HBM)
            for array in (
                counts.reshape(-1, LANES),
                dest.reshape(-1, LANES),
                patches,
                w_qkv.reshape(3 * HD, width),
                w_out,
                text,
            )
        )
    )


def solution(mesh):
    placed = (P("mp", "dp"), P(), P(), P(None, "mp", None), P("mp", None), P(("dp", "mp"), None))
    return jax.shard_map(
        on_device,
        mesh=mesh,
        in_specs=placed,
        out_specs=(P("dp", "mp"), P(("dp", "mp"), None)),
        check_vma=False,
    )
```

```python
import math

import jax
import jax.numpy as jnp
from jax import lax
from jax.experimental import pallas as pl
from jax.experimental.pallas import tpu as pltpu
from jax.sharding import PartitionSpec as P

HD = 72
MAXP = 16
NYL = 4
NYH = 2
NX = 4
NG = NYH * NX
LANES = 128
F32 = jnp.float32
BF16 = jnp.bfloat16
MESH = pl.DeviceIdType.MESH


def iota(shape, dim):
    return lax.broadcasted_iota(jnp.int32, shape, dim)


def dot_nn(a, b):
    return lax.dot_general(a, b, (((1,), (0,)), ((), ())), preferred_element_type=F32)


def dot_nt(a, b):
    return lax.dot_general(a, b, (((1,), (1,)), ((), ())), preferred_element_type=F32)


def wrap(value, size):
    return jnp.where(value >= size, value - size, value)


def make_kernel(dp_size, width, texts_here):
    nz = dp_size // NYL
    half = dp_size // 2
    images_here = half // NG
    pieces = width // LANES
    used = images_here * pieces
    packed = -(-used // 16) * 16
    slots = dp_size * MAXP
    half_slots = half * MAXP
    plane = NYL * NG
    rows = NYL * half
    text_rows = texts_here * 2 * nz
    wide = -(-(4 * HD) // LANES) * LANES

    def kernel(
        counts_in,
        dest_in,
        patches_in,
        w_qkv_in,
        w_out_in,
        text_arg,
        grad_image,
        grad_text,
        counts,
        dest,
        patches,
        w_qkv,
        w_out,
        text,
        in_sem,
        outbox,
        inbox,
        w_qkv_peer,
        w_out_peer,
        feats,
        got_box,
        text_f,
        text_box,
        text_in,
        text_wide,
        text_full,
        text_pad,
        part_f,
        part_b,
        part_in,
        mean_f,
        unit_in,
        unit_wide,
        unit_full,
        gi_box,
        gi_in,
        gi_sum,
        gy_box,
        gy_in,
        gt_f,
        gt_in,
        gt_box,
        gtz_in,
        local_sem,
        a2a_send,
        a2a_recv,
        w_send,
        w_recv,
        g_send,
        g_recv,
        text_send,
        text_recv,
        swap_send,
        swap_recv,
        part_send,
        part_recv,
        unit_send,
        unit_recv,
        gi_send,
        gi_recv,
        gy_send,
        gy_recv,
        gt_send,
        gt_recv,
        gtz_send,
        gtz_recv,
    ):
        me = lax.axis_index("dp")
        mp = lax.axis_index("mp")
        g, c = mp // 2, mp % 2
        z, ylo = me // NYL, me % NYL
        yhi, x = g // NX, g % NX
        y = yhi * NYL + ylo
        other = 1 - c
        partner = (me, g * 2 + other)
        my_half = me // half
        my_slot = me % half
        extra = jnp.where(my_half == c, 0, 1)

        loads = [
            pltpu.make_async_copy(src, dst, in_sem.at[i])
            for i, (src, dst) in enumerate(
                (
                    (dest_in, dest),
                    (counts_in, counts),
                    (patches_in, patches),
                    (w_qkv_in, w_qkv),
                    (w_out_in, w_out),
                    (text_arg, text),
                )
            )
        ]
        for load in loads:
            load.start()

        barrier = pltpu.get_barrier_semaphore()

        def greet(device):
            pl.semaphore_signal(barrier, inc=1, device_id=device, device_id_type=MESH)

        @pl.loop(0, half)
        def _(i):
            src = half * c + i
            greet((src, g * 2 + other))

            @pl.when(src != me)
            def _():
                greet((src, mp))

        greet(partner)

        @pl.loop(1, nz)
        def _(i):
            greet((wrap(z + i, nz) * NYL + ylo, mp))

        place = ylo * NG + g

        @pl.loop(1, 2 * NYL)
        def _(i):
            q = (y + i) % (2 * NYL)
            greet((z * NYL + q % NYL, ((q // NYL) * NX + x) * 2))
            greet((z * NYL + q % NYL, ((q // NYL) * NX + x) * 2 + 1))

        for i in range(1, NX):
            greet((me, (yhi * NX + (x + i) % NX) * 2 + c))
            greet((me, ((1 - yhi) * NX + (x + i) % NX) * 2 + c))

        for buffer in (text_f, text_pad, part_f, mean_f, gt_f, gy_box):
            buffer[...] = jnp.zeros_like(buffer)

        loads[0].wait()
        loads[1].wait()
        first = me * dp_size
        table_rows = dp_size * dp_size // LANES
        span = iota((dp_size, LANES), 1)
        order = iota((dp_size, LANES), 0)
        step = (order // NYL + 1) // 2
        target = wrap(z + jnp.where(order // NYL % 2 == 1, step, nz - step), nz)
        target = target * NYL + (ylo + NYL - 1 - order % NYL) % NYL
        index = jnp.zeros((dp_size, 1), jnp.int32)
        base = first // LANES
        own_rows = []
        for r in range(2):
            row = jnp.minimum(base + r, table_rows - 1)
            image = (base + r) * LANES + span - first
            inside = (image >= 0) & (image < dp_size) & (base + r < table_rows)
            image = jnp.where(inside, image, dp_size)
            own_rows.append((image, counts[pl.ds(row, 1), :]))
            hit = inside & (dest[pl.ds(row, 1), :] == target)
            index = index + jnp.sum(jnp.where(hit, image, 0), axis=1, keepdims=True)
        start = jnp.zeros((dp_size, 1), jnp.int32)
        count = jnp.zeros((dp_size, 1), jnp.int32)
        for image, own in own_rows:
            start = start + jnp.sum(jnp.where(image < index, own, 0), axis=1, keepdims=True)
            count = count + jnp.sum(jnp.where(image == index, own, 0), axis=1, keepdims=True)
        position = iota((dp_size, MAXP, 1), 1)
        column = jnp.where(
            position < count.reshape(dp_size, 1, 1), start.reshape(dp_size, 1, 1) + position, -1
        ).reshape(slots, 1)
        loads[2].wait()

        def image_copy(at, d):
            return pltpu.make_async_remote_copy(
                src_ref=outbox.at[at],
                dst_ref=inbox.at[c * half + my_slot],
                send_sem=a2a_send,
                recv_sem=a2a_recv.at[my_slot // NG],
                device_id=(d, g * 2 + my_half),
                device_id_type=MESH,
            )

        total = (2 * half - 1 + extra) + 1 + (nz - 1) + 2 * (2 * NYL - 1) + 2 * (NX - 1)
        blocks = 4
        block_rows = slots // blocks
        block_images = dp_size // blocks
        block_z = nz // blocks
        for n in range(blocks):
            chosen = iota((block_rows, patches.shape[1]), 1) == column[
                n * block_rows : (n + 1) * block_rows
            ]
            picked = dot_nt(chosen.astype(F32).astype(BF16), patches[...]).astype(BF16)
            outbox[n * block_images : (n + 1) * block_images] = picked.reshape(
                block_images, MAXP, HD
            )
            if n == 0:
                pl.semaphore_wait(barrier, total)
                for i in range(NYL - 1):
                    image_copy(i, z * NYL + (ylo + NYL - 1 - i) % NYL).start()

            @pl.loop(n * block_z + (1 if n == 0 else 0), (n + 1) * block_z)
            def _(j):
                step = (j + 1) // 2
                zz = wrap(z + jnp.where(j % 2 == 1, step, nz - step), nz)
                for i in range(NYL):
                    d = zz * NYL + (ylo + NYL - 1 - i) % NYL
                    image_copy(j * NYL + i, d).start()

        own_copy = pltpu.make_async_copy(
            outbox.at[NYL - 1], inbox.at[c * half + my_slot], local_sem
        )

        @pl.when(my_half == c)
        def _():
            own_copy.start()

        @pl.when(my_half != c)
        def _():
            image_copy(NYL - 1, me).start()

        def swap(src, dst, i):
            return pltpu.make_async_remote_copy(
                src_ref=src,
                dst_ref=dst,
                send_sem=w_send.at[i],
                recv_sem=w_recv.at[i],
                device_id=partner,
                device_id_type=MESH,
            )

        swap_qkv = swap(w_qkv, w_qkv_peer, 0)
        swap_out = swap(w_out, w_out_peer, 1)
        loads[3].wait()
        swap_qkv.start()
        loads[4].wait()
        swap_out.start()

        loads[5].wait()
        text_float = text[...].astype(F32)
        text_unit = text_float * lax.rsqrt(
            jnp.sum(text_float * text_float, axis=1, keepdims=True) + 1e-6
        )
        for t in range(texts_here):
            for k in range(pieces):
                text_f[t * pieces + k : t * pieces + k + 1, :] = text_unit[
                    t : t + 1, k * LANES : (k + 1) * LANES
                ]
        own_text = text_f[...].astype(BF16)
        text_box[...] = own_text
        text_in[c * nz + z] = own_text

        def text_copy(zz):
            return pltpu.make_async_remote_copy(
                src_ref=text_box,
                dst_ref=text_in.at[c * nz + z],
                send_sem=text_send,
                recv_sem=text_recv,
                device_id=(zz * NYL + ylo, mp),
                device_id_type=MESH,
            )

        own_texts = text_in.at[pl.ds(c * nz, nz)]
        text_swap = pltpu.make_async_remote_copy(
            src_ref=own_texts,
            dst_ref=own_texts,
            send_sem=swap_send,
            recv_sem=swap_recv,
            device_id=partner,
            device_id_type=MESH,
        )

        got = jnp.zeros((half, LANES), jnp.int32)
        slot_row, slot_lane = iota((half, LANES), 0), iota((half, LANES), 1)
        half_rows = half * dp_size // LANES
        for r in range(half_rows):
            row = pl.ds(half_rows * c + r, 1)
            inside = (r * LANES + slot_lane) // dp_size == slot_row
            got = got + jnp.where(inside & (dest[row, :] == me), counts[row, :], 0)
        got_box[...] = jnp.broadcast_to(jnp.sum(got, axis=1, keepdims=True), (half, LANES))

        def near_first(core):
            if images_here == 1:
                return [0]
            away = []
            for k in range(images_here):
                gap = jnp.abs(2 * z - (core * nz + 4 * k + 1))
                away.append(jnp.minimum(gap, 2 * nz - gap))
            d0, d1, d2 = away
            nearest = jnp.where(
                d0 < d1, jnp.where(d0 < d2, 0, 2), jnp.where(d1 < d2, 1, 2)
            )
            farthest = jnp.where(
                d0 > d1, jnp.where(d0 > d2, 0, 2), jnp.where(d1 > d2, 1, 2)
            )
            return [nearest, 3 - nearest - farthest, farthest]

        chunk_of = near_first(c)
        eye = (iota((HD, HD), 0) == iota((HD, HD), 1)).astype(F32).astype(BF16)

        def arrive(k):
            chunk = chunk_of[k]
            holds_own = (my_half == c) & (my_slot // NG == chunk)

            def wait_images(many):
                pltpu.make_async_remote_copy(
                    src_ref=inbox.at[pl.ds(0, many)],
                    dst_ref=inbox.at[pl.ds(0, many)],
                    send_sem=a2a_send,
                    recv_sem=a2a_recv.at[chunk],
                    device_id=partner,
                    device_id_type=MESH,
                ).wait_recv()

            @pl.when(holds_own)
            def _():
                own_copy.wait()
                wait_images(2 * NG - 1)

            @pl.when(jnp.logical_not(holds_own))
            def _():
                wait_images(2 * NG)

            low, high = (
                dot_nt(eye, inbox[pl.ds(r + chunk * NG, NG)].reshape(LANES, HD))
                for r in (0, half)
            )
            feats[k, g] = jnp.concatenate([low, high], axis=0).astype(BF16)
            feat_copy(k, g, across).start()
            feat_copy(k, g, left).start()
            feat_copy(k, g, right).start()

        across = (1 - yhi) * NX + x
        left_x, right_x = lax.rem(x + NX - 1, NX), lax.rem(x + 1, NX)
        far_x = lax.rem(x + 2, NX)

        def feat_copy(k, owner, to):
            return pltpu.make_async_remote_copy(
                src_ref=feats.at[k, owner],
                dst_ref=feats.at[k, owner],
                send_sem=g_send.at[k],
                recv_sem=g_recv.at[k, owner],
                device_id=(me, to * 2 + c),
                device_id_type=MESH,
            )

        own_row, far_row = yhi * NX, (1 - yhi) * NX
        left, right = own_row + left_x, own_row + right_x
        def pass_row(k):
            feat_copy(k, left, left).wait_recv()
            if k % 2 == 0:
                feat_copy(k, left, right).start()
            feat_copy(k, right, left).wait_recv()
            if k % 2 == 1:
                feat_copy(k, right, left).start()

        def pass_across(k):
            feat_copy(k, across, across).wait_recv()
            feat_copy(k, across, own_row + far_x).start()
            feat_copy(k, across, left).start()
            feat_copy(k, across, right).start()

        def send_texts():
            @pl.loop(1, nz)
            def _(i):
                text_copy(wrap(z + i, nz)).start()

        row8, lane8 = iota((NG, LANES), 0), iota((NG, LANES), 1)
        same = iota((LANES, LANES), 0) // MAXP == iota((LANES, LANES), 1) // MAXP
        heads = ([], [])
        got_now = []

        def attend(k):
            feat_copy(k, own_row + far_x, left).wait_recv()
            for xx in (left_x, right_x, far_x):
                feat_copy(k, far_row + xx, left).wait_recv()
            full = feats[k].reshape(width, LANES).astype(F32)
            centred = full - jnp.sum(full, axis=0, keepdims=True) / width
            variance = jnp.sum(centred * centred, axis=0, keepdims=True) / width
            normed = (centred * lax.rsqrt(variance + 1e-6)).astype(BF16)
            got_k = got_box[pl.ds(pl.multiple_of(chunk_of[k] * NG, NG), NG), 0:1]
            got_now.append(got_k)
            got_float = got_k.astype(F32)
            real = (lane8 // MAXP == row8) & (lane8 % MAXP < got_k)
            member = real.astype(F32).astype(BF16)
            key_count = jnp.broadcast_to(got_k.reshape(NG, 1, 1), (NG, MAXP, 1))
            key_count = key_count.reshape(LANES, 1)
            keep = same & (iota((LANES, 1), 0) % MAXP < key_count)
            for h, wq in enumerate((w_qkv, w_qkv_peer)):
                projected = dot_nn(wq[...], normed)
                query = projected[0:HD].astype(BF16)
                key = jnp.transpose(projected[HD : 2 * HD]).astype(BF16)
                value = projected[2 * HD : 3 * HD].astype(BF16)
                scores = dot_nn(key, query) / math.sqrt(HD)
                scores = jnp.where(keep, scores, -1e30)
                raised = jnp.exp(scores - jnp.max(scores, axis=0, keepdims=True))
                weights = (raised / jnp.sum(raised, axis=0, keepdims=True)).astype(BF16)
                mixed = dot_nn(value, weights).astype(BF16)
                heads[h].append(dot_nt(member, mixed) / got_float)

        arrive(0)
        if images_here == 3:
            arrive(1)
            pass_row(0)
            pass_across(0)
            arrive(2)
            send_texts()
            pass_row(1)
            pass_across(1)
        else:
            send_texts()
            pass_row(0)
            pass_across(0)
        swap_qkv.wait()
        swap_out.wait()
        attend(0)
        if images_here == 3:
            pass_row(2)
            pass_across(2)
            attend(1)
            attend(2)
        pltpu.make_async_remote_copy(
            src_ref=text_in.at[pl.ds(0, nz - 1)],
            dst_ref=text_in.at[pl.ds(0, nz - 1)],
            send_sem=text_send,
            recv_sem=text_recv,
            device_id=partner,
            device_id_type=MESH,
        ).wait()
        text_swap.start()
        term = jnp.zeros((half, width), F32)
        for pooled, wo in zip(heads, (w_out, w_out_peer)):
            term = term + dot_nn(jnp.concatenate(pooled, axis=0).astype(BF16), wo[...])
        for k in range(images_here):
            for p in range(pieces):
                part_f[pl.ds(k * pieces + p, NG, stride=packed), :] = term[
                    k * NG : (k + 1) * NG, p * LANES : (p + 1) * LANES
                ]

        part_b[...] = part_f[...].astype(BF16).reshape(NG, packed, LANES)

        def part_copy(gg):
            return pltpu.make_async_remote_copy(
                src_ref=part_b.at[gg],
                dst_ref=part_in.at[g],
                send_sem=part_send,
                recv_sem=part_recv,
                device_id=(me, gg * 2 + c),
                device_id_type=MESH,
            )

        for row in (1 - yhi, yhi):
            for i in (2, 1, 3):
                part_copy(row * NX + (x + i) % NX).start()
        part_copy(across).start()

        part_in[g] = part_b[g]

        here = (lane8 // MAXP == g).astype(F32).astype(BF16)
        for k in range(images_here):
            own_got = jnp.sum(
                jnp.where(iota((NG, 1), 0) == g, got_now[k], 0),
                axis=0,
                keepdims=True,
            ).astype(F32)
            mean = dot_nt(here, feats[k].reshape(width, LANES)) / own_got
            for p in range(pieces):
                r = k * pieces + p
                mean_f[r : r + 1, :] = mean[0:1, p * LANES : (p + 1) * LANES]

        text_swap.wait()
        text_wide[...] = text_in[...].astype(F32).reshape(2 * nz * packed, LANES)
        for t in range(texts_here):
            for p in range(pieces):
                text_full[t * 2 * nz : (t + 1) * 2 * nz, p * LANES : (p + 1) * LANES] = (
                    text_wide[pl.ds(t * pieces + p, 2 * nz, stride=packed), :]
                )
        for xx in range(NX):
            for q in range(4):
                m = ((q // 2) * NX + xx) * 2 + q % 2
                text_pad[:, xx * wide + q * HD : xx * wide + (q + 1) * HD] = text_full[
                    :, m * HD : (m + 1) * HD
                ]
        text_rows_b = text_full[...].astype(BF16)
        text_cols_b = text_pad[...].astype(BF16)

        part_seven = pltpu.make_async_remote_copy(
            src_ref=part_in.at[pl.ds(0, NG - 1)],
            dst_ref=part_in.at[pl.ds(0, NG - 1)],
            send_sem=part_send,
            recv_sem=part_recv,
            device_id=partner,
            device_id_type=MESH,
        )
        part_seven.wait()
        pooled = jnp.sum(part_in[...].astype(F32), axis=0) + mean_f[...]
        squares = jnp.sum(pooled * pooled, axis=1, keepdims=True)
        row_id = iota((packed, 1), 0)
        scale = jnp.zeros((packed, 1), F32)
        for k in range(images_here):
            inside = (row_id >= k * pieces) & (row_id < (k + 1) * pieces)
            norm = jnp.sum(jnp.where(inside, squares, 0.0), axis=0, keepdims=True)
            scale = jnp.where(inside, lax.rsqrt(norm + 1e-6), scale)
        own_unit = (pooled * scale).astype(BF16)
        unit_in[place] = own_unit

        def unit_y(step, at):
            q = (y + step) % (2 * NYL)
            return pltpu.make_async_remote_copy(
                src_ref=unit_in.at[at],
                dst_ref=unit_in.at[at],
                send_sem=unit_send,
                recv_sem=unit_recv.at[step],
                device_id=(z * NYL + q % NYL, ((q // NYL) * NX + x) * 2 + c),
                device_id_type=MESH,
            )

        def unit_x(at):
            for i in (2, 1, 3):
                pltpu.make_async_remote_copy(
                    src_ref=unit_in.at[at],
                    dst_ref=unit_in.at[at],
                    send_sem=unit_send,
                    recv_sem=unit_recv.at[0],
                    device_id=(me, (yhi * NX + (x + i) % NX) * 2 + c),
                    device_id_type=MESH,
                ).start()

        for step in (4, 3, 5, 2, 6, 1, 7):
            unit_y(step, place).start()
        unit_x(place)

        text_row = iota((text_rows, 1), 0)
        text_source = (text_row % nz) * NYL + ylo
        text_core = (text_row % (2 * nz)) // nz
        pair_at = text_source * dp_size + (g * 2 + text_core) * texts_here + text_row // (2 * nz)
        pair_lane = iota((text_rows, LANES), 1)
        pair_dest = jnp.zeros((text_rows, LANES), jnp.int32)
        for r in range(table_rows):
            pair_dest = pair_dest + jnp.where(
                pair_at == r * LANES + pair_lane, dest[r : r + 1, :], 0
            )
        pair_dest = jnp.sum(pair_dest, axis=1, keepdims=True)
        image_lane = iota((text_rows, rows), 1)
        image_source = c * half + image_lane % NG
        for k in range(images_here):
            image_source = image_source + jnp.where(
                image_lane % half // NG == k, chunk_of[k] * NG, 0
            )
        image_dest = z * NYL + image_lane // half
        paired = (image_source == text_source) & (image_dest == pair_dest)
        labels = jnp.where(paired, 1.0, -1.0)

        for step in (1, 7, 2, 6, 3, 5, 4):
            q = (y + 2 * NYL - step) % (2 * NYL)
            at = (q % NYL) * NG + (q // NYL) * NX + x
            unit_y(step, at).wait_recv()
            unit_x(at)
        pltpu.make_async_remote_copy(
            src_ref=unit_in.at[pl.ds(0, plane - 2 * NYL)],
            dst_ref=unit_in.at[pl.ds(0, plane - 2 * NYL)],
            send_sem=unit_send,
            recv_sem=unit_recv.at[0],
            device_id=partner,
            device_id_type=MESH,
        ).wait_recv()
        unit_wide[...] = unit_in[...].astype(F32).reshape(plane * packed, LANES)
        for yy in range(NYL):
            for k in range(images_here):
                for p in range(pieces):
                    unit_full[
                        yy * half + k * NG : yy * half + (k + 1) * NG,
                        p * LANES : (p + 1) * LANES,
                    ] = unit_wide[
                        pl.ds(yy * NG * packed + k * pieces + p, NG, stride=packed), :
                    ]
        units = unit_full[...].astype(BF16)

        logits = 4.0 * dot_nt(text_rows_b, units) - 2.0
        dscaled = -4.0 * labels / (1.0 + jnp.exp(labels * logits))
        turned = jnp.transpose(dscaled).astype(BF16)
        dscaled = dscaled.astype(BF16)

        def gi_copy(n, xx):
            return pltpu.make_async_remote_copy(
                src_ref=gi_box.at[n, xx],
                dst_ref=gi_in.at[n, x],
                send_sem=gi_send.at[n],
                recv_sem=gi_recv.at[n],
                device_id=(me, (yhi * NX + xx) * 2 + c),
                device_id_type=MESH,
            )

        pair_rows = 2 * half
        for n in range(2):
            for xx in range(NX):
                gi_box[n, xx] = dot_nn(
                    turned[n * pair_rows : (n + 1) * pair_rows],
                    text_cols_b[:, xx * wide : (xx + 1) * wide],
                ).astype(BF16)
            for i in (2, 1, 3):
                gi_copy(n, (x + i) % NX).start()
            gi_in[n, x] = gi_box[n, x]

        text_grad = dot_nn(dscaled, units)
        for t in range(texts_here):
            for p in range(pieces):
                gt_f[pl.ds(t * pieces + p, 2 * nz, stride=packed), :] = text_grad[
                    t * 2 * nz : (t + 1) * 2 * nz, p * LANES : (p + 1) * LANES
                ]
        core_rows = nz * packed
        gt_copy = pltpu.make_async_remote_copy(
            src_ref=gt_f.at[pl.ds(pl.multiple_of(other * core_rows, 8), core_rows)],
            dst_ref=gt_in,
            send_sem=gt_send,
            recv_sem=gt_recv,
            device_id=partner,
            device_id_type=MESH,
        )
        gt_copy.start()

        gt_copy.wait()
        own_sums = gt_f[pl.ds(pl.multiple_of(c * core_rows, 8), core_rows), :]
        gt_box[...] = (own_sums + gt_in[...]).astype(BF16).reshape(nz, packed, LANES)

        def gtz_copy(zz):
            return pltpu.make_async_remote_copy(
                src_ref=gt_box.at[zz],
                dst_ref=gtz_in.at[z],
                send_sem=gtz_send,
                recv_sem=gtz_recv,
                device_id=(zz * NYL + ylo, mp),
                device_id_type=MESH,
            )

        for i in sorted(range(1, nz), key=lambda step: -min(step, nz - step)):
            gtz_copy(wrap(z + i, nz)).start()

        gtz_in[z] = gt_box[z]

        def gy_copy(yy, core):
            return pltpu.make_async_remote_copy(
                src_ref=gy_box.at[yy * 2 + core],
                dst_ref=gy_in.at[c * 2 * NYL + y],
                send_sem=gy_send,
                recv_sem=gy_recv,
                device_id=(z * NYL + yy % NYL, ((yy // NYL) * NX + x) * 2 + core),
                device_id_type=MESH,
            )

        for n in range(2):
            pltpu.make_async_remote_copy(
                src_ref=gi_in.at[n, pl.ds(0, NX - 1)],
                dst_ref=gi_in.at[n, pl.ds(0, NX - 1)],
                send_sem=gi_send.at[n],
                recv_sem=gi_recv.at[n],
                device_id=partner,
                device_id_type=MESH,
            ).wait()
            gi_sum[...] = jnp.sum(gi_in[n].astype(F32), axis=0)
            turn = [(row * NYL + 2 * n + r, core) for row in (0, 1) for r in (0, 1) for core in (0, 1)]
            for yy, core in turn:
                q = (yy // NYL) * 2 + core
                r = (yy % 2) * half
                gy_box[yy * 2 + core, :, 0:HD] = gi_sum[
                    r : r + half, q * HD : (q + 1) * HD
                ].astype(BF16)
            for yy, core in turn:

                @pl.when((yy != y) | (core != c))
                def _():
                    gy_copy(yy, core).start()

        gy_in[c * 2 * NYL + y] = gy_box[y * 2 + c]

        pltpu.make_async_remote_copy(
            src_ref=gtz_in.at[pl.ds(0, nz - 1)],
            dst_ref=gtz_in.at[pl.ds(0, nz - 1)],
            send_sem=gtz_send,
            recv_sem=gtz_recv,
            device_id=partner,
            device_id_type=MESH,
        ).wait()
        summed = jnp.sum(gtz_in[...].astype(F32), axis=0)
        for t in range(texts_here):
            for p in range(pieces):
                r = t * pieces + p
                grad_text[t : t + 1, p * LANES : (p + 1) * LANES] = summed[r : r + 1, :]

        pltpu.make_async_remote_copy(
            src_ref=gy_in.at[pl.ds(0, 4 * NYL - 1)],
            dst_ref=gy_in.at[pl.ds(0, 4 * NYL - 1)],
            send_sem=gy_send,
            recv_sem=gy_recv,
            device_id=partner,
            device_id_type=MESH,
        ).wait()
        for core in range(2):
            part = gy_in[core * 2 * NYL : (core + 1) * 2 * NYL].astype(F32)
            part = jnp.sum(part, axis=0)
            for k, chunk in enumerate(near_first(core)):
                row = pl.multiple_of(core * half + chunk * NG, NG)
                grad_image[pl.ds(row, NG), :] = part[k * NG : (k + 1) * NG, 0:HD]

        pltpu.make_async_remote_copy(
            src_ref=unit_in.at[pl.ds(0, plane - 1)],
            dst_ref=unit_in.at[pl.ds(0, plane - 1)],
            send_sem=unit_send,
            recv_sem=unit_recv.at[0],
            device_id=partner,
            device_id_type=MESH,
        ).wait_send()

        @pl.when(my_half == c)
        def _():
            pltpu.make_async_remote_copy(
                src_ref=outbox.at[pl.ds(0, dp_size - 1)],
                dst_ref=outbox.at[pl.ds(0, dp_size - 1)],
                send_sem=a2a_send,
                recv_sem=a2a_recv.at[0],
                device_id=partner,
                device_id_type=MESH,
            ).wait_send()

        @pl.when(my_half != c)
        def _():
            pltpu.make_async_remote_copy(
                src_ref=outbox,
                dst_ref=outbox,
                send_sem=a2a_send,
                recv_sem=a2a_recv.at[0],
                device_id=partner,
                device_id_type=MESH,
            ).wait_send()

        for k in range(images_here):
            pltpu.make_async_remote_copy(
                src_ref=feats.at[k, pl.ds(0, NG - 1)],
                dst_ref=feats.at[k, pl.ds(0, NG - 1)],
                send_sem=g_send.at[k],
                recv_sem=g_recv.at[k, 0],
                device_id=partner,
                device_id_type=MESH,
            ).wait_send()

    dma = pltpu.SemaphoreType.DMA
    scratch = [
        pltpu.VMEM((dp_size * dp_size // LANES, LANES), jnp.int32),
        pltpu.VMEM((dp_size * dp_size // LANES, LANES), jnp.int32),
        pltpu.VMEM((HD, dp_size * MAXP), BF16),
        pltpu.VMEM((3 * HD, width), BF16),
        pltpu.VMEM((HD, width), BF16),
        pltpu.VMEM((texts_here, width), BF16),
        dma((6,)),
        pltpu.VMEM((dp_size, MAXP, HD), BF16),
        pltpu.VMEM((2 * half, MAXP, HD), BF16),
        pltpu.VMEM((3 * HD, width), BF16),
        pltpu.VMEM((HD, width), BF16),
        pltpu.VMEM((images_here, NG, 2 * HD, LANES), BF16),
        pltpu.VMEM((half, LANES), jnp.int32),
        pltpu.VMEM((packed, LANES), F32),
        pltpu.VMEM((packed, LANES), BF16),
        pltpu.VMEM((2 * nz, packed, LANES), BF16),
        pltpu.VMEM((2 * nz * packed, LANES), F32),
        pltpu.VMEM((text_rows, width), F32),
        pltpu.VMEM((text_rows, NX * wide), F32),
        pltpu.VMEM((NG * packed, LANES), F32),
        pltpu.VMEM((NG, packed, LANES), BF16),
        pltpu.VMEM((NG, packed, LANES), BF16),
        pltpu.VMEM((packed, LANES), F32),
        pltpu.VMEM((plane, packed, LANES), BF16),
        pltpu.VMEM((plane * packed, LANES), F32),
        pltpu.VMEM((rows, width), F32),
        pltpu.VMEM((2, NX, rows // 2, wide), BF16),
        pltpu.VMEM((2, NX, rows // 2, wide), BF16),
        pltpu.VMEM((rows // 2, wide), F32),
        pltpu.VMEM((4 * NYL, half, LANES), BF16),
        pltpu.VMEM((4 * NYL, half, LANES), BF16),
        pltpu.VMEM((2 * nz * packed, LANES), F32),
        pltpu.VMEM((nz * packed, LANES), F32),
        pltpu.VMEM((nz, packed, LANES), BF16),
        pltpu.VMEM((nz, packed, LANES), BF16),
        dma,
        dma,
        dma((images_here,)),
        dma((2,)),
        dma((2,)),
        dma((images_here,)),
        dma((images_here, NG)),
        dma,
        dma,
        dma,
        dma,
        dma,
        dma,
        dma,
        dma((2 * NYL,)),
        dma((2,)),
        dma((2,)),
        dma,
        dma,
        dma,
        dma,
        dma,
        dma,
    ]
    return kernel, scratch


def on_device(patches, counts, dest, w_qkv, w_out, text):
    dp_size = lax.axis_size("dp")
    width = w_qkv.shape[2]
    texts_here = text.shape[0]
    kernel, scratch = make_kernel(dp_size, width, texts_here)
    vmem = pl.BlockSpec(memory_space=pltpu.VMEM)
    return pl.pallas_call(
        kernel,
        out_shape=(
            jax.ShapeDtypeStruct((dp_size, HD), F32),
            jax.ShapeDtypeStruct((texts_here, width), F32),
        ),
        in_specs=[pl.BlockSpec(memory_space=pltpu.HBM)] * 6,
        out_specs=(vmem, vmem),
        scratch_shapes=scratch,
        compiler_params=pltpu.CompilerParams(
            collective_id=0, has_side_effects=True, vmem_limit_bytes=40 * 1024 * 1024
        ),
    )(
        *(
            pltpu.with_memory_space_constraint(array, pltpu.HBM)
            for array in (
                counts.reshape(-1, LANES),
                dest.reshape(-1, LANES),
                patches,
                w_qkv.reshape(3 * HD, width),
                w_out,
                text,
            )
        )
    )


def solution(mesh):
    placed = (P("mp", "dp"), P(), P(), P(None, "mp", None), P("mp", None), P(("dp", "mp"), None))
    return jax.shard_map(
        on_device,
        mesh=mesh,
        in_specs=placed,
        out_specs=(P("dp", "mp"), P(("dp", "mp"), None)),
        check_vma=False,
    )
```

```python
import math

import jax
import jax.numpy as jnp
from jax import lax
from jax.experimental import pallas as pl
from jax.experimental.pallas import tpu as pltpu
from jax.sharding import PartitionSpec as P

HD = 72
MAXP = 16
NYL = 4
NYH = 2
NX = 4
NG = NYH * NX
LANES = 128
F32 = jnp.float32
BF16 = jnp.bfloat16
MESH = pl.DeviceIdType.MESH


def iota(shape, dim):
    return lax.broadcasted_iota(jnp.int32, shape, dim)


def dot_nn(a, b):
    return lax.dot_general(a, b, (((1,), (0,)), ((), ())), preferred_element_type=F32)


def dot_nt(a, b):
    return lax.dot_general(a, b, (((1,), (1,)), ((), ())), preferred_element_type=F32)


def wrap(value, size):
    return jnp.where(value >= size, value - size, value)


def make_kernel(dp_size, width, texts_here):
    nz = dp_size // NYL
    half = dp_size // 2
    images_here = half // NG
    pieces = width // LANES
    used = images_here * pieces
    packed = -(-used // 16) * 16
    slots = dp_size * MAXP
    half_slots = half * MAXP
    plane = NYL * NG
    rows = NYL * half
    text_rows = texts_here * 2 * nz
    wide = -(-(4 * HD) // LANES) * LANES

    def kernel(
        counts_in,
        dest_in,
        patches_in,
        w_qkv_in,
        w_out_in,
        text_arg,
        grad_image,
        grad_text,
        counts,
        dest,
        patches,
        w_qkv,
        w_out,
        text,
        in_sem,
        outbox,
        inbox,
        w_qkv_peer,
        w_out_peer,
        feats,
        qkv,
        text_f,
        text_box,
        text_in,
        text_wide,
        text_full,
        text_pad,
        part_f,
        part_b,
        part_in,
        mean_f,
        unit_in,
        unit_wide,
        unit_full,
        gi_box,
        gi_in,
        gi_sum,
        gy_box,
        gy_in,
        gt_f,
        gt_in,
        gt_box,
        gtz_in,
        local_sem,
        a2a_send,
        a2a_recv,
        w_send,
        w_recv,
        g_send,
        g_recv,
        text_send,
        text_recv,
        swap_send,
        swap_recv,
        part_send,
        part_recv,
        unit_send,
        unit_recv,
        gi_send,
        gi_recv,
        gy_send,
        gy_recv,
        gt_send,
        gt_recv,
        gtz_send,
        gtz_recv,
    ):
        me = lax.axis_index("dp")
        mp = lax.axis_index("mp")
        g, c = mp // 2, mp % 2
        z, ylo = me // NYL, me % NYL
        yhi, x = g // NX, g % NX
        y = yhi * NYL + ylo
        other = 1 - c
        partner = (me, g * 2 + other)
        my_half = me // half
        my_slot = me % half
        extra = jnp.where(my_half == c, 0, 1)

        loads = [
            pltpu.make_async_copy(src, dst, in_sem.at[i])
            for i, (src, dst) in enumerate(
                (
                    (dest_in, dest),
                    (counts_in, counts),
                    (patches_in, patches),
                    (w_qkv_in, w_qkv),
                    (w_out_in, w_out),
                    (text_arg, text),
                )
            )
        ]
        barrier = pltpu.get_barrier_semaphore()

        def greet(device):
            pl.semaphore_signal(barrier, inc=1, device_id=device, device_id_type=MESH)

        @pl.loop(0, half)
        def _(i):
            src = half * c + i
            greet((src, g * 2 + other))

            @pl.when(src != me)
            def _():
                greet((src, mp))

        greet(partner)

        for load in loads:
            load.start()

        @pl.loop(1, nz)
        def _(i):
            greet((wrap(z + i, nz) * NYL + ylo, mp))

        place = ylo * NG + g

        @pl.loop(1, 2 * NYL)
        def _(i):
            q = (y + i) % (2 * NYL)
            greet((z * NYL + q % NYL, ((q // NYL) * NX + x) * 2))
            greet((z * NYL + q % NYL, ((q // NYL) * NX + x) * 2 + 1))

        for i in range(1, NX):
            greet((me, (yhi * NX + (x + i) % NX) * 2 + c))
            greet((me, ((1 - yhi) * NX + (x + i) % NX) * 2 + c))

        for buffer in (text_f, text_pad, part_f, mean_f, gt_f, gy_box):
            buffer[...] = jnp.zeros_like(buffer)

        loads[0].wait()
        loads[1].wait()
        first = me * dp_size
        table_rows = dp_size * dp_size // LANES
        span = iota((dp_size, LANES), 1)
        order = iota((dp_size, LANES), 0)
        step = (order // NYL + 1) // 2
        target = wrap(z + nz // 2 + jnp.where(order // NYL % 2 == 1, nz - step, step), nz)
        target = wrap(target, nz) * NYL + (ylo + NYL - 1 - order % NYL) % NYL
        index = jnp.zeros((dp_size, 1), jnp.int32)
        base = first // LANES
        own_rows = []
        for r in range(2):
            row = jnp.minimum(base + r, table_rows - 1)
            image = (base + r) * LANES + span - first
            inside = (image >= 0) & (image < dp_size) & (base + r < table_rows)
            image = jnp.where(inside, image, dp_size)
            own_rows.append((image, counts[pl.ds(row, 1), :]))
            hit = inside & (dest[pl.ds(row, 1), :] == target)
            index = index + jnp.sum(jnp.where(hit, image, 0), axis=1, keepdims=True)
        start = jnp.zeros((dp_size, 1), jnp.int32)
        count = jnp.zeros((dp_size, 1), jnp.int32)
        for image, own in own_rows:
            start = start + jnp.sum(jnp.where(image < index, own, 0), axis=1, keepdims=True)
            count = count + jnp.sum(jnp.where(image == index, own, 0), axis=1, keepdims=True)
        position = iota((dp_size, MAXP, 1), 1)
        column = jnp.where(
            position < count.reshape(dp_size, 1, 1), start.reshape(dp_size, 1, 1) + position, -1
        ).reshape(slots, 1)
        loads[2].wait()

        def image_copy(at, d):
            return pltpu.make_async_remote_copy(
                src_ref=outbox.at[at],
                dst_ref=inbox.at[c * half + my_slot],
                send_sem=a2a_send,
                recv_sem=a2a_recv,
                device_id=(d, g * 2 + my_half),
                device_id_type=MESH,
            )

        total = (2 * half - 1 + extra) + 1 + (nz - 1) + 2 * (2 * NYL - 1) + 2 * (NX - 1)
        chosen = iota((slots, patches.shape[1]), 1) == column
        picked = dot_nt(chosen.astype(F32).astype(BF16), patches[...]).astype(BF16)
        outbox[...] = picked.reshape(dp_size, MAXP, HD)
        pl.semaphore_wait(barrier, total)

        @pl.loop(0, nz - 1)
        def _(j):
            step = (j + 1) // 2
            zz = wrap(z + nz // 2 + jnp.where(j % 2 == 1, nz - step, step), nz)
            zz = wrap(zz, nz)
            for i in range(NYL):
                d = zz * NYL + (ylo + NYL - 1 - i) % NYL
                image_copy(j * NYL + i, d).start()

        for i in range(NYL - 1):
            d = z * NYL + (ylo + NYL - 1 - i) % NYL
            image_copy((nz - 1) * NYL + i, d).start()

        own_copy = pltpu.make_async_copy(
            outbox.at[dp_size - 1], inbox.at[c * half + my_slot], local_sem
        )

        @pl.when(my_half == c)
        def _():
            own_copy.start()

        @pl.when(my_half != c)
        def _():
            image_copy(dp_size - 1, me).start()

        def swap(src, dst, i):
            return pltpu.make_async_remote_copy(
                src_ref=src,
                dst_ref=dst,
                send_sem=w_send.at[i],
                recv_sem=w_recv.at[i],
                device_id=partner,
                device_id_type=MESH,
            )

        swap_qkv = swap(w_qkv, w_qkv_peer, 0)
        swap_out = swap(w_out, w_out_peer, 1)
        loads[3].wait()
        swap_qkv.start()
        loads[4].wait()
        swap_out.start()

        loads[5].wait()
        text_float = text[...].astype(F32)
        text_unit = text_float * lax.rsqrt(
            jnp.sum(text_float * text_float, axis=1, keepdims=True) + 1e-6
        )
        for t in range(texts_here):
            for k in range(pieces):
                text_f[t * pieces + k : t * pieces + k + 1, :] = text_unit[
                    t : t + 1, k * LANES : (k + 1) * LANES
                ]
        own_text = text_f[...].astype(BF16)
        text_box[...] = own_text
        text_in[c * nz + z] = own_text

        def text_copy(zz):
            return pltpu.make_async_remote_copy(
                src_ref=text_box,
                dst_ref=text_in.at[c * nz + z],
                send_sem=text_send,
                recv_sem=text_recv,
                device_id=(zz * NYL + ylo, mp),
                device_id_type=MESH,
            )

        own_texts = text_in.at[pl.ds(c * nz, nz)]
        text_swap = pltpu.make_async_remote_copy(
            src_ref=own_texts,
            dst_ref=own_texts,
            send_sem=swap_send,
            recv_sem=swap_recv,
            device_id=partner,
            device_id_type=MESH,
        )

        got = jnp.zeros((half, LANES), jnp.int32)
        slot_row, slot_lane = iota((half, LANES), 0), iota((half, LANES), 1)
        half_rows = half * dp_size // LANES
        for r in range(half_rows):
            row = pl.ds(half_rows * c + r, 1)
            inside = (r * LANES + slot_lane) // dp_size == slot_row
            got = got + jnp.where(inside & (dest[row, :] == me), counts[row, :], 0)
        got = jnp.sum(got, axis=1, keepdims=True)

        @pl.when(my_half == c)
        def _():
            own_copy.wait()
            pltpu.make_async_remote_copy(
                src_ref=inbox.at[pl.ds(0, 2 * half - 1)],
                dst_ref=inbox.at[pl.ds(0, 2 * half - 1)],
                send_sem=a2a_send,
                recv_sem=a2a_recv,
                device_id=partner,
                device_id_type=MESH,
            ).wait_recv()

        @pl.when(my_half != c)
        def _():
            pltpu.make_async_remote_copy(
                src_ref=inbox,
                dst_ref=inbox,
                send_sem=a2a_send,
                recv_sem=a2a_recv,
                device_id=partner,
                device_id_type=MESH,
            ).wait_recv()

        eye = (iota((HD, HD), 0) == iota((HD, HD), 1)).astype(F32).astype(BF16)

        across = (1 - yhi) * NX + x
        left_x, right_x = lax.rem(x + NX - 1, NX), lax.rem(x + 1, NX)
        far_x = lax.rem(x + 2, NX)

        def feat_copy(k, owner, to):
            return pltpu.make_async_remote_copy(
                src_ref=feats.at[k, owner],
                dst_ref=feats.at[k, owner],
                send_sem=g_send.at[k],
                recv_sem=g_recv.at[k, owner],
                device_id=(me, to * 2 + c),
                device_id_type=MESH,
            )

        own_row, far_row = yhi * NX, (1 - yhi) * NX
        left, right = own_row + left_x, own_row + right_x
        for k in range(images_here):
            low, high = (
                dot_nt(eye, inbox[r + k * NG : r + (k + 1) * NG].reshape(LANES, HD))
                for r in (0, half)
            )
            feats[k, g] = jnp.concatenate([low, high], axis=0).astype(BF16)
            feat_copy(k, g, across).start()
            feat_copy(k, g, left).start()
            feat_copy(k, g, right).start()

        @pl.loop(1, nz)
        def _(i):
            text_copy(wrap(z + i, nz)).start()

        for k in range(images_here):
            feat_copy(k, left, left).wait_recv()
            if k % 2 == 0:
                feat_copy(k, left, right).start()
            feat_copy(k, right, left).wait_recv()
            if k % 2 == 1:
                feat_copy(k, right, left).start()
            feat_copy(k, across, across).wait_recv()
            feat_copy(k, across, own_row + far_x).start()
            feat_copy(k, across, left).start()
            feat_copy(k, across, right).start()

        swap_qkv.wait()
        swap_out.wait()

        for k in range(images_here):
            feat_copy(k, own_row + far_x, left).wait_recv()
            for xx in (left_x, right_x, far_x):
                feat_copy(k, far_row + xx, left).wait_recv()
            full = feats[k].reshape(width, LANES).astype(F32)
            centred = full - jnp.sum(full, axis=0, keepdims=True) / width
            variance = jnp.sum(centred * centred, axis=0, keepdims=True) / width
            normed = (centred * lax.rsqrt(variance + 1e-6)).astype(BF16)
            qkv[k, 0] = dot_nn(w_qkv[...], normed)
            qkv[k, 1] = dot_nn(w_qkv_peer[...], normed)
        pltpu.make_async_remote_copy(
            src_ref=text_in.at[pl.ds(0, nz - 1)],
            dst_ref=text_in.at[pl.ds(0, nz - 1)],
            send_sem=text_send,
            recv_sem=text_recv,
            device_id=partner,
            device_id_type=MESH,
        ).wait()
        text_swap.start()
        row8, lane8 = iota((NG, LANES), 0), iota((NG, LANES), 1)
        same = iota((LANES, LANES), 0) // MAXP == iota((LANES, LANES), 1) // MAXP
        heads = ([], [])
        for k in range(images_here):
            got_k = got[k * NG : (k + 1) * NG]
            got_float = got_k.astype(F32)
            real = (lane8 // MAXP == row8) & (lane8 % MAXP < got_k)
            member = real.astype(F32).astype(BF16)
            key_count = jnp.broadcast_to(got_k.reshape(NG, 1, 1), (NG, MAXP, 1))
            key_count = key_count.reshape(LANES, 1)
            keep = same & (iota((LANES, 1), 0) % MAXP < key_count)
            for h in range(2):
                query = qkv[k, h, 0:HD].astype(BF16)
                key = jnp.transpose(qkv[k, h, HD : 2 * HD]).astype(BF16)
                value = qkv[k, h, 2 * HD : 3 * HD].astype(BF16)
                scores = dot_nn(key, query) * (1.0 / math.sqrt(HD))
                scores = jnp.where(keep, scores, -1e30)
                raised = jnp.exp(scores - jnp.max(scores, axis=0, keepdims=True))
                mixed = dot_nn(value, raised.astype(BF16))
                mixed = (mixed / jnp.sum(raised, axis=0, keepdims=True)).astype(BF16)
                heads[h].append(dot_nt(member, mixed) / got_float)
        term = jnp.zeros((half, width), F32)
        for pooled, wo in zip(heads, (w_out, w_out_peer)):
            term = term + dot_nn(jnp.concatenate(pooled, axis=0).astype(BF16), wo[...])
        for k in range(images_here):
            for p in range(pieces):
                part_f[pl.ds(k * pieces + p, NG, stride=packed), :] = term[
                    k * NG : (k + 1) * NG, p * LANES : (p + 1) * LANES
                ]

        part_b[...] = part_f[...].astype(BF16).reshape(NG, packed, LANES)

        def part_copy(gg):
            return pltpu.make_async_remote_copy(
                src_ref=part_b.at[gg],
                dst_ref=part_in.at[g],
                send_sem=part_send,
                recv_sem=part_recv,
                device_id=(me, gg * 2 + c),
                device_id_type=MESH,
            )

        for row in (1 - yhi, yhi):
            for i in (2, 1, 3):
                part_copy(row * NX + (x + i) % NX).start()
        part_copy(across).start()

        part_in[g] = part_b[g]

        here = (lane8 // MAXP == g).astype(F32).astype(BF16)
        for k in range(images_here):
            own_got = jnp.sum(
                jnp.where(iota((NG, 1), 0) == g, got[k * NG : (k + 1) * NG], 0),
                axis=0,
                keepdims=True,
            ).astype(F32)
            mean = dot_nt(here, feats[k].reshape(width, LANES)) / own_got
            for p in range(pieces):
                r = k * pieces + p
                mean_f[r : r + 1, :] = mean[0:1, p * LANES : (p + 1) * LANES]

        text_swap.wait()
        text_wide[...] = text_in[...].astype(F32).reshape(2 * nz * packed, LANES)
        for t in range(texts_here):
            for p in range(pieces):
                text_full[t * 2 * nz : (t + 1) * 2 * nz, p * LANES : (p + 1) * LANES] = (
                    text_wide[pl.ds(t * pieces + p, 2 * nz, stride=packed), :]
                )
        for xx in range(NX):
            for q in range(4):
                m = ((q // 2) * NX + xx) * 2 + q % 2
                text_pad[:, xx * wide + q * HD : xx * wide + (q + 1) * HD] = text_full[
                    :, m * HD : (m + 1) * HD
                ]
        text_rows_b = text_full[...].astype(BF16)
        text_cols_b = text_pad[...].astype(BF16)

        part_seven = pltpu.make_async_remote_copy(
            src_ref=part_in.at[pl.ds(0, NG - 1)],
            dst_ref=part_in.at[pl.ds(0, NG - 1)],
            send_sem=part_send,
            recv_sem=part_recv,
            device_id=partner,
            device_id_type=MESH,
        )
        part_seven.wait()
        pooled = jnp.sum(part_in[...].astype(F32), axis=0) + mean_f[...]
        squares = jnp.sum(pooled * pooled, axis=1, keepdims=True)
        row_id = iota((packed, 1), 0)
        scale = jnp.zeros((packed, 1), F32)
        for k in range(images_here):
            inside = (row_id >= k * pieces) & (row_id < (k + 1) * pieces)
            norm = jnp.sum(jnp.where(inside, squares, 0.0), axis=0, keepdims=True)
            scale = jnp.where(inside, lax.rsqrt(norm + 1e-6), scale)
        own_unit = (pooled * scale).astype(BF16)
        unit_in[place] = own_unit

        def unit_y(step, at):
            q = (y + step) % (2 * NYL)
            return pltpu.make_async_remote_copy(
                src_ref=unit_in.at[at],
                dst_ref=unit_in.at[at],
                send_sem=unit_send,
                recv_sem=unit_recv.at[step],
                device_id=(z * NYL + q % NYL, ((q // NYL) * NX + x) * 2 + c),
                device_id_type=MESH,
            )

        def unit_x(at):
            for i in (2, 1, 3):
                pltpu.make_async_remote_copy(
                    src_ref=unit_in.at[at],
                    dst_ref=unit_in.at[at],
                    send_sem=unit_send,
                    recv_sem=unit_recv.at[0],
                    device_id=(me, (yhi * NX + (x + i) % NX) * 2 + c),
                    device_id_type=MESH,
                ).start()

        for step in (4, 3, 5, 2, 6, 1, 7):
            unit_y(step, place).start()
        unit_x(place)

        text_row = iota((text_rows, 1), 0)
        text_source = (text_row % nz) * NYL + ylo
        text_core = (text_row % (2 * nz)) // nz
        pair_at = text_source * dp_size + (g * 2 + text_core) * texts_here + text_row // (2 * nz)
        pair_lane = iota((text_rows, LANES), 1)
        pair_dest = jnp.zeros((text_rows, LANES), jnp.int32)
        for r in range(table_rows):
            pair_dest = pair_dest + jnp.where(
                pair_at == r * LANES + pair_lane, dest[r : r + 1, :], 0
            )
        pair_dest = jnp.sum(pair_dest, axis=1, keepdims=True)
        image_lane = iota((text_rows, rows), 1)
        image_source = c * half + image_lane % half
        image_dest = z * NYL + image_lane // half
        paired = (image_source == text_source) & (image_dest == pair_dest)
        labels = jnp.where(paired, 1.0, -1.0)

        for step in (1, 7, 2, 6, 3, 5, 4):
            q = (y + 2 * NYL - step) % (2 * NYL)
            at = (q % NYL) * NG + (q // NYL) * NX + x
            unit_y(step, at).wait_recv()
            unit_x(at)
        pltpu.make_async_remote_copy(
            src_ref=unit_in.at[pl.ds(0, plane - 2 * NYL)],
            dst_ref=unit_in.at[pl.ds(0, plane - 2 * NYL)],
            send_sem=unit_send,
            recv_sem=unit_recv.at[0],
            device_id=partner,
            device_id_type=MESH,
        ).wait_recv()
        unit_wide[...] = unit_in[...].astype(F32).reshape(plane * packed, LANES)
        for yy in range(NYL):
            for k in range(images_here):
                for p in range(pieces):
                    unit_full[
                        yy * half + k * NG : yy * half + (k + 1) * NG,
                        p * LANES : (p + 1) * LANES,
                    ] = unit_wide[
                        pl.ds(yy * NG * packed + k * pieces + p, NG, stride=packed), :
                    ]
        units = unit_full[...].astype(BF16)

        logits = 4.0 * dot_nt(text_rows_b, units) - 2.0
        dscaled = -4.0 * labels / (1.0 + jnp.exp(labels * logits))
        turned = jnp.transpose(dscaled).astype(BF16)
        dscaled = dscaled.astype(BF16)

        def gi_copy(n, xx):
            return pltpu.make_async_remote_copy(
                src_ref=gi_box.at[n, xx],
                dst_ref=gi_in.at[n, x],
                send_sem=gi_send.at[n],
                recv_sem=gi_recv.at[n],
                device_id=(me, (yhi * NX + xx) * 2 + c),
                device_id_type=MESH,
            )

        pair_rows = 2 * half
        for n in range(2):
            for xx in range(NX):
                gi_box[n, xx] = dot_nn(
                    turned[n * pair_rows : (n + 1) * pair_rows],
                    text_cols_b[:, xx * wide : (xx + 1) * wide],
                ).astype(BF16)
            for i in (2, 1, 3):
                gi_copy(n, (x + i) % NX).start()
            gi_in[n, x] = gi_box[n, x]

        text_grad = dot_nn(dscaled, units)
        for t in range(texts_here):
            for p in range(pieces):
                gt_f[pl.ds(t * pieces + p, 2 * nz, stride=packed), :] = text_grad[
                    t * 2 * nz : (t + 1) * 2 * nz, p * LANES : (p + 1) * LANES
                ]
        core_rows = nz * packed
        gt_copy = pltpu.make_async_remote_copy(
            src_ref=gt_f.at[pl.ds(pl.multiple_of(other * core_rows, 8), core_rows)],
            dst_ref=gt_in,
            send_sem=gt_send,
            recv_sem=gt_recv,
            device_id=partner,
            device_id_type=MESH,
        )
        gt_copy.start()

        gt_copy.wait()
        own_sums = gt_f[pl.ds(pl.multiple_of(c * core_rows, 8), core_rows), :]
        gt_box[...] = (own_sums + gt_in[...]).astype(BF16).reshape(nz, packed, LANES)

        def gtz_copy(zz):
            return pltpu.make_async_remote_copy(
                src_ref=gt_box.at[zz],
                dst_ref=gtz_in.at[z],
                send_sem=gtz_send,
                recv_sem=gtz_recv,
                device_id=(zz * NYL + ylo, mp),
                device_id_type=MESH,
            )

        for i in sorted(range(1, nz), key=lambda step: -min(step, nz - step)):
            gtz_copy(wrap(z + i, nz)).start()

        gtz_in[z] = gt_box[z]

        def gy_copy(yy, core):
            return pltpu.make_async_remote_copy(
                src_ref=gy_box.at[yy * 2 + core],
                dst_ref=gy_in.at[c * 2 * NYL + y],
                send_sem=gy_send,
                recv_sem=gy_recv,
                device_id=(z * NYL + yy % NYL, ((yy // NYL) * NX + x) * 2 + core),
                device_id_type=MESH,
            )

        for n in range(2):
            pltpu.make_async_remote_copy(
                src_ref=gi_in.at[n, pl.ds(0, NX - 1)],
                dst_ref=gi_in.at[n, pl.ds(0, NX - 1)],
                send_sem=gi_send.at[n],
                recv_sem=gi_recv.at[n],
                device_id=partner,
                device_id_type=MESH,
            ).wait()
            gi_sum[...] = jnp.sum(gi_in[n].astype(F32), axis=0)
            turn = [(row * NYL + 2 * n + r, core) for row in (0, 1) for r in (0, 1) for core in (0, 1)]
            for yy, core in turn:
                q = (yy // NYL) * 2 + core
                r = (yy % 2) * half
                gy_box[yy * 2 + core, :, 0:HD] = gi_sum[
                    r : r + half, q * HD : (q + 1) * HD
                ].astype(BF16)
            for yy, core in turn:

                @pl.when((yy != y) | (core != c))
                def _():
                    gy_copy(yy, core).start()

        gy_in[c * 2 * NYL + y] = gy_box[y * 2 + c]

        pltpu.make_async_remote_copy(
            src_ref=gtz_in.at[pl.ds(0, nz - 1)],
            dst_ref=gtz_in.at[pl.ds(0, nz - 1)],
            send_sem=gtz_send,
            recv_sem=gtz_recv,
            device_id=partner,
            device_id_type=MESH,
        ).wait()
        summed = jnp.sum(gtz_in[...].astype(F32), axis=0)
        for t in range(texts_here):
            for p in range(pieces):
                r = t * pieces + p
                grad_text[t : t + 1, p * LANES : (p + 1) * LANES] = summed[r : r + 1, :]

        pltpu.make_async_remote_copy(
            src_ref=gy_in.at[pl.ds(0, 4 * NYL - 1)],
            dst_ref=gy_in.at[pl.ds(0, 4 * NYL - 1)],
            send_sem=gy_send,
            recv_sem=gy_recv,
            device_id=partner,
            device_id_type=MESH,
        ).wait()
        for core in range(2):
            part = gy_in[core * 2 * NYL : (core + 1) * 2 * NYL].astype(F32)
            grad_image[core * half : (core + 1) * half, :] = jnp.sum(part, axis=0)[:, 0:HD]

        pltpu.make_async_remote_copy(
            src_ref=unit_in.at[pl.ds(0, plane - 1)],
            dst_ref=unit_in.at[pl.ds(0, plane - 1)],
            send_sem=unit_send,
            recv_sem=unit_recv.at[0],
            device_id=partner,
            device_id_type=MESH,
        ).wait_send()

        @pl.when(my_half == c)
        def _():
            pltpu.make_async_remote_copy(
                src_ref=outbox.at[pl.ds(0, dp_size - 1)],
                dst_ref=outbox.at[pl.ds(0, dp_size - 1)],
                send_sem=a2a_send,
                recv_sem=a2a_recv,
                device_id=partner,
                device_id_type=MESH,
            ).wait_send()

        @pl.when(my_half != c)
        def _():
            pltpu.make_async_remote_copy(
                src_ref=outbox,
                dst_ref=outbox,
                send_sem=a2a_send,
                recv_sem=a2a_recv,
                device_id=partner,
                device_id_type=MESH,
            ).wait_send()

        for k in range(images_here):
            pltpu.make_async_remote_copy(
                src_ref=feats.at[k, pl.ds(0, NG - 1)],
                dst_ref=feats.at[k, pl.ds(0, NG - 1)],
                send_sem=g_send.at[k],
                recv_sem=g_recv.at[k, 0],
                device_id=partner,
                device_id_type=MESH,
            ).wait_send()

    dma = pltpu.SemaphoreType.DMA
    scratch = [
        pltpu.VMEM((dp_size * dp_size // LANES, LANES), jnp.int32),
        pltpu.VMEM((dp_size * dp_size // LANES, LANES), jnp.int32),
        pltpu.VMEM((HD, dp_size * MAXP), BF16),
        pltpu.VMEM((3 * HD, width), BF16),
        pltpu.VMEM((HD, width), BF16),
        pltpu.VMEM((texts_here, width), BF16),
        dma((6,)),
        pltpu.VMEM((dp_size, MAXP, HD), BF16),
        pltpu.VMEM((2 * half, MAXP, HD), BF16),
        pltpu.VMEM((3 * HD, width), BF16),
        pltpu.VMEM((HD, width), BF16),
        pltpu.VMEM((images_here, NG, 2 * HD, LANES), BF16),
        pltpu.VMEM((images_here, 2, 3 * HD, LANES), F32),
        pltpu.VMEM((packed, LANES), F32),
        pltpu.VMEM((packed, LANES), BF16),
        pltpu.VMEM((2 * nz, packed, LANES), BF16),
        pltpu.VMEM((2 * nz * packed, LANES), F32),
        pltpu.VMEM((text_rows, width), F32),
        pltpu.VMEM((text_rows, NX * wide), F32),
        pltpu.VMEM((NG * packed, LANES), F32),
        pltpu.VMEM((NG, packed, LANES), BF16),
        pltpu.VMEM((NG, packed, LANES), BF16),
        pltpu.VMEM((packed, LANES), F32),
        pltpu.VMEM((plane, packed, LANES), BF16),
        pltpu.VMEM((plane * packed, LANES), F32),
        pltpu.VMEM((rows, width), F32),
        pltpu.VMEM((2, NX, rows // 2, wide), BF16),
        pltpu.VMEM((2, NX, rows // 2, wide), BF16),
        pltpu.VMEM((rows // 2, wide), F32),
        pltpu.VMEM((4 * NYL, half, LANES), BF16),
        pltpu.VMEM((4 * NYL, half, LANES), BF16),
        pltpu.VMEM((2 * nz * packed, LANES), F32),
        pltpu.VMEM((nz * packed, LANES), F32),
        pltpu.VMEM((nz, packed, LANES), BF16),
        pltpu.VMEM((nz, packed, LANES), BF16),
        dma,
        dma,
        dma,
        dma((2,)),
        dma((2,)),
        dma((images_here,)),
        dma((images_here, NG)),
        dma,
        dma,
        dma,
        dma,
        dma,
        dma,
        dma,
        dma((2 * NYL,)),
        dma((2,)),
        dma((2,)),
        dma,
        dma,
        dma,
        dma,
        dma,
        dma,
    ]
    return kernel, scratch


def on_device(patches, counts, dest, w_qkv, w_out, text):
    dp_size = lax.axis_size("dp")
    width = w_qkv.shape[2]
    texts_here = text.shape[0]
    kernel, scratch = make_kernel(dp_size, width, texts_here)
    vmem = pl.BlockSpec(memory_space=pltpu.VMEM)
    return pl.pallas_call(
        kernel,
        out_shape=(
            jax.ShapeDtypeStruct((dp_size, HD), F32),
            jax.ShapeDtypeStruct((texts_here, width), F32),
        ),
        in_specs=[pl.BlockSpec(memory_space=pltpu.HBM)] * 6,
        out_specs=(vmem, vmem),
        scratch_shapes=scratch,
        compiler_params=pltpu.CompilerParams(
            collective_id=0, has_side_effects=True, vmem_limit_bytes=40 * 1024 * 1024
        ),
    )(
        *(
            pltpu.with_memory_space_constraint(array, pltpu.HBM)
            for array in (
                counts.reshape(-1, LANES),
                dest.reshape(-1, LANES),
                patches,
                w_qkv.reshape(3 * HD, width),
                w_out,
                text,
            )
        )
    )


def solution(mesh):
    placed = (P("mp", "dp"), P(), P(), P(None, "mp", None), P("mp", None), P(("dp", "mp"), None))
    return jax.shard_map(
        on_device,
        mesh=mesh,
        in_specs=placed,
        out_specs=(P("dp", "mp"), P(("dp", "mp"), None)),
        check_vma=False,
    )
```

```python
import math

import jax
import jax.numpy as jnp
from jax import lax
from jax.experimental import pallas as pl
from jax.experimental.pallas import tpu as pltpu
from jax.sharding import PartitionSpec as P

HD = 72
MAXP = 16
NYL = 4
NYH = 2
NX = 4
NG = NYH * NX
LANES = 128
F32 = jnp.float32
BF16 = jnp.bfloat16
MESH = pl.DeviceIdType.MESH


def iota(shape, dim):
    return lax.broadcasted_iota(jnp.int32, shape, dim)


def dot_nn(a, b):
    return lax.dot_general(a, b, (((1,), (0,)), ((), ())), preferred_element_type=F32)


def dot_nt(a, b):
    return lax.dot_general(a, b, (((1,), (1,)), ((), ())), preferred_element_type=F32)


def wrap(value, size):
    return jnp.where(value >= size, value - size, value)


def make_kernel(dp_size, width, texts_here):
    nz = dp_size // NYL
    half = dp_size // 2
    images_here = half // NG
    pieces = width // LANES
    used = images_here * pieces
    packed = -(-used // 16) * 16
    slots = dp_size * MAXP
    half_slots = half * MAXP
    plane = NYL * NG
    rows = NYL * half
    text_rows = texts_here * 2 * nz
    wide = -(-(4 * HD) // LANES) * LANES

    def kernel(
        counts_in,
        dest_in,
        patches_in,
        w_qkv_in,
        w_out_in,
        text_arg,
        grad_image,
        grad_text,
        counts,
        dest,
        patches,
        w_qkv,
        w_out,
        text,
        in_sem,
        outbox,
        inbox,
        w_qkv_peer,
        w_out_peer,
        feats,
        qkv,
        text_f,
        text_box,
        text_in,
        text_wide,
        text_full,
        text_pad,
        part_f,
        part_b,
        part_in,
        mean_f,
        unit_in,
        unit_wide,
        unit_full,
        gi_box,
        gi_in,
        gi_sum,
        gy_box,
        gy_in,
        gt_f,
        gt_in,
        gt_box,
        gtz_in,
        local_sem,
        a2a_send,
        a2a_recv,
        w_send,
        w_recv,
        g_send,
        g_recv,
        text_send,
        text_recv,
        swap_send,
        swap_recv,
        part_send,
        part_recv,
        unit_send,
        unit_recv,
        gi_send,
        gi_recv,
        gy_send,
        gy_recv,
        gt_send,
        gt_recv,
        gtz_send,
        gtz_recv,
    ):
        me = lax.axis_index("dp")
        mp = lax.axis_index("mp")
        g, c = mp // 2, mp % 2
        z, ylo = me // NYL, me % NYL
        yhi, x = g // NX, g % NX
        y = yhi * NYL + ylo
        other = 1 - c
        partner = (me, g * 2 + other)
        my_half = me // half
        my_slot = me % half
        extra = jnp.where(my_half == c, 0, 1)

        loads = [
            pltpu.make_async_copy(src, dst, in_sem.at[i])
            for i, (src, dst) in enumerate(
                (
                    (dest_in, dest),
                    (counts_in, counts),
                    (patches_in, patches),
                    (w_qkv_in, w_qkv),
                    (w_out_in, w_out),
                    (text_arg, text),
                )
            )
        ]
        for load in loads:
            load.start()

        barrier = pltpu.get_barrier_semaphore()

        def greet(device):
            pl.semaphore_signal(barrier, inc=1, device_id=device, device_id_type=MESH)

        @pl.loop(0, half)
        def _(i):
            src = half * c + i
            greet((src, g * 2 + other))

            @pl.when(src != me)
            def _():
                greet((src, mp))

        greet(partner)

        @pl.loop(1, nz)
        def _(i):
            greet((wrap(z + i, nz) * NYL + ylo, mp))

        place = ylo * NG + g

        @pl.loop(1, 2 * NYL)
        def _(i):
            q = (y + i) % (2 * NYL)
            greet((z * NYL + q % NYL, ((q // NYL) * NX + x) * 2))
            greet((z * NYL + q % NYL, ((q // NYL) * NX + x) * 2 + 1))

        for i in range(1, NX):
            greet((me, (yhi * NX + (x + i) % NX) * 2 + c))
            greet((me, ((1 - yhi) * NX + (x + i) % NX) * 2 + c))

        for buffer in (text_f, text_pad, part_f, mean_f, gt_f, gy_box):
            buffer[...] = jnp.zeros_like(buffer)

        loads[0].wait()
        loads[1].wait()
        first = me * dp_size
        table_rows = dp_size * dp_size // LANES
        span = iota((dp_size, LANES), 1)
        order = iota((dp_size, LANES), 0)
        step = (order // NYL + 1) // 2
        target = wrap(z + nz // 2 + jnp.where(order // NYL % 2 == 1, nz - step, step), nz)
        target = wrap(target, nz) * NYL + (ylo + NYL - 1 - order % NYL) % NYL
        index = jnp.zeros((dp_size, 1), jnp.int32)
        base = first // LANES
        own_rows = []
        for r in range(2):
            row = jnp.minimum(base + r, table_rows - 1)
            image = (base + r) * LANES + span - first
            inside = (image >= 0) & (image < dp_size) & (base + r < table_rows)
            image = jnp.where(inside, image, dp_size)
            own_rows.append((image, counts[pl.ds(row, 1), :]))
            hit = inside & (dest[pl.ds(row, 1), :] == target)
            index = index + jnp.sum(jnp.where(hit, image, 0), axis=1, keepdims=True)
        start = jnp.zeros((dp_size, 1), jnp.int32)
        count = jnp.zeros((dp_size, 1), jnp.int32)
        for image, own in own_rows:
            start = start + jnp.sum(jnp.where(image < index, own, 0), axis=1, keepdims=True)
            count = count + jnp.sum(jnp.where(image == index, own, 0), axis=1, keepdims=True)
        position = iota((dp_size, MAXP, 1), 1)
        column = jnp.where(
            position < count.reshape(dp_size, 1, 1), start.reshape(dp_size, 1, 1) + position, -1
        ).reshape(slots, 1)
        loads[2].wait()

        def image_copy(at, d):
            return pltpu.make_async_remote_copy(
                src_ref=outbox.at[at],
                dst_ref=inbox.at[c * half + my_slot],
                send_sem=a2a_send,
                recv_sem=a2a_recv,
                device_id=(d, g * 2 + my_half),
                device_id_type=MESH,
            )

        total = (2 * half - 1 + extra) + 1 + (nz - 1) + 2 * (2 * NYL - 1) + 2 * (NX - 1)
        blocks = 4
        block_rows = slots // blocks
        block_images = dp_size // blocks
        block_z = nz // blocks
        for n in range(blocks):
            chosen = iota((block_rows, patches.shape[1]), 1) == column[
                n * block_rows : (n + 1) * block_rows
            ]
            picked = dot_nt(chosen.astype(F32).astype(BF16), patches[...]).astype(BF16)
            outbox[n * block_images : (n + 1) * block_images] = picked.reshape(
                block_images, MAXP, HD
            )
            if n == 0:
                pl.semaphore_wait(barrier, total)
            last = n == blocks - 1

            @pl.loop(n * block_z, (n + 1) * block_z - (1 if last else 0))
            def _(j):
                step = (j + 1) // 2
                zz = wrap(z + nz // 2 + jnp.where(j % 2 == 1, nz - step, step), nz)
                zz = wrap(zz, nz)
                for i in range(NYL):
                    d = zz * NYL + (ylo + NYL - 1 - i) % NYL
                    image_copy(j * NYL + i, d).start()

            if last:
                for i in range(NYL - 1):
                    d = z * NYL + (ylo + NYL - 1 - i) % NYL
                    image_copy((nz - 1) * NYL + i, d).start()

        own_copy = pltpu.make_async_copy(
            outbox.at[dp_size - 1], inbox.at[c * half + my_slot], local_sem
        )

        @pl.when(my_half == c)
        def _():
            own_copy.start()

        @pl.when(my_half != c)
        def _():
            image_copy(dp_size - 1, me).start()

        def swap(src, dst, i):
            return pltpu.make_async_remote_copy(
                src_ref=src,
                dst_ref=dst,
                send_sem=w_send.at[i],
                recv_sem=w_recv.at[i],
                device_id=partner,
                device_id_type=MESH,
            )

        swap_qkv = swap(w_qkv, w_qkv_peer, 0)
        swap_out = swap(w_out, w_out_peer, 1)
        loads[3].wait()
        swap_qkv.start()
        loads[4].wait()
        swap_out.start()

        loads[5].wait()
        text_float = text[...].astype(F32)
        text_unit = text_float * lax.rsqrt(
            jnp.sum(text_float * text_float, axis=1, keepdims=True) + 1e-6
        )
        for t in range(texts_here):
            for k in range(pieces):
                text_f[t * pieces + k : t * pieces + k + 1, :] = text_unit[
                    t : t + 1, k * LANES : (k + 1) * LANES
                ]
        own_text = text_f[...].astype(BF16)
        text_box[...] = own_text
        text_in[c * nz + z] = own_text

        def text_copy(zz):
            return pltpu.make_async_remote_copy(
                src_ref=text_box,
                dst_ref=text_in.at[c * nz + z],
                send_sem=text_send,
                recv_sem=text_recv,
                device_id=(zz * NYL + ylo, mp),
                device_id_type=MESH,
            )

        own_texts = text_in.at[pl.ds(c * nz, nz)]
        text_swap = pltpu.make_async_remote_copy(
            src_ref=own_texts,
            dst_ref=own_texts,
            send_sem=swap_send,
            recv_sem=swap_recv,
            device_id=partner,
            device_id_type=MESH,
        )

        got = jnp.zeros((half, LANES), jnp.int32)
        slot_row, slot_lane = iota((half, LANES), 0), iota((half, LANES), 1)
        half_rows = half * dp_size // LANES
        for r in range(half_rows):
            row = pl.ds(half_rows * c + r, 1)
            inside = (r * LANES + slot_lane) // dp_size == slot_row
            got = got + jnp.where(inside & (dest[row, :] == me), counts[row, :], 0)
        got = jnp.sum(got, axis=1, keepdims=True)

        @pl.when(my_half == c)
        def _():
            own_copy.wait()
            pltpu.make_async_remote_copy(
                src_ref=inbox.at[pl.ds(0, 2 * half - 1)],
                dst_ref=inbox.at[pl.ds(0, 2 * half - 1)],
                send_sem=a2a_send,
                recv_sem=a2a_recv,
                device_id=partner,
                device_id_type=MESH,
            ).wait_recv()

        @pl.when(my_half != c)
        def _():
            pltpu.make_async_remote_copy(
                src_ref=inbox,
                dst_ref=inbox,
                send_sem=a2a_send,
                recv_sem=a2a_recv,
                device_id=partner,
                device_id_type=MESH,
            ).wait_recv()

        eye = (iota((HD, HD), 0) == iota((HD, HD), 1)).astype(F32).astype(BF16)

        across = (1 - yhi) * NX + x
        left_x, right_x = lax.rem(x + NX - 1, NX), lax.rem(x + 1, NX)
        far_x = lax.rem(x + 2, NX)

        def feat_copy(k, owner, to):
            return pltpu.make_async_remote_copy(
                src_ref=feats.at[k, owner],
                dst_ref=feats.at[k, owner],
                send_sem=g_send.at[k],
                recv_sem=g_recv.at[k, owner],
                device_id=(me, to * 2 + c),
                device_id_type=MESH,
            )

        own_row, far_row = yhi * NX, (1 - yhi) * NX
        left, right = own_row + left_x, own_row + right_x
        for k in range(images_here):
            low, high = (
                dot_nt(eye, inbox[r + k * NG : r + (k + 1) * NG].reshape(LANES, HD))
                for r in (0, half)
            )
            feats[k, g] = jnp.concatenate([low, high], axis=0).astype(BF16)
            feat_copy(k, g, across).start()
            feat_copy(k, g, left).start()
            feat_copy(k, g, right).start()

        @pl.loop(1, nz)
        def _(i):
            text_copy(wrap(z + i, nz)).start()

        for k in range(images_here):
            feat_copy(k, left, left).wait_recv()
            if k % 2 == 0:
                feat_copy(k, left, right).start()
            feat_copy(k, right, left).wait_recv()
            if k % 2 == 1:
                feat_copy(k, right, left).start()
            feat_copy(k, across, across).wait_recv()
            feat_copy(k, across, own_row + far_x).start()
            feat_copy(k, across, left).start()
            feat_copy(k, across, right).start()

        swap_qkv.wait()
        swap_out.wait()

        for k in range(images_here):
            feat_copy(k, own_row + far_x, left).wait_recv()
            for xx in (left_x, right_x, far_x):
                feat_copy(k, far_row + xx, left).wait_recv()
            full = feats[k].reshape(width, LANES).astype(F32)
            centred = full - jnp.sum(full, axis=0, keepdims=True) / width
            variance = jnp.sum(centred * centred, axis=0, keepdims=True) / width
            normed = (centred * lax.rsqrt(variance + 1e-6)).astype(BF16)
            qkv[k, 0] = dot_nn(w_qkv[...], normed)
            qkv[k, 1] = dot_nn(w_qkv_peer[...], normed)
        pltpu.make_async_remote_copy(
            src_ref=text_in.at[pl.ds(0, nz - 1)],
            dst_ref=text_in.at[pl.ds(0, nz - 1)],
            send_sem=text_send,
            recv_sem=text_recv,
            device_id=partner,
            device_id_type=MESH,
        ).wait()
        text_swap.start()
        row8, lane8 = iota((NG, LANES), 0), iota((NG, LANES), 1)
        same = iota((LANES, LANES), 0) // MAXP == iota((LANES, LANES), 1) // MAXP
        heads = ([], [])
        for k in range(images_here):
            got_k = got[k * NG : (k + 1) * NG]
            got_float = got_k.astype(F32)
            real = (lane8 // MAXP == row8) & (lane8 % MAXP < got_k)
            member = real.astype(F32).astype(BF16)
            key_count = jnp.broadcast_to(got_k.reshape(NG, 1, 1), (NG, MAXP, 1))
            key_count = key_count.reshape(LANES, 1)
            keep = same & (iota((LANES, 1), 0) % MAXP < key_count)
            for h in range(2):
                query = qkv[k, h, 0:HD].astype(BF16)
                key = jnp.transpose(qkv[k, h, HD : 2 * HD]).astype(BF16)
                value = qkv[k, h, 2 * HD : 3 * HD].astype(BF16)
                scores = dot_nn(key, query) / math.sqrt(HD)
                scores = jnp.where(keep, scores, -1e30)
                raised = jnp.exp(scores - jnp.max(scores, axis=0, keepdims=True))
                weights = (raised / jnp.sum(raised, axis=0, keepdims=True)).astype(BF16)
                mixed = dot_nn(value, weights).astype(BF16)
                heads[h].append(dot_nt(member, mixed) / got_float)
        term = jnp.zeros((half, width), F32)
        for pooled, wo in zip(heads, (w_out, w_out_peer)):
            term = term + dot_nn(jnp.concatenate(pooled, axis=0).astype(BF16), wo[...])
        for k in range(images_here):
            for p in range(pieces):
                part_f[pl.ds(k * pieces + p, NG, stride=packed), :] = term[
                    k * NG : (k + 1) * NG, p * LANES : (p + 1) * LANES
                ]

        part_b[...] = part_f[...].astype(BF16).reshape(NG, packed, LANES)

        def part_copy(gg):
            return pltpu.make_async_remote_copy(
                src_ref=part_b.at[gg],
                dst_ref=part_in.at[g],
                send_sem=part_send,
                recv_sem=part_recv,
                device_id=(me, gg * 2 + c),
                device_id_type=MESH,
            )

        for row in (1 - yhi, yhi):
            for i in (2, 1, 3):
                part_copy(row * NX + (x + i) % NX).start()
        part_copy(across).start()

        part_in[g] = part_b[g]

        here = (lane8 // MAXP == g).astype(F32).astype(BF16)
        for k in range(images_here):
            own_got = jnp.sum(
                jnp.where(iota((NG, 1), 0) == g, got[k * NG : (k + 1) * NG], 0),
                axis=0,
                keepdims=True,
            ).astype(F32)
            mean = dot_nt(here, feats[k].reshape(width, LANES)) / own_got
            for p in range(pieces):
                r = k * pieces + p
                mean_f[r : r + 1, :] = mean[0:1, p * LANES : (p + 1) * LANES]

        text_swap.wait()
        text_wide[...] = text_in[...].astype(F32).reshape(2 * nz * packed, LANES)
        for t in range(texts_here):
            for p in range(pieces):
                text_full[t * 2 * nz : (t + 1) * 2 * nz, p * LANES : (p + 1) * LANES] = (
                    text_wide[pl.ds(t * pieces + p, 2 * nz, stride=packed), :]
                )
        for xx in range(NX):
            for q in range(4):
                m = ((q // 2) * NX + xx) * 2 + q % 2
                text_pad[:, xx * wide + q * HD : xx * wide + (q + 1) * HD] = text_full[
                    :, m * HD : (m + 1) * HD
                ]
        text_rows_b = text_full[...].astype(BF16)
        text_cols_b = text_pad[...].astype(BF16)

        part_seven = pltpu.make_async_remote_copy(
            src_ref=part_in.at[pl.ds(0, NG - 1)],
            dst_ref=part_in.at[pl.ds(0, NG - 1)],
            send_sem=part_send,
            recv_sem=part_recv,
            device_id=partner,
            device_id_type=MESH,
        )
        part_seven.wait()
        pooled = jnp.sum(part_in[...].astype(F32), axis=0) + mean_f[...]
        squares = jnp.sum(pooled * pooled, axis=1, keepdims=True)
        row_id = iota((packed, 1), 0)
        scale = jnp.zeros((packed, 1), F32)
        for k in range(images_here):
            inside = (row_id >= k * pieces) & (row_id < (k + 1) * pieces)
            norm = jnp.sum(jnp.where(inside, squares, 0.0), axis=0, keepdims=True)
            scale = jnp.where(inside, lax.rsqrt(norm + 1e-6), scale)
        own_unit = (pooled * scale).astype(BF16)
        unit_in[place] = own_unit

        def unit_y(step, at):
            q = (y + step) % (2 * NYL)
            return pltpu.make_async_remote_copy(
                src_ref=unit_in.at[at],
                dst_ref=unit_in.at[at],
                send_sem=unit_send,
                recv_sem=unit_recv.at[step],
                device_id=(z * NYL + q % NYL, ((q // NYL) * NX + x) * 2 + c),
                device_id_type=MESH,
            )

        def unit_x(at):
            for i in (2, 1, 3):
                pltpu.make_async_remote_copy(
                    src_ref=unit_in.at[at],
                    dst_ref=unit_in.at[at],
                    send_sem=unit_send,
                    recv_sem=unit_recv.at[0],
                    device_id=(me, (yhi * NX + (x + i) % NX) * 2 + c),
                    device_id_type=MESH,
                ).start()

        for step in (4, 3, 5, 2, 6, 1, 7):
            unit_y(step, place).start()
        unit_x(place)

        text_row = iota((text_rows, 1), 0)
        text_source = (text_row % nz) * NYL + ylo
        text_core = (text_row % (2 * nz)) // nz
        pair_at = text_source * dp_size + (g * 2 + text_core) * texts_here + text_row // (2 * nz)
        pair_lane = iota((text_rows, LANES), 1)
        pair_dest = jnp.zeros((text_rows, LANES), jnp.int32)
        for r in range(table_rows):
            pair_dest = pair_dest + jnp.where(
                pair_at == r * LANES + pair_lane, dest[r : r + 1, :], 0
            )
        pair_dest = jnp.sum(pair_dest, axis=1, keepdims=True)
        image_lane = iota((text_rows, rows), 1)
        image_source = c * half + image_lane % half
        image_dest = z * NYL + image_lane // half
        paired = (image_source == text_source) & (image_dest == pair_dest)
        labels = jnp.where(paired, 1.0, -1.0)

        for step in (1, 7, 2, 6, 3, 5, 4):
            q = (y + 2 * NYL - step) % (2 * NYL)
            at = (q % NYL) * NG + (q // NYL) * NX + x
            unit_y(step, at).wait_recv()
            unit_x(at)
        pltpu.make_async_remote_copy(
            src_ref=unit_in.at[pl.ds(0, plane - 2 * NYL)],
            dst_ref=unit_in.at[pl.ds(0, plane - 2 * NYL)],
            send_sem=unit_send,
            recv_sem=unit_recv.at[0],
            device_id=partner,
            device_id_type=MESH,
        ).wait_recv()
        unit_wide[...] = unit_in[...].astype(F32).reshape(plane * packed, LANES)
        for yy in range(NYL):
            for k in range(images_here):
                for p in range(pieces):
                    unit_full[
                        yy * half + k * NG : yy * half + (k + 1) * NG,
                        p * LANES : (p + 1) * LANES,
                    ] = unit_wide[
                        pl.ds(yy * NG * packed + k * pieces + p, NG, stride=packed), :
                    ]
        units = unit_full[...].astype(BF16)

        logits = 4.0 * dot_nt(text_rows_b, units) - 2.0
        dscaled = -4.0 * labels / (1.0 + jnp.exp(labels * logits))
        turned = jnp.transpose(dscaled).astype(BF16)
        dscaled = dscaled.astype(BF16)

        def gi_copy(n, xx):
            return pltpu.make_async_remote_copy(
                src_ref=gi_box.at[n, xx],
                dst_ref=gi_in.at[n, x],
                send_sem=gi_send.at[n],
                recv_sem=gi_recv.at[n],
                device_id=(me, (yhi * NX + xx) * 2 + c),
                device_id_type=MESH,
            )

        pair_rows = 2 * half
        def send_half(n):
            for xx in range(NX):
                gi_box[n, xx] = dot_nn(
                    turned[n * pair_rows : (n + 1) * pair_rows],
                    text_cols_b[:, xx * wide : (xx + 1) * wide],
                ).astype(BF16)
            for i in (2, 1, 3):
                gi_copy(n, (x + i) % NX).start()
            gi_in[n, x] = gi_box[n, x]

        send_half(0)

        text_grad = dot_nn(dscaled, units)
        for t in range(texts_here):
            for p in range(pieces):
                gt_f[pl.ds(t * pieces + p, 2 * nz, stride=packed), :] = text_grad[
                    t * 2 * nz : (t + 1) * 2 * nz, p * LANES : (p + 1) * LANES
                ]
        core_rows = nz * packed
        gt_copy = pltpu.make_async_remote_copy(
            src_ref=gt_f.at[pl.ds(pl.multiple_of(other * core_rows, 8), core_rows)],
            dst_ref=gt_in,
            send_sem=gt_send,
            recv_sem=gt_recv,
            device_id=partner,
            device_id_type=MESH,
        )
        gt_copy.start()
        send_half(1)

        gt_copy.wait()
        own_sums = gt_f[pl.ds(pl.multiple_of(c * core_rows, 8), core_rows), :]
        gt_box[...] = (own_sums + gt_in[...]).astype(BF16).reshape(nz, packed, LANES)

        def gtz_copy(zz):
            return pltpu.make_async_remote_copy(
                src_ref=gt_box.at[zz],
                dst_ref=gtz_in.at[z],
                send_sem=gtz_send,
                recv_sem=gtz_recv,
                device_id=(zz * NYL + ylo, mp),
                device_id_type=MESH,
            )

        for i in sorted(range(1, nz), key=lambda step: -min(step, nz - step)):
            gtz_copy(wrap(z + i, nz)).start()

        gtz_in[z] = gt_box[z]

        def gy_copy(yy, core):
            return pltpu.make_async_remote_copy(
                src_ref=gy_box.at[yy * 2 + core],
                dst_ref=gy_in.at[c * 2 * NYL + y],
                send_sem=gy_send,
                recv_sem=gy_recv,
                device_id=(z * NYL + yy % NYL, ((yy // NYL) * NX + x) * 2 + core),
                device_id_type=MESH,
            )

        for n in range(2):
            pltpu.make_async_remote_copy(
                src_ref=gi_in.at[n, pl.ds(0, NX - 1)],
                dst_ref=gi_in.at[n, pl.ds(0, NX - 1)],
                send_sem=gi_send.at[n],
                recv_sem=gi_recv.at[n],
                device_id=partner,
                device_id_type=MESH,
            ).wait()
            gi_sum[...] = jnp.sum(gi_in[n].astype(F32), axis=0)
            turn = [(row * NYL + 2 * n + r, core) for row in (0, 1) for r in (0, 1) for core in (0, 1)]
            for yy, core in turn:
                q = (yy // NYL) * 2 + core
                r = (yy % 2) * half
                gy_box[yy * 2 + core, :, 0:HD] = gi_sum[
                    r : r + half, q * HD : (q + 1) * HD
                ].astype(BF16)
            for yy, core in turn:

                @pl.when((yy != y) | (core != c))
                def _():
                    gy_copy(yy, core).start()

        gy_in[c * 2 * NYL + y] = gy_box[y * 2 + c]

        pltpu.make_async_remote_copy(
            src_ref=gtz_in.at[pl.ds(0, nz - 1)],
            dst_ref=gtz_in.at[pl.ds(0, nz - 1)],
            send_sem=gtz_send,
            recv_sem=gtz_recv,
            device_id=partner,
            device_id_type=MESH,
        ).wait()
        summed = jnp.sum(gtz_in[...].astype(F32), axis=0)
        for t in range(texts_here):
            for p in range(pieces):
                r = t * pieces + p
                grad_text[t : t + 1, p * LANES : (p + 1) * LANES] = summed[r : r + 1, :]

        pltpu.make_async_remote_copy(
            src_ref=gy_in.at[pl.ds(0, 4 * NYL - 1)],
            dst_ref=gy_in.at[pl.ds(0, 4 * NYL - 1)],
            send_sem=gy_send,
            recv_sem=gy_recv,
            device_id=partner,
            device_id_type=MESH,
        ).wait()
        for core in range(2):
            part = gy_in[core * 2 * NYL : (core + 1) * 2 * NYL].astype(F32)
            grad_image[core * half : (core + 1) * half, :] = jnp.sum(part, axis=0)[:, 0:HD]

        pltpu.make_async_remote_copy(
            src_ref=unit_in.at[pl.ds(0, plane - 1)],
            dst_ref=unit_in.at[pl.ds(0, plane - 1)],
            send_sem=unit_send,
            recv_sem=unit_recv.at[0],
            device_id=partner,
            device_id_type=MESH,
        ).wait_send()

        @pl.when(my_half == c)
        def _():
            pltpu.make_async_remote_copy(
                src_ref=outbox.at[pl.ds(0, dp_size - 1)],
                dst_ref=outbox.at[pl.ds(0, dp_size - 1)],
                send_sem=a2a_send,
                recv_sem=a2a_recv,
                device_id=partner,
                device_id_type=MESH,
            ).wait_send()

        @pl.when(my_half != c)
        def _():
            pltpu.make_async_remote_copy(
                src_ref=outbox,
                dst_ref=outbox,
                send_sem=a2a_send,
                recv_sem=a2a_recv,
                device_id=partner,
                device_id_type=MESH,
            ).wait_send()

        for k in range(images_here):
            pltpu.make_async_remote_copy(
                src_ref=feats.at[k, pl.ds(0, NG - 1)],
                dst_ref=feats.at[k, pl.ds(0, NG - 1)],
                send_sem=g_send.at[k],
                recv_sem=g_recv.at[k, 0],
                device_id=partner,
                device_id_type=MESH,
            ).wait_send()

    dma = pltpu.SemaphoreType.DMA
    scratch = [
        pltpu.VMEM((dp_size * dp_size // LANES, LANES), jnp.int32),
        pltpu.VMEM((dp_size * dp_size // LANES, LANES), jnp.int32),
        pltpu.VMEM((HD, dp_size * MAXP), BF16),
        pltpu.VMEM((3 * HD, width), BF16),
        pltpu.VMEM((HD, width), BF16),
        pltpu.VMEM((texts_here, width), BF16),
        dma((6,)),
        pltpu.VMEM((dp_size, MAXP, HD), BF16),
        pltpu.VMEM((2 * half, MAXP, HD), BF16),
        pltpu.VMEM((3 * HD, width), BF16),
        pltpu.VMEM((HD, width), BF16),
        pltpu.VMEM((images_here, NG, 2 * HD, LANES), BF16),
        pltpu.VMEM((images_here, 2, 3 * HD, LANES), F32),
        pltpu.VMEM((packed, LANES), F32),
        pltpu.VMEM((packed, LANES), BF16),
        pltpu.VMEM((2 * nz, packed, LANES), BF16),
        pltpu.VMEM((2 * nz * packed, LANES), F32),
        pltpu.VMEM((text_rows, width), F32),
        pltpu.VMEM((text_rows, NX * wide), F32),
        pltpu.VMEM((NG * packed, LANES), F32),
        pltpu.VMEM((NG, packed, LANES), BF16),
        pltpu.VMEM((NG, packed, LANES), BF16),
        pltpu.VMEM((packed, LANES), F32),
        pltpu.VMEM((plane, packed, LANES), BF16),
        pltpu.VMEM((plane * packed, LANES), F32),
        pltpu.VMEM((rows, width), F32),
        pltpu.VMEM((2, NX, rows // 2, wide), BF16),
        pltpu.VMEM((2, NX, rows // 2, wide), BF16),
        pltpu.VMEM((rows // 2, wide), F32),
        pltpu.VMEM((4 * NYL, half, LANES), BF16),
        pltpu.VMEM((4 * NYL, half, LANES), BF16),
        pltpu.VMEM((2 * nz * packed, LANES), F32),
        pltpu.VMEM((nz * packed, LANES), F32),
        pltpu.VMEM((nz, packed, LANES), BF16),
        pltpu.VMEM((nz, packed, LANES), BF16),
        dma,
        dma,
        dma,
        dma((2,)),
        dma((2,)),
        dma((images_here,)),
        dma((images_here, NG)),
        dma,
        dma,
        dma,
        dma,
        dma,
        dma,
        dma,
        dma((2 * NYL,)),
        dma((2,)),
        dma((2,)),
        dma,
        dma,
        dma,
        dma,
        dma,
        dma,
    ]
    return kernel, scratch


def on_device(patches, counts, dest, w_qkv, w_out, text):
    dp_size = lax.axis_size("dp")
    width = w_qkv.shape[2]
    texts_here = text.shape[0]
    kernel, scratch = make_kernel(dp_size, width, texts_here)
    vmem = pl.BlockSpec(memory_space=pltpu.VMEM)
    return pl.pallas_call(
        kernel,
        out_shape=(
            jax.ShapeDtypeStruct((dp_size, HD), F32),
            jax.ShapeDtypeStruct((texts_here, width), F32),
        ),
        in_specs=[pl.BlockSpec(memory_space=pltpu.HBM)] * 6,
        out_specs=(vmem, vmem),
        scratch_shapes=scratch,
        compiler_params=pltpu.CompilerParams(
            collective_id=0, has_side_effects=True, vmem_limit_bytes=40 * 1024 * 1024
        ),
    )(
        *(
            pltpu.with_memory_space_constraint(array, pltpu.HBM)
            for array in (
                counts.reshape(-1, LANES),
                dest.reshape(-1, LANES),
                patches,
                w_qkv.reshape(3 * HD, width),
                w_out,
                text,
            )
        )
    )


def solution(mesh):
    placed = (P("mp", "dp"), P(), P(), P(None, "mp", None), P("mp", None), P(("dp", "mp"), None))
    return jax.shard_map(
        on_device,
        mesh=mesh,
        in_specs=placed,
        out_specs=(P("dp", "mp"), P(("dp", "mp"), None)),
        check_vma=False,
    )
```

```python
import math

import jax
import jax.numpy as jnp
from jax import lax
from jax.experimental import pallas as pl
from jax.experimental.pallas import tpu as pltpu
from jax.sharding import PartitionSpec as P

HD = 72
MAXP = 16
NYL = 4
NYH = 2
NX = 4
NG = NYH * NX
LANES = 128
F32 = jnp.float32
BF16 = jnp.bfloat16
MESH = pl.DeviceIdType.MESH


def iota(shape, dim):
    return lax.broadcasted_iota(jnp.int32, shape, dim)


def dot_nn(a, b):
    return lax.dot_general(a, b, (((1,), (0,)), ((), ())), preferred_element_type=F32)


def dot_nt(a, b):
    return lax.dot_general(a, b, (((1,), (1,)), ((), ())), preferred_element_type=F32)


def wrap(value, size):
    return jnp.where(value >= size, value - size, value)


def make_kernel(dp_size, width, texts_here):
    nz = dp_size // NYL
    half = dp_size // 2
    images_here = half // NG
    pieces = width // LANES
    used = images_here * pieces
    packed = -(-used // 16) * 16
    slots = dp_size * MAXP
    half_slots = half * MAXP
    plane = NYL * NG
    rows = NYL * half
    text_rows = texts_here * 2 * nz
    wide = -(-(4 * HD) // LANES) * LANES

    def kernel(
        counts_in,
        dest_in,
        patches_in,
        w_qkv_in,
        w_out_in,
        text_arg,
        grad_image,
        grad_text,
        counts,
        dest,
        patches,
        w_qkv,
        w_out,
        text,
        in_sem,
        outbox,
        inbox,
        w_qkv_peer,
        w_out_peer,
        feats,
        qkv,
        text_f,
        text_box,
        text_in,
        text_wide,
        text_full,
        text_pad,
        part_f,
        part_b,
        part_in,
        mean_f,
        unit_in,
        unit_wide,
        unit_full,
        gi_box,
        gi_in,
        gi_sum,
        gy_box,
        gy_in,
        gt_f,
        gt_in,
        gt_box,
        gtz_in,
        local_sem,
        a2a_send,
        a2a_recv,
        w_send,
        w_recv,
        g_send,
        g_recv,
        text_send,
        text_recv,
        swap_send,
        swap_recv,
        part_send,
        part_recv,
        unit_send,
        unit_recv,
        gi_send,
        gi_recv,
        gy_send,
        gy_recv,
        gt_send,
        gt_recv,
        gtz_send,
        gtz_recv,
    ):
        me = lax.axis_index("dp")
        mp = lax.axis_index("mp")
        g, c = mp // 2, mp % 2
        z, ylo = me // NYL, me % NYL
        yhi, x = g // NX, g % NX
        y = yhi * NYL + ylo
        other = 1 - c
        partner = (me, g * 2 + other)
        my_half = me // half
        my_slot = me % half
        extra = jnp.where(my_half == c, 0, 1)

        loads = [
            pltpu.make_async_copy(src, dst, in_sem.at[i])
            for i, (src, dst) in enumerate(
                (
                    (dest_in, dest),
                    (counts_in, counts),
                    (patches_in, patches),
                    (w_qkv_in, w_qkv),
                    (w_out_in, w_out),
                    (text_arg, text),
                )
            )
        ]
        for load in loads:
            load.start()

        barrier = pltpu.get_barrier_semaphore()

        def greet(device):
            pl.semaphore_signal(barrier, inc=1, device_id=device, device_id_type=MESH)

        @pl.loop(0, half)
        def _(i):
            src = half * c + i
            greet((src, g * 2 + other))

            @pl.when(src != me)
            def _():
                greet((src, mp))

        greet(partner)

        @pl.loop(1, nz)
        def _(i):
            greet((wrap(z + i, nz) * NYL + ylo, mp))

        place = ylo * NG + g

        @pl.loop(1, 2 * NYL)
        def _(i):
            q = (y + i) % (2 * NYL)
            greet((z * NYL + q % NYL, ((q // NYL) * NX + x) * 2))
            greet((z * NYL + q % NYL, ((q // NYL) * NX + x) * 2 + 1))

        for i in range(1, NX):
            greet((me, (yhi * NX + (x + i) % NX) * 2 + c))
            greet((me, ((1 - yhi) * NX + (x + i) % NX) * 2 + c))

        for buffer in (text_f, text_pad, part_f, mean_f, gt_f, gy_box):
            buffer[...] = jnp.zeros_like(buffer)

        loads[0].wait()
        loads[1].wait()
        first = me * dp_size
        table_rows = dp_size * dp_size // LANES
        span = iota((dp_size, LANES), 1)
        order = iota((dp_size, LANES), 0)
        step = (order // NYL + 1) // 2
        target = wrap(z + nz // 2 + jnp.where(order // NYL % 2 == 1, nz - step, step), nz)
        target = wrap(target, nz) * NYL + (ylo + NYL - 1 - order % NYL) % NYL
        index = jnp.zeros((dp_size, 1), jnp.int32)
        base = first // LANES
        own_rows = []
        for r in range(2):
            row = jnp.minimum(base + r, table_rows - 1)
            image = (base + r) * LANES + span - first
            inside = (image >= 0) & (image < dp_size) & (base + r < table_rows)
            image = jnp.where(inside, image, dp_size)
            own_rows.append((image, counts[pl.ds(row, 1), :]))
            hit = inside & (dest[pl.ds(row, 1), :] == target)
            index = index + jnp.sum(jnp.where(hit, image, 0), axis=1, keepdims=True)
        start = jnp.zeros((dp_size, 1), jnp.int32)
        count = jnp.zeros((dp_size, 1), jnp.int32)
        for image, own in own_rows:
            start = start + jnp.sum(jnp.where(image < index, own, 0), axis=1, keepdims=True)
            count = count + jnp.sum(jnp.where(image == index, own, 0), axis=1, keepdims=True)
        position = iota((dp_size, MAXP, 1), 1)
        column = jnp.where(
            position < count.reshape(dp_size, 1, 1), start.reshape(dp_size, 1, 1) + position, -1
        ).reshape(slots, 1)
        loads[2].wait()

        def image_copy(at, d):
            return pltpu.make_async_remote_copy(
                src_ref=outbox.at[at],
                dst_ref=inbox.at[c * half + my_slot],
                send_sem=a2a_send,
                recv_sem=a2a_recv,
                device_id=(d, g * 2 + my_half),
                device_id_type=MESH,
            )

        total = (2 * half - 1 + extra) + 1 + (nz - 1) + 2 * (2 * NYL - 1) + 2 * (NX - 1)
        blocks = 4
        block_rows = slots // blocks
        block_images = dp_size // blocks
        block_z = nz // blocks
        for n in range(blocks):
            chosen = iota((block_rows, patches.shape[1]), 1) == column[
                n * block_rows : (n + 1) * block_rows
            ]
            picked = dot_nt(chosen.astype(F32).astype(BF16), patches[...]).astype(BF16)
            outbox[n * block_images : (n + 1) * block_images] = picked.reshape(
                block_images, MAXP, HD
            )
            if n == 0:
                pl.semaphore_wait(barrier, total)
            last = n == blocks - 1

            @pl.loop(n * block_z, (n + 1) * block_z - (1 if last else 0))
            def _(j):
                step = (j + 1) // 2
                zz = wrap(z + nz // 2 + jnp.where(j % 2 == 1, nz - step, step), nz)
                zz = wrap(zz, nz)
                for i in range(NYL):
                    d = zz * NYL + (ylo + NYL - 1 - i) % NYL
                    image_copy(j * NYL + i, d).start()

            if last:
                for i in range(NYL - 1):
                    d = z * NYL + (ylo + NYL - 1 - i) % NYL
                    image_copy((nz - 1) * NYL + i, d).start()

        own_copy = pltpu.make_async_copy(
            outbox.at[dp_size - 1], inbox.at[c * half + my_slot], local_sem
        )

        @pl.when(my_half == c)
        def _():
            own_copy.start()

        @pl.when(my_half != c)
        def _():
            image_copy(dp_size - 1, me).start()

        def swap(src, dst, i):
            return pltpu.make_async_remote_copy(
                src_ref=src,
                dst_ref=dst,
                send_sem=w_send.at[i],
                recv_sem=w_recv.at[i],
                device_id=partner,
                device_id_type=MESH,
            )

        swap_qkv = swap(w_qkv, w_qkv_peer, 0)
        swap_out = swap(w_out, w_out_peer, 1)
        loads[3].wait()
        swap_qkv.start()
        loads[4].wait()
        swap_out.start()

        loads[5].wait()
        text_float = text[...].astype(F32)
        text_unit = text_float * lax.rsqrt(
            jnp.sum(text_float * text_float, axis=1, keepdims=True) + 1e-6
        )
        for t in range(texts_here):
            for k in range(pieces):
                text_f[t * pieces + k : t * pieces + k + 1, :] = text_unit[
                    t : t + 1, k * LANES : (k + 1) * LANES
                ]
        own_text = text_f[...].astype(BF16)
        text_box[...] = own_text
        text_in[c * nz + z] = own_text

        def text_copy(zz):
            return pltpu.make_async_remote_copy(
                src_ref=text_box,
                dst_ref=text_in.at[c * nz + z],
                send_sem=text_send,
                recv_sem=text_recv,
                device_id=(zz * NYL + ylo, mp),
                device_id_type=MESH,
            )

        own_texts = text_in.at[pl.ds(c * nz, nz)]
        text_swap = pltpu.make_async_remote_copy(
            src_ref=own_texts,
            dst_ref=own_texts,
            send_sem=swap_send,
            recv_sem=swap_recv,
            device_id=partner,
            device_id_type=MESH,
        )

        got = jnp.zeros((half, LANES), jnp.int32)
        slot_row, slot_lane = iota((half, LANES), 0), iota((half, LANES), 1)
        half_rows = half * dp_size // LANES
        for r in range(half_rows):
            row = pl.ds(half_rows * c + r, 1)
            inside = (r * LANES + slot_lane) // dp_size == slot_row
            got = got + jnp.where(inside & (dest[row, :] == me), counts[row, :], 0)
        got = jnp.sum(got, axis=1, keepdims=True)

        @pl.when(my_half == c)
        def _():
            own_copy.wait()
            pltpu.make_async_remote_copy(
                src_ref=inbox.at[pl.ds(0, 2 * half - 1)],
                dst_ref=inbox.at[pl.ds(0, 2 * half - 1)],
                send_sem=a2a_send,
                recv_sem=a2a_recv,
                device_id=partner,
                device_id_type=MESH,
            ).wait_recv()

        @pl.when(my_half != c)
        def _():
            pltpu.make_async_remote_copy(
                src_ref=inbox,
                dst_ref=inbox,
                send_sem=a2a_send,
                recv_sem=a2a_recv,
                device_id=partner,
                device_id_type=MESH,
            ).wait_recv()

        eye = (iota((HD, HD), 0) == iota((HD, HD), 1)).astype(F32).astype(BF16)

        across = (1 - yhi) * NX + x
        left_x, right_x = lax.rem(x + NX - 1, NX), lax.rem(x + 1, NX)
        far_x = lax.rem(x + 2, NX)

        def feat_copy(k, owner, to):
            return pltpu.make_async_remote_copy(
                src_ref=feats.at[k, owner],
                dst_ref=feats.at[k, owner],
                send_sem=g_send.at[k],
                recv_sem=g_recv.at[k, owner],
                device_id=(me, to * 2 + c),
                device_id_type=MESH,
            )

        own_row, far_row = yhi * NX, (1 - yhi) * NX
        left, right = own_row + left_x, own_row + right_x
        for k in range(images_here):
            low, high = (
                dot_nt(eye, inbox[r + k * NG : r + (k + 1) * NG].reshape(LANES, HD))
                for r in (0, half)
            )
            feats[k, g] = jnp.concatenate([low, high], axis=0).astype(BF16)
            feat_copy(k, g, across).start()
            feat_copy(k, g, left).start()
            feat_copy(k, g, right).start()

        @pl.loop(1, nz)
        def _(i):
            text_copy(wrap(z + i, nz)).start()

        for k in range(images_here):
            feat_copy(k, left, left).wait_recv()
            if k % 2 == 0:
                feat_copy(k, left, right).start()
            feat_copy(k, right, left).wait_recv()
            if k % 2 == 1:
                feat_copy(k, right, left).start()
            feat_copy(k, across, across).wait_recv()
            feat_copy(k, across, own_row + far_x).start()
            feat_copy(k, across, left).start()
            feat_copy(k, across, right).start()

        swap_qkv.wait()
        swap_out.wait()

        for k in range(images_here):
            feat_copy(k, own_row + far_x, left).wait_recv()
            for xx in (left_x, right_x, far_x):
                feat_copy(k, far_row + xx, left).wait_recv()
            full = feats[k].reshape(width, LANES).astype(F32)
            centred = full - jnp.sum(full, axis=0, keepdims=True) / width
            variance = jnp.sum(centred * centred, axis=0, keepdims=True) / width
            normed = (centred * lax.rsqrt(variance + 1e-6)).astype(BF16)
            qkv[k, 0] = dot_nn(w_qkv[...], normed)
            qkv[k, 1] = dot_nn(w_qkv_peer[...], normed)
        pltpu.make_async_remote_copy(
            src_ref=text_in.at[pl.ds(0, nz - 1)],
            dst_ref=text_in.at[pl.ds(0, nz - 1)],
            send_sem=text_send,
            recv_sem=text_recv,
            device_id=partner,
            device_id_type=MESH,
        ).wait()
        text_swap.start()
        row8, lane8 = iota((NG, LANES), 0), iota((NG, LANES), 1)
        same = iota((LANES, LANES), 0) // MAXP == iota((LANES, LANES), 1) // MAXP
        heads = ([], [])
        for k in range(images_here):
            got_k = got[k * NG : (k + 1) * NG]
            got_float = got_k.astype(F32)
            real = (lane8 // MAXP == row8) & (lane8 % MAXP < got_k)
            member = real.astype(F32).astype(BF16)
            key_count = jnp.broadcast_to(got_k.reshape(NG, 1, 1), (NG, MAXP, 1))
            key_count = key_count.reshape(LANES, 1)
            keep = same & (iota((LANES, 1), 0) % MAXP < key_count)
            for h in range(2):
                query = qkv[k, h, 0:HD].astype(BF16)
                key = jnp.transpose(qkv[k, h, HD : 2 * HD]).astype(BF16)
                value = qkv[k, h, 2 * HD : 3 * HD].astype(BF16)
                scores = dot_nn(key, query) / math.sqrt(HD)
                scores = jnp.where(keep, scores, -1e30)
                raised = jnp.exp(scores - jnp.max(scores, axis=0, keepdims=True))
                weights = (raised / jnp.sum(raised, axis=0, keepdims=True)).astype(BF16)
                mixed = dot_nn(value, weights).astype(BF16)
                heads[h].append(dot_nt(member, mixed) / got_float)
        term = jnp.zeros((half, width), F32)
        for pooled, wo in zip(heads, (w_out, w_out_peer)):
            term = term + dot_nn(jnp.concatenate(pooled, axis=0).astype(BF16), wo[...])
        for k in range(images_here):
            for p in range(pieces):
                part_f[pl.ds(k * pieces + p, NG, stride=packed), :] = term[
                    k * NG : (k + 1) * NG, p * LANES : (p + 1) * LANES
                ]

        part_b[...] = part_f[0 : NG * packed].astype(BF16).reshape(NG, packed, LANES)

        def part_copy(gg):
            return pltpu.make_async_remote_copy(
                src_ref=part_b.at[gg],
                dst_ref=part_in.at[g],
                send_sem=part_send,
                recv_sem=part_recv,
                device_id=(me, gg * 2 + c),
                device_id_type=MESH,
            )

        for row in (1 - yhi, yhi):
            for i in (2, 1, 3):
                part_copy(row * NX + (x + i) % NX).start()
        part_copy(across).start()

        part_in[g] = part_b[g]

        here = (lane8 // MAXP == g).astype(F32).astype(BF16)
        for k in range(images_here):
            own_got = jnp.sum(
                jnp.where(iota((NG, 1), 0) == g, got[k * NG : (k + 1) * NG], 0),
                axis=0,
                keepdims=True,
            ).astype(F32)
            mean = dot_nt(here, feats[k].reshape(width, LANES)) / own_got
            for p in range(pieces):
                r = k * pieces + p
                mean_f[r : r + 1, :] = mean[0:1, p * LANES : (p + 1) * LANES]

        text_swap.wait()
        text_wide[0 : 2 * nz * packed] = text_in[...].astype(F32).reshape(-1, LANES)
        for t in range(texts_here):
            for p in range(pieces):
                text_full[t * 2 * nz : (t + 1) * 2 * nz, p * LANES : (p + 1) * LANES] = (
                    text_wide[pl.ds(t * pieces + p, 2 * nz, stride=packed), :]
                )
        for xx in range(NX):
            for q in range(4):
                m = ((q // 2) * NX + xx) * 2 + q % 2
                text_pad[:, xx * wide + q * HD : xx * wide + (q + 1) * HD] = text_full[
                    :, m * HD : (m + 1) * HD
                ]
        text_rows_b = text_full[...].astype(BF16)
        text_cols_b = text_pad[...].astype(BF16)

        part_seven = pltpu.make_async_remote_copy(
            src_ref=part_in.at[pl.ds(0, NG - 1)],
            dst_ref=part_in.at[pl.ds(0, NG - 1)],
            send_sem=part_send,
            recv_sem=part_recv,
            device_id=partner,
            device_id_type=MESH,
        )
        part_seven.wait()
        pooled = jnp.sum(part_in[...].astype(F32), axis=0) + mean_f[...]
        squares = jnp.sum(pooled * pooled, axis=1, keepdims=True)
        row_id = iota((packed, 1), 0)
        scale = jnp.zeros((packed, 1), F32)
        for k in range(images_here):
            inside = (row_id >= k * pieces) & (row_id < (k + 1) * pieces)
            norm = jnp.sum(jnp.where(inside, squares, 0.0), axis=0, keepdims=True)
            scale = jnp.where(inside, lax.rsqrt(norm + 1e-6), scale)
        own_unit = (pooled * scale).astype(BF16)
        unit_in[place] = own_unit

        def unit_y(step, at):
            q = (y + step) % (2 * NYL)
            return pltpu.make_async_remote_copy(
                src_ref=unit_in.at[at],
                dst_ref=unit_in.at[at],
                send_sem=unit_send,
                recv_sem=unit_recv.at[step],
                device_id=(z * NYL + q % NYL, ((q // NYL) * NX + x) * 2 + c),
                device_id_type=MESH,
            )

        def unit_x(at):
            for i in (2, 1, 3):
                pltpu.make_async_remote_copy(
                    src_ref=unit_in.at[at],
                    dst_ref=unit_in.at[at],
                    send_sem=unit_send,
                    recv_sem=unit_recv.at[0],
                    device_id=(me, (yhi * NX + (x + i) % NX) * 2 + c),
                    device_id_type=MESH,
                ).start()

        for step in (4, 3, 5, 2, 6, 1, 7):
            unit_y(step, place).start()
        unit_x(place)

        text_row = iota((text_rows, 1), 0)
        text_source = (text_row % nz) * NYL + ylo
        text_core = (text_row % (2 * nz)) // nz
        pair_at = text_source * dp_size + (g * 2 + text_core) * texts_here + text_row // (2 * nz)
        pair_lane = iota((text_rows, LANES), 1)
        pair_dest = jnp.zeros((text_rows, LANES), jnp.int32)
        for r in range(table_rows):
            pair_dest = pair_dest + jnp.where(
                pair_at == r * LANES + pair_lane, dest[r : r + 1, :], 0
            )
        pair_dest = jnp.sum(pair_dest, axis=1, keepdims=True)
        image_lane = iota((text_rows, rows), 1)
        image_source = c * half + image_lane % half
        image_dest = z * NYL + image_lane // half
        paired = (image_source == text_source) & (image_dest == pair_dest)
        labels = jnp.where(paired, 1.0, -1.0)

        for step in (1, 7, 2, 6, 3, 5, 4):
            q = (y + 2 * NYL - step) % (2 * NYL)
            at = (q % NYL) * NG + (q // NYL) * NX + x
            unit_y(step, at).wait_recv()
            unit_x(at)
        pltpu.make_async_remote_copy(
            src_ref=unit_in.at[pl.ds(0, plane - 2 * NYL)],
            dst_ref=unit_in.at[pl.ds(0, plane - 2 * NYL)],
            send_sem=unit_send,
            recv_sem=unit_recv.at[0],
            device_id=partner,
            device_id_type=MESH,
        ).wait_recv()
        unit_wide[0 : plane * packed] = unit_in[...].astype(F32).reshape(-1, LANES)
        for yy in range(NYL):
            for k in range(images_here):
                for p in range(pieces):
                    unit_full[
                        yy * half + k * NG : yy * half + (k + 1) * NG,
                        p * LANES : (p + 1) * LANES,
                    ] = unit_wide[
                        pl.ds(yy * NG * packed + k * pieces + p, NG, stride=packed), :
                    ]
        units = unit_full[...].astype(BF16)

        logits = 4.0 * dot_nt(text_rows_b, units) - 2.0
        dscaled = -4.0 * labels / (1.0 + jnp.exp(labels * logits))
        turned = jnp.transpose(dscaled).astype(BF16)
        dscaled = dscaled.astype(BF16)

        def gi_copy(n, xx):
            return pltpu.make_async_remote_copy(
                src_ref=gi_box.at[n, xx],
                dst_ref=gi_in.at[n, x],
                send_sem=gi_send.at[n],
                recv_sem=gi_recv.at[n],
                device_id=(me, (yhi * NX + xx) * 2 + c),
                device_id_type=MESH,
            )

        pair_rows = 2 * half
        def send_half(n):
            for xx in range(NX):
                gi_box[n, xx] = dot_nn(
                    turned[n * pair_rows : (n + 1) * pair_rows],
                    text_cols_b[:, xx * wide : (xx + 1) * wide],
                ).astype(BF16)
            for i in (2, 1, 3):
                gi_copy(n, (x + i) % NX).start()
            gi_in[n, x] = gi_box[n, x]

        send_half(0)

        text_grad = dot_nn(dscaled, units)
        for t in range(texts_here):
            for p in range(pieces):
                gt_f[pl.ds(t * pieces + p, 2 * nz, stride=packed), :] = text_grad[
                    t * 2 * nz : (t + 1) * 2 * nz, p * LANES : (p + 1) * LANES
                ]
        core_rows = nz * packed
        gt_copy = pltpu.make_async_remote_copy(
            src_ref=gt_f.at[pl.ds(pl.multiple_of(other * core_rows, 8), core_rows)],
            dst_ref=gt_in,
            send_sem=gt_send,
            recv_sem=gt_recv,
            device_id=partner,
            device_id_type=MESH,
        )
        gt_copy.start()
        send_half(1)

        gt_copy.wait()
        own_sums = gt_f[pl.ds(pl.multiple_of(c * core_rows, 8), core_rows), :]
        gt_box[...] = (own_sums + gt_in[...]).astype(BF16).reshape(nz, packed, LANES)

        def gtz_copy(zz):
            return pltpu.make_async_remote_copy(
                src_ref=gt_box.at[zz],
                dst_ref=gtz_in.at[z],
                send_sem=gtz_send,
                recv_sem=gtz_recv,
                device_id=(zz * NYL + ylo, mp),
                device_id_type=MESH,
            )

        for i in sorted(range(1, nz), key=lambda step: -min(step, nz - step)):
            gtz_copy(wrap(z + i, nz)).start()

        gtz_in[z] = gt_box[z]

        def gy_copy(yy, core):
            return pltpu.make_async_remote_copy(
                src_ref=gy_box.at[yy * 2 + core],
                dst_ref=gy_in.at[c * 2 * NYL + y],
                send_sem=gy_send,
                recv_sem=gy_recv,
                device_id=(z * NYL + yy % NYL, ((yy // NYL) * NX + x) * 2 + core),
                device_id_type=MESH,
            )

        for n in range(2):
            pltpu.make_async_remote_copy(
                src_ref=gi_in.at[n, pl.ds(0, NX - 1)],
                dst_ref=gi_in.at[n, pl.ds(0, NX - 1)],
                send_sem=gi_send.at[n],
                recv_sem=gi_recv.at[n],
                device_id=partner,
                device_id_type=MESH,
            ).wait()
            gi_sum[...] = jnp.sum(gi_in[n].astype(F32), axis=0)
            turn = [(row * NYL + 2 * n + r, core) for row in (0, 1) for r in (0, 1) for core in (0, 1)]
            for yy, core in turn:
                q = (yy // NYL) * 2 + core
                r = (yy % 2) * half
                gy_box[yy * 2 + core, :, 0:HD] = gi_sum[
                    r : r + half, q * HD : (q + 1) * HD
                ].astype(BF16)
            for yy, core in turn:

                @pl.when((yy != y) | (core != c))
                def _():
                    gy_copy(yy, core).start()

        gy_in[c * 2 * NYL + y] = gy_box[y * 2 + c]

        pltpu.make_async_remote_copy(
            src_ref=gtz_in.at[pl.ds(0, nz - 1)],
            dst_ref=gtz_in.at[pl.ds(0, nz - 1)],
            send_sem=gtz_send,
            recv_sem=gtz_recv,
            device_id=partner,
            device_id_type=MESH,
        ).wait()
        summed = jnp.sum(gtz_in[...].astype(F32), axis=0)
        for t in range(texts_here):
            for p in range(pieces):
                r = t * pieces + p
                grad_text[t : t + 1, p * LANES : (p + 1) * LANES] = summed[r : r + 1, :]

        pltpu.make_async_remote_copy(
            src_ref=gy_in.at[pl.ds(0, 4 * NYL - 1)],
            dst_ref=gy_in.at[pl.ds(0, 4 * NYL - 1)],
            send_sem=gy_send,
            recv_sem=gy_recv,
            device_id=partner,
            device_id_type=MESH,
        ).wait()
        for core in range(2):
            part = gy_in[core * 2 * NYL : (core + 1) * 2 * NYL].astype(F32)
            grad_image[core * half : (core + 1) * half, :] = jnp.sum(part, axis=0)[:, 0:HD]

        pltpu.make_async_remote_copy(
            src_ref=unit_in.at[pl.ds(0, plane - 1)],
            dst_ref=unit_in.at[pl.ds(0, plane - 1)],
            send_sem=unit_send,
            recv_sem=unit_recv.at[0],
            device_id=partner,
            device_id_type=MESH,
        ).wait_send()

        @pl.when(my_half == c)
        def _():
            pltpu.make_async_remote_copy(
                src_ref=outbox.at[pl.ds(0, dp_size - 1)],
                dst_ref=outbox.at[pl.ds(0, dp_size - 1)],
                send_sem=a2a_send,
                recv_sem=a2a_recv,
                device_id=partner,
                device_id_type=MESH,
            ).wait_send()

        @pl.when(my_half != c)
        def _():
            pltpu.make_async_remote_copy(
                src_ref=outbox,
                dst_ref=outbox,
                send_sem=a2a_send,
                recv_sem=a2a_recv,
                device_id=partner,
                device_id_type=MESH,
            ).wait_send()

        for k in range(images_here):
            pltpu.make_async_remote_copy(
                src_ref=feats.at[k, pl.ds(0, NG - 1)],
                dst_ref=feats.at[k, pl.ds(0, NG - 1)],
                send_sem=g_send.at[k],
                recv_sem=g_recv.at[k, 0],
                device_id=partner,
                device_id_type=MESH,
            ).wait_send()

    dma = pltpu.SemaphoreType.DMA
    scratch = [
        pltpu.VMEM((dp_size * dp_size // LANES, LANES), jnp.int32),
        pltpu.VMEM((dp_size * dp_size // LANES, LANES), jnp.int32),
        pltpu.VMEM((HD, dp_size * MAXP), BF16),
        pltpu.VMEM((3 * HD, width), BF16),
        pltpu.VMEM((HD, width), BF16),
        pltpu.VMEM((texts_here, width), BF16),
        dma((6,)),
        pltpu.VMEM((dp_size, MAXP, HD), BF16),
        pltpu.VMEM((2 * half, MAXP, HD), BF16),
        pltpu.VMEM((3 * HD, width), BF16),
        pltpu.VMEM((HD, width), BF16),
        pltpu.VMEM((images_here, NG, 2 * HD, LANES), BF16),
        pltpu.VMEM((images_here, 2, 3 * HD, LANES), F32),
        pltpu.VMEM((packed, LANES), F32),
        pltpu.VMEM((packed, LANES), BF16),
        pltpu.VMEM((2 * nz, packed, LANES), BF16),
        pltpu.VMEM(((2 * nz + 1) * packed, LANES), F32),
        pltpu.VMEM((text_rows, width), F32),
        pltpu.VMEM((text_rows, NX * wide), F32),
        pltpu.VMEM(((NG + 1) * packed, LANES), F32),
        pltpu.VMEM((NG, packed, LANES), BF16),
        pltpu.VMEM((NG, packed, LANES), BF16),
        pltpu.VMEM((packed, LANES), F32),
        pltpu.VMEM((plane, packed, LANES), BF16),
        pltpu.VMEM(((plane + 1) * packed, LANES), F32),
        pltpu.VMEM((rows, width), F32),
        pltpu.VMEM((2, NX, rows // 2, wide), BF16),
        pltpu.VMEM((2, NX, rows // 2, wide), BF16),
        pltpu.VMEM((rows // 2, wide), F32),
        pltpu.VMEM((4 * NYL, half, LANES), BF16),
        pltpu.VMEM((4 * NYL, half, LANES), BF16),
        pltpu.VMEM(((2 * nz + 1) * packed, LANES), F32),
        pltpu.VMEM((nz * packed, LANES), F32),
        pltpu.VMEM((nz, packed, LANES), BF16),
        pltpu.VMEM((nz, packed, LANES), BF16),
        dma,
        dma,
        dma,
        dma((2,)),
        dma((2,)),
        dma((images_here,)),
        dma((images_here, NG)),
        dma,
        dma,
        dma,
        dma,
        dma,
        dma,
        dma,
        dma((2 * NYL,)),
        dma((2,)),
        dma((2,)),
        dma,
        dma,
        dma,
        dma,
        dma,
        dma,
    ]
    return kernel, scratch


def on_device(patches, counts, dest, w_qkv, w_out, text):
    dp_size = lax.axis_size("dp")
    width = w_qkv.shape[2]
    texts_here = text.shape[0]
    kernel, scratch = make_kernel(dp_size, width, texts_here)
    vmem = pl.BlockSpec(memory_space=pltpu.VMEM)
    return pl.pallas_call(
        kernel,
        out_shape=(
            jax.ShapeDtypeStruct((dp_size, HD), F32),
            jax.ShapeDtypeStruct((texts_here, width), F32),
        ),
        in_specs=[pl.BlockSpec(memory_space=pltpu.HBM)] * 6,
        out_specs=(vmem, vmem),
        scratch_shapes=scratch,
        compiler_params=pltpu.CompilerParams(
            collective_id=0, has_side_effects=True, vmem_limit_bytes=40 * 1024 * 1024
        ),
    )(
        *(
            pltpu.with_memory_space_constraint(array, pltpu.HBM)
            for array in (
                counts.reshape(-1, LANES),
                dest.reshape(-1, LANES),
                patches,
                w_qkv.reshape(3 * HD, width),
                w_out,
                text,
            )
        )
    )


def solution(mesh):
    placed = (P("mp", "dp"), P(), P(), P(None, "mp", None), P("mp", None), P(("dp", "mp"), None))
    return jax.shard_map(
        on_device,
        mesh=mesh,
        in_specs=placed,
        out_specs=(P("dp", "mp"), P(("dp", "mp"), None)),
        check_vma=False,
    )
```
